32 devices in a mesh: row: 8 (over y, x, core), col: 4 (over z).
Axes of the slice: x: 2, y: 2, z: 4, core: 2. Of those that a mesh axis runs over, the one named last changes fastest.
Arguments:
- top_inverse: bfloat16 [8, 4, 8, 4, 128, 128], P('row', None, None, 'col'), as said below
- upper_panel: bfloat16 [3, 8, 4, 128, 128], P(None, 'row', 'col'), may hold values from -0.25 to 0.25
- upper_pattern: int32 [3, 8, 4], P(None, 'row', 'col'), may hold values from 0 to 1
- upper_diagonal: float32 [3, 128, 128], replicated, may hold values from -6 to 6
- lower_panel: bfloat16 [8, 8, 4, 128, 128], P(None, 'row', 'col'), may hold values from -0.25 to 0.25
- lower_pattern: int32 [8, 8, 4], P(None, 'row', 'col'), may hold values from 0 to 1, as said below
- parents: int32 [8], replicated, may hold values from 0 to 2, as said below
- parent_panel: bfloat16 [8, 128, 128], replicated, may hold values from -0.5 to 0.5
- lower_diagonal: float32 [8, 128, 128], replicated, may hold values from -6 to 6
Outputs:
- upper_columns: bfloat16 [3, 8, 4, 128, 128], P(None, 'row', 'col')
- upper_blocks: float32 [3, 128, 128], replicated
- lower_columns: bfloat16 [8, 8, 4, 128, 128], P(None, 'row', 'col')
- lower_cross: float32 [8, 128, 128], replicated
- lower_blocks: float32 [8, 128, 128], replicated
The draws below stay inside these ranges and needn't reach their ends.
Inputs may be any that keep to these rules, and one draw needn't show every extreme that they name: top_inverse is symmetric: block (I, J) is the transpose of block (J, I). `lower_pattern`: A second-level pattern is zero wherever the pattern of its parent is zero. `parents`: every first-level supernode is the parent of some second-level supernode.
All inputs are finite; a program needn't handle non-finite values.
Results may differ from the reference program's by a relative error of at most 0.0041.
Values may be sent and summed in bfloat16 or wider, within the bound.
No kernel may reach another device: no remote copies, remote signals or barrier semaphores. Data moves between devices by JAX's collectives and lax.ppermute only.
A program may use at most 128 MiB of HBM per device.

```python
import math
import jax
import jax.numpy as jnp
from jax import lax

BLOCK = 128
UPPER = 3
LOWER = 8
TOP_ROWS = 8
TOP_COLS = 4


def pattern_tables(key):
    order = jax.random.permutation(jax.random.fold_in(key, 11), LOWER)
    chosen = jax.random.randint(jax.random.fold_in(key, 14), (LOWER,), 0, UPPER).astype(jnp.int32)
    parents = chosen.at[order[:UPPER]].set(jnp.arange(UPPER, dtype=jnp.int32)).astype(jnp.int32)
    upper = jax.random.randint(jax.random.fold_in(key, 12), (UPPER, TOP_ROWS, TOP_COLS), 0, 2).astype(jnp.int32)
    keeping = jax.random.randint(jax.random.fold_in(key, 13), (LOWER, TOP_ROWS, TOP_COLS), 0, 4)
    lower = upper[parents] * (keeping > 0).astype(jnp.int32)
    return (parents, upper, lower)


def draw_parents(key, part):
    return pattern_tables(key)[0]


def draw_upper_pattern(key, part):
    return pattern_tables(key)[1]


def draw_lower_pattern(key, part):
    return pattern_tables(key)[2]


def draw_top_inverse(key, part):
    normal = jax.random.normal(key, (TOP_ROWS, TOP_COLS, TOP_ROWS, TOP_COLS, BLOCK, BLOCK), jnp.float32)
    symmetric = 0.5 * (normal + jnp.transpose(normal, (2, 3, 0, 1, 5, 4)))
    factor = 4.0 / math.sqrt(TOP_ROWS * TOP_COLS)
    return (symmetric * factor).astype(jnp.bfloat16)


def level_of(rng, shape, split, low, largest):
    gain, own = 1.0, jax.random.fold_in(rng, 6)
    for dim, shards_of in split:
        heights = jnp.exp(jax.random.uniform(jax.random.fold_in(own, dim), (shards_of,), jnp.float32, low / len(split), largest / len(split)))
        gain = gain * jnp.repeat(heights, shape[dim] // shards_of).reshape([-1 if axis == dim else 1 for axis in range(len(shape))])
    return gain


def noise(rng, dims, scale, reach, split=(), kind=jnp.bfloat16):
    array = scale * jax.random.normal(rng, dims, jnp.float32)
    if split:
        array = array * level_of(rng, dims, split, -0.22, 0.18)
    return jnp.clip(array, -reach, reach).astype(kind)


def setup_inputs(seed: int = 0) -> dict:
    splits = jax.random.split(jax.random.key(seed), 10)
    return {
        "top_inverse": draw_top_inverse(jax.random.fold_in(splits[9], 71), 0),
        "upper_panel": noise(splits[1], (UPPER, TOP_ROWS, TOP_COLS, BLOCK, BLOCK), (BLOCK * 4) ** -0.5, 0.25, ((1, 8), (2, 4))),
        "upper_pattern": draw_upper_pattern(jax.random.fold_in(splits[9], 71), 0),
        "upper_diagonal": noise(splits[3], (UPPER, BLOCK, BLOCK), 1.0, 6.0, (), jnp.float32),
        "lower_panel": noise(splits[4], (LOWER, TOP_ROWS, TOP_COLS, BLOCK, BLOCK), (BLOCK * 4) ** -0.5, 0.25, ((1, 8), (2, 4))),
        "lower_pattern": draw_lower_pattern(jax.random.fold_in(splits[9], 71), 0),
        "parents": draw_parents(jax.random.fold_in(splits[9], 71), 0),
        "parent_panel": noise(splits[7], (LOWER, BLOCK, BLOCK), BLOCK ** -0.5, 0.5),
        "lower_diagonal": noise(splits[8], (LOWER, BLOCK, BLOCK), 1.0, 6.0, (), jnp.float32),
    }


HIGH = lax.Precision.HIGHEST


def column_product(top_inverse, masked):
    wide = masked.astype(jnp.float32)

    def one_slab(top_slab):
        return jnp.einsum("ibjxy,kbjyz->kixz", top_slab.astype(jnp.float32), wide, precision=HIGH)

    stacked = lax.map(one_slab, top_inverse)
    return jnp.transpose(stacked, (1, 0, 2, 3, 4))


def reference(top_inverse, upper_panel, upper_pattern, upper_diagonal, lower_panel, lower_pattern, parents, parent_panel, lower_diagonal):
    upper_mask = upper_pattern.astype(jnp.float32)[:, :, :, None, None]
    upper_masked = upper_panel * upper_mask.astype(jnp.bfloat16)
    upper_product = column_product(top_inverse, upper_masked)
    upper_columns = (-upper_product * upper_mask).astype(jnp.bfloat16)
    upper_blocks = upper_diagonal - jnp.einsum("ktsxy,ktsxz->kyz", upper_masked.astype(jnp.float32), upper_columns.astype(jnp.float32), precision=HIGH)
    lower_mask = lower_pattern.astype(jnp.float32)[:, :, :, None, None]
    lower_masked = lower_panel * lower_mask.astype(jnp.bfloat16)
    lower_product = column_product(top_inverse, lower_masked)
    selected = jnp.take(upper_columns, parents.astype(jnp.int32), axis=0).astype(jnp.float32)
    panel_wide = parent_panel.astype(jnp.float32)
    extension = jnp.einsum("mtsxy,myz->mtsxz", selected, panel_wide, precision=HIGH)
    lower_columns = (-(lower_product + extension) * lower_mask).astype(jnp.bfloat16)
    parent_blocks = jnp.take(upper_blocks, parents.astype(jnp.int32), axis=0)
    lower_cross = -jnp.einsum("mtsxy,mtsxz->myz", selected, lower_masked.astype(jnp.float32), precision=HIGH) - jnp.einsum("mxy,myz->mxz", parent_blocks, panel_wide, precision=HIGH)
    lower_blocks = lower_diagonal - jnp.einsum("mtsxy,mtsxz->myz", lower_masked.astype(jnp.float32), lower_columns.astype(jnp.float32), precision=HIGH) - jnp.einsum("myx,myz->mxz", panel_wide, lower_cross, precision=HIGH)
    return (upper_columns, upper_blocks, lower_columns, lower_cross, lower_blocks)
```

```python
import jax
import jax.numpy as jnp
from jax import lax
from jax.sharding import PartitionSpec as P

HIGH = lax.Precision.HIGHEST
ALL = ("row", "col")


def all_sum(blocks, count):
    shape = blocks.shape
    flat = blocks.reshape(-1, shape[-1])
    rows = flat.shape[0]
    chunk = -(-rows // (16 * count)) * 16
    flat = jnp.pad(flat.astype(jnp.bfloat16), ((0, chunk * count - rows), (0, 0)))
    parts = lax.all_to_all(
        flat.reshape(count, chunk, shape[-1]), ALL, split_axis=0, concat_axis=0, tiled=True
    )
    mine = jnp.sum(parts.astype(jnp.float32), axis=0).astype(jnp.bfloat16)
    spread = jnp.broadcast_to(mine[None], (count, chunk, shape[-1]))
    whole = lax.all_to_all(spread, ALL, split_axis=0, concat_axis=0, tiled=True)
    return whole.reshape(chunk * count, shape[-1])[:rows].reshape(shape).astype(jnp.float32)


def per_device(
    top_inverse,
    upper_panel,
    upper_pattern,
    upper_diagonal,
    lower_panel,
    lower_pattern,
    parents,
    parent_panel,
    lower_diagonal,
):
    count = lax.axis_size("row") * lax.axis_size("col")
    uppers = upper_panel.shape[0]
    block = upper_panel.shape[-1]
    upper_panel = upper_panel.reshape(-1, block, block)
    lower_panel = lower_panel.reshape(-1, block, block)
    upper_mask = upper_pattern.reshape(-1, 1, 1).astype(jnp.float32)
    lower_mask = lower_pattern.reshape(-1, 1, 1).astype(jnp.float32)
    masked = jnp.concatenate(
        [
            upper_panel * upper_mask.astype(jnp.bfloat16),
            lower_panel * lower_mask.astype(jnp.bfloat16),
        ]
    )
    upper_masked, lower_masked = masked[:uppers], masked[uppers:]
    gathered = lax.all_gather(masked, "col", axis=0)
    partial_value = jnp.einsum(
        "bjxy,bkxz->jkyz",
        top_inverse[0, :, :, 0],
        gathered,
        preferred_element_type=jnp.float32,
    ).astype(jnp.bfloat16)
    parts = lax.all_to_all(partial_value, "row", split_axis=0, concat_axis=0, tiled=True)
    product = jnp.sum(parts.astype(jnp.float32), axis=0)

    upper_columns = (-product[:uppers] * upper_mask).astype(jnp.bfloat16)
    selected = jnp.take(upper_columns, parents, axis=0)
    local_upper = jnp.einsum(
        "kxy,kxz->kyz", upper_masked, upper_columns, preferred_element_type=jnp.float32
    )
    local_cross = jnp.einsum(
        "mxy,mxz->myz", selected, lower_masked, preferred_element_type=jnp.float32
    )
    extension = jnp.einsum(
        "mxy,myz->mxz", selected, parent_panel, preferred_element_type=jnp.float32
    )
    lower_columns = (-(product[uppers:] + extension) * lower_mask).astype(jnp.bfloat16)
    local_lower = jnp.einsum(
        "mxy,mxz->myz", lower_masked, lower_columns, preferred_element_type=jnp.float32
    )
    sums = all_sum(jnp.concatenate([local_upper, local_cross, local_lower]), count)
    lowers = lower_panel.shape[0]
    summed_upper = sums[:uppers]
    summed_cross = sums[uppers : uppers + lowers]
    summed_lower = sums[uppers + lowers :]
    upper_blocks = upper_diagonal - summed_upper
    panel_wide = parent_panel.astype(jnp.float32)
    parent_blocks = jnp.take(upper_blocks, parents, axis=0)
    lower_cross = -summed_cross - jnp.einsum(
        "mxy,myz->mxz", parent_blocks, panel_wide, precision=HIGH
    )
    lower_blocks = (
        lower_diagonal
        - summed_lower
        - jnp.einsum("myx,myz->mxz", panel_wide, lower_cross, precision=HIGH)
    )
    return (
        upper_columns[:, None, None],
        upper_blocks,
        lower_columns[:, None, None],
        lower_cross,
        lower_blocks,
    )


def solution(mesh):
    return jax.shard_map(
        per_device,
        mesh=mesh,
        in_specs=(
            P("row", None, None, "col", None, None),
            P(None, "row", "col", None, None),
            P(None, "row", "col"),
            P(),
            P(None, "row", "col", None, None),
            P(None, "row", "col"),
            P(),
            P(),
            P(),
        ),
        out_specs=(
            P(None, "row", "col", None, None),
            P(),
            P(None, "row", "col", None, None),
            P(),
            P(),
        ),
        check_vma=False,
    )
```

```python
import jax
import jax.numpy as jnp
from jax import lax
from jax.sharding import PartitionSpec as P

HIGH = lax.Precision.HIGHEST
WIRE = jnp.bfloat16


def bits_of(axis):
    return lax.axis_size(axis).bit_length() - 1


def flip(value, axis, bit):
    size = lax.axis_size(axis)
    return lax.ppermute(value, axis, [(i, i ^ (1 << bit)) for i in range(size)])


def shift(value, axis, step):
    size = lax.axis_size(axis)
    return lax.ppermute(value, axis, [(i, (i + step) % size) for i in range(size)])


def gather_shifts(value, axis):
    size = lax.axis_size(axis)
    me = lax.axis_index(axis)
    pieces = jnp.stack([value] + [shift(value, axis, s) for s in range(1, size)])
    return jnp.take(pieces, (me - jnp.arange(size)) % size, axis=0)


def scatter_shifts(parts, axis):
    size = lax.axis_size(axis)
    me = lax.axis_index(axis)
    total = lax.dynamic_index_in_dim(parts, me, 0, keepdims=False)
    for s in range(1, size):
        piece = lax.dynamic_index_in_dim(parts, (me + s) % size, 0, keepdims=False)
        total = total + shift(piece, axis, s)
    return total


def scatter_halves(parts, axis, order):
    me = lax.axis_index(axis)
    left = sorted(order, reverse=True)
    value = parts.reshape((2,) * len(left) + parts.shape[1:])
    for bit in order:
        place = left.index(bit)
        mine = (me >> bit) & 1
        away = lax.dynamic_index_in_dim(value, 1 - mine, place, keepdims=False)
        keep = lax.dynamic_index_in_dim(value, mine, place, keepdims=False)
        kind = jnp.float32 if bit == 0 else WIRE
        value = keep.astype(jnp.float32) + flip(away.astype(kind), axis, bit).astype(jnp.float32)
        left.remove(bit)
    return value


def gather_doubles(value, axis, order):
    me = lax.axis_index(axis)
    done = []
    for bit in order:
        done = sorted(done + [bit], reverse=True)
        place = done.index(bit)
        other = flip(value, axis, bit)
        mine = (me >> bit) & 1
        value = jnp.stack(
            [jnp.where(mine == 0, value, other), jnp.where(mine == 0, other, value)], axis=place
        )
    return value


def all_sum(blocks):
    shape = blocks.shape
    rows_n, cols_n = lax.axis_size("row"), lax.axis_size("col")
    count = rows_n * cols_n
    flat = blocks.reshape(-1, shape[-1])
    rows = flat.shape[0]
    chunk = -(-rows // (16 * count)) * 16
    flat = jnp.pad(flat, ((0, chunk * count - rows), (0, 0)))
    parts = flat.reshape(rows_n, cols_n * chunk, shape[-1])
    order = list(range(bits_of("row")))
    part = scatter_halves(parts, "row", order)
    part = scatter_shifts(part.reshape(cols_n, chunk, shape[-1]), "col")
    part = gather_shifts(part.astype(WIRE), "col").reshape(cols_n * chunk, shape[-1])
    whole = gather_doubles(part, "row", order[::-1])
    return whole.reshape(chunk * count, shape[-1])[:rows].reshape(shape).astype(jnp.float32)


def product_parts(top, gathered):
    return jnp.einsum("bjxy,bkxz->jkyz", top, gathered, preferred_element_type=jnp.float32)


def per_device(
    top_inverse,
    upper_panel,
    upper_pattern,
    upper_diagonal,
    lower_panel,
    lower_pattern,
    parents,
    parent_panel,
    lower_diagonal,
):
    uppers, block = upper_panel.shape[0], upper_panel.shape[-1]
    lowers = lower_panel.shape[0]
    top = top_inverse[0, :, :, 0]
    upper_mask = upper_pattern.reshape(-1, 1, 1).astype(jnp.float32)
    lower_mask = lower_pattern.reshape(-1, 1, 1).astype(jnp.float32)
    upper_masked = upper_panel.reshape(-1, block, block) * upper_mask.astype(jnp.bfloat16)
    lower_masked = lower_panel.reshape(-1, block, block) * lower_mask.astype(jnp.bfloat16)
    order = list(range(bits_of("row")))
    turned = order[:1] + order[1:][::-1]

    upper_parts = product_parts(top, gather_shifts(upper_masked, "col"))
    upper_product = scatter_halves(upper_parts, "row", order)
    upper_columns = (-upper_product * upper_mask).astype(jnp.bfloat16)
    selected = jnp.take(upper_columns, parents, axis=0)
    local_upper = jnp.einsum(
        "kxy,kxz->kyz", upper_masked, upper_columns, preferred_element_type=jnp.float32
    )
    local_cross = jnp.einsum(
        "mxy,mxz->myz", selected, lower_masked, preferred_element_type=jnp.float32
    )
    first = all_sum(jnp.concatenate([local_upper, local_cross]))

    lower_parts = product_parts(top, gather_shifts(lower_masked, "col"))
    half = lowers // 2
    lower_product = jnp.concatenate(
        [
            scatter_halves(lower_parts[:, :half], "row", order),
            scatter_halves(lower_parts[:, half:], "row", turned),
        ]
    )
    extension = jnp.einsum(
        "mxy,myz->mxz", selected, parent_panel, preferred_element_type=jnp.float32
    )
    lower_columns = (-(lower_product + extension) * lower_mask).astype(jnp.bfloat16)
    local_lower = jnp.einsum(
        "mxy,mxz->myz", lower_masked, lower_columns, preferred_element_type=jnp.float32
    )
    summed_lower = all_sum(local_lower)

    upper_blocks = upper_diagonal - first[:uppers]
    panel_wide = parent_panel.astype(jnp.float32)
    parent_blocks = jnp.take(upper_blocks, parents, axis=0)
    lower_cross = -first[uppers:] - jnp.einsum(
        "mxy,myz->mxz", parent_blocks, panel_wide, precision=HIGH
    )
    lower_blocks = (
        lower_diagonal
        - summed_lower
        - jnp.einsum("myx,myz->mxz", panel_wide, lower_cross, precision=HIGH)
    )
    return (
        upper_columns[:, None, None],
        upper_blocks,
        lower_columns[:, None, None],
        lower_cross,
        lower_blocks,
    )


def solution(mesh):
    return jax.shard_map(
        per_device,
        mesh=mesh,
        in_specs=(
            P("row", None, None, "col", None, None),
            P(None, "row", "col", None, None),
            P(None, "row", "col"),
            P(),
            P(None, "row", "col", None, None),
            P(None, "row", "col"),
            P(),
            P(),
            P(),
        ),
        out_specs=(
            P(None, "row", "col", None, None),
            P(),
            P(None, "row", "col", None, None),
            P(),
            P(),
        ),
        check_vma=False,
    )
```

```python
import functools

import jax
import jax.numpy as jnp
from jax import lax
from jax.experimental import pallas as pl
from jax.experimental.pallas import tpu as pltpu
from jax.sharding import PartitionSpec as P

F32 = jnp.float32
WIRE = jnp.bfloat16
PARAMS = pltpu.CompilerParams(vmem_limit_bytes=56 * 1024 * 1024)
VMEM = pl.BlockSpec(memory_space=pltpu.VMEM)
SMEM = pl.BlockSpec(memory_space=pltpu.SMEM)


def shape_of(dims, kind):
    return jax.ShapeDtypeStruct(dims, kind)


def flip(value, axis, mask):
    size = lax.axis_size(axis)
    return lax.ppermute(value, axis, [(i, i ^ mask) for i in range(size)])


def shift(value, axis, step):
    size = lax.axis_size(axis)
    return lax.ppermute(value, axis, [(i, (i + step) % size) for i in range(size)])


def mask_kernel(upper_pattern, lower_pattern, upper_panel, lower_panel, masked, turned):
    uppers, lowers = upper_panel.shape[0], lower_panel.shape[0]
    for k in range(uppers + lowers):
        if k < uppers:
            value = upper_panel[k].astype(F32) * upper_pattern[k].astype(F32)
        else:
            value = lower_panel[k - uppers].astype(F32) * lower_pattern[k - uppers].astype(F32)
        masked[k] = value.astype(jnp.bfloat16)
        turned[k] = value.T.astype(jnp.bfloat16)


def turn_kernel(place, top, out):
    depth, width, block, _ = top.shape

    def step(index, carry):
        m, o = index // depth, index % depth
        tile = top[(place[1] + o) % depth, place[0] ^ m].astype(F32).T
        out[o, pl.ds(pl.multiple_of(m * block, block), block), :] = tile.astype(jnp.bfloat16)
        return carry

    lax.fori_loop(0, depth * width, step, 0)


def product_kernel(depth, width, uppers, parents, top, *refs):
    pieces, turned = refs[:depth], refs[depth : depth + width]
    keep, away, sums, both = refs[depth + width :]
    total, block = pieces[0].shape[0], pieces[0].shape[-1]
    lowers = total - uppers

    def columns(pair, carry):
        first = 2 * pair
        second = jnp.minimum(first + 1, total - 1)
        value = jnp.zeros((width * block, 2 * block), F32)
        for o in range(0, depth, 2):
            span = range(o, min(o + 2, depth))
            left = jnp.concatenate([top[i] for i in span], axis=1)
            right = jnp.concatenate(
                [jnp.concatenate([pieces[i][first], pieces[i][second]], axis=1) for i in span],
                axis=0,
            )
            value = value + jnp.dot(left, right, preferred_element_type=F32)
        for half, k in enumerate((first, second)):
            part = value[:, half * block : (half + 1) * block]
            for m in range(width):
                tile = part[m * block : (m + 1) * block]
                (away if m & 1 else keep)[m // 2, k] = tile
            high = part.astype(jnp.bfloat16)
            both[k, :, :block] = high
            both[k, :, block:] = (part - high.astype(F32)).astype(jnp.bfloat16)
        return carry

    lax.fori_loop(0, -(-total // 2), columns, 0)

    def fold(rows, k):
        value = jnp.dot(rows, both[k], preferred_element_type=F32)
        return value[:, :block] + value[:, block:]

    def row_of(k):
        return jnp.concatenate([turned[m][k] for m in range(width)], axis=1)

    def upper_step(k, carry):
        sums[k] = fold(row_of(k), k)
        return carry

    def lower_step(m, carry):
        rows = jnp.concatenate([row_of(uppers + m), row_of(parents[m])], axis=0)
        value = fold(rows, uppers + m)
        sums[uppers + lowers + m] = value[:block]
        sums[uppers + m] = value[block:]
        return carry

    lax.fori_loop(0, uppers, upper_step, 0)
    lax.fori_loop(0, lowers, lower_step, 0)


def columns_kernel(parents, upper_pattern, lower_pattern, product, panel, upper_out, lower_out):
    uppers, lowers = upper_out.shape[0], lower_out.shape[0]
    for k in range(uppers):
        value = -product[k] * upper_pattern[k].astype(F32)
        upper_out[k] = value.astype(jnp.bfloat16)
    for m in range(lowers):
        extension = jnp.dot(upper_out[parents[m]], panel[m], preferred_element_type=F32)
        value = -(product[uppers + m] + extension) * lower_pattern[m].astype(F32)
        lower_out[m] = value.astype(jnp.bfloat16)


def split_dot(wide, narrow):
    high = wide.astype(jnp.bfloat16)
    rest = wide - high.astype(F32)
    low = rest.astype(jnp.bfloat16)
    last = (rest - low.astype(F32)).astype(jnp.bfloat16)
    value = jnp.dot(last, narrow, preferred_element_type=F32)
    value = value + jnp.dot(low, narrow, preferred_element_type=F32)
    return value + jnp.dot(high, narrow, preferred_element_type=F32)


def blocks_kernel(
    parents, sums, upper_diagonal, lower_diagonal, panel, upper_out, cross_out, lower_out
):
    uppers, lowers = upper_out.shape[0], lower_out.shape[0]
    for k in range(uppers):
        upper_out[k] = upper_diagonal[k] + sums[k].astype(F32)
    for m in range(lowers):
        forms = sums[uppers + m].astype(F32)
        cross = forms - split_dot(upper_out[parents[m]], panel[m])
        cross_out[m] = cross
        back = split_dot(forms.T, panel[m]) + split_dot(cross.T, panel[m]).T
        lower_out[m] = lower_diagonal[m] + sums[uppers + lowers + m].astype(F32) - back


def gather_shifts(value, axis):
    size = lax.axis_size(axis)
    return [value] + [shift(value, axis, -o) for o in range(1, size)]


def gather_flips(value, axis):
    pieces = [value]
    for m in range(1, lax.axis_size(axis)):
        pieces.append(flip(pieces[m - 1], axis, 1) if m & 1 else flip(value, axis, m))
    return pieces


def scatter_halves(parts, axis, order):
    me = lax.axis_index(axis)
    left = sorted(order, reverse=True)
    value = parts.reshape((2,) * len(left) + parts.shape[1:])
    for bit in order:
        place = left.index(bit)
        mine = (me >> bit) & 1
        away = lax.dynamic_index_in_dim(value, 1 - mine, place, keepdims=False)
        keep = lax.dynamic_index_in_dim(value, mine, place, keepdims=False)
        kind = F32 if bit == 0 else WIRE
        value = keep + flip(away.astype(kind), axis, 1 << bit).astype(F32)
        left.remove(bit)
    return value


def gather_doubles(value, axis, order):
    me = lax.axis_index(axis)
    done = []
    for bit in order:
        done = sorted(done + [bit], reverse=True)
        place = done.index(bit)
        other = flip(value, axis, 1 << bit)
        mine = (me >> bit) & 1
        value = jnp.stack(
            [jnp.where(mine == 0, value, other), jnp.where(mine == 0, other, value)], axis=place
        )
    return value


def all_sum(blocks):
    shape = blocks.shape
    rows_n, cols_n = lax.axis_size("row"), lax.axis_size("col")
    order = list(range(rows_n.bit_length() - 1))
    part = scatter_halves(blocks.reshape(rows_n, -1, shape[-1]), "row", order)
    me = lax.axis_index("col")
    pieces = jnp.stack(gather_shifts(part.astype(WIRE), "col"))
    total = lax.dynamic_index_in_dim(pieces, (-me) % cols_n, 0, keepdims=False).astype(F32)
    for c in range(1, cols_n):
        piece = lax.dynamic_index_in_dim(pieces, (c - me) % cols_n, 0, keepdims=False)
        total = total + piece.astype(F32)
    whole = gather_doubles(total.astype(WIRE), "row", order[::-1])
    return whole.reshape(shape)


def scatter_relative(value, axis, order):
    left = list(range(len(order), 0, -1))
    value = value.reshape((2,) * len(left) + value.shape[1:])
    for bit in order:
        place = left.index(bit)
        away = lax.index_in_dim(value, 1, place, keepdims=False).astype(WIRE)
        keep = lax.index_in_dim(value, 0, place, keepdims=False)
        value = keep + flip(away, axis, 1 << bit).astype(F32)
        left.remove(bit)
    return value


def per_device(
    top_inverse,
    upper_panel,
    upper_pattern,
    upper_diagonal,
    lower_panel,
    lower_pattern,
    parents,
    parent_panel,
    lower_diagonal,
):
    uppers, block = upper_panel.shape[0], upper_panel.shape[-1]
    lowers = lower_panel.shape[0]
    total = uppers + lowers
    width, depth = lax.axis_size("row"), lax.axis_size("col")
    upper_pattern, lower_pattern = upper_pattern.reshape(-1), lower_pattern.reshape(-1)
    place = jnp.stack([lax.axis_index("row"), lax.axis_index("col")])

    masked, turned = pl.pallas_call(
        mask_kernel,
        out_shape=[shape_of((total, block, block), jnp.bfloat16)] * 2,
        in_specs=[SMEM, SMEM, VMEM, VMEM],
        out_specs=[VMEM, VMEM],
        name="mask",
    )(
        upper_pattern,
        lower_pattern,
        upper_panel.reshape(-1, block, block),
        lower_panel.reshape(-1, block, block),
    )
    pieces = gather_shifts(masked, "col")
    across = gather_flips(turned, "row")

    top = pl.pallas_call(
        turn_kernel,
        out_shape=shape_of((depth, width * block, block), jnp.bfloat16),
        in_specs=[SMEM, VMEM],
        out_specs=VMEM,
        compiler_params=PARAMS,
        name="turn",
    )(place, top_inverse[0, :, :, 0])

    keep, away, sums = pl.pallas_call(
        functools.partial(product_kernel, depth, width, uppers),
        out_shape=[
            shape_of((width // 2, total, block, block), F32),
            shape_of((width // 2, total, block, block), F32),
            shape_of((uppers + 2 * lowers, block, block), F32),
        ],
        in_specs=[SMEM] + [VMEM] * (1 + depth + width),
        out_specs=[VMEM] * 3,
        scratch_shapes=[pltpu.VMEM((total, width * block, 2 * block), jnp.bfloat16)],
        compiler_params=PARAMS,
        name="product",
    )(parents, top, *pieces, *across)

    sums = all_sum(sums)
    value = keep + flip(away, "row", 1)
    order = list(range(1, width.bit_length() - 1))
    half = total // 2
    product = jnp.concatenate(
        [
            scatter_relative(value[:, :half], "row", order),
            scatter_relative(value[:, half:], "row", order[::-1]),
        ]
    )
    upper_columns, lower_columns = pl.pallas_call(
        columns_kernel,
        out_shape=[
            shape_of((uppers, block, block), jnp.bfloat16),
            shape_of((lowers, block, block), jnp.bfloat16),
        ],
        in_specs=[SMEM, SMEM, SMEM, VMEM, VMEM],
        out_specs=[VMEM, VMEM],
        name="columns",
    )(parents, upper_pattern, lower_pattern, product, parent_panel)

    upper_blocks, lower_cross, lower_blocks = pl.pallas_call(
        blocks_kernel,
        out_shape=[
            shape_of((uppers, block, block), F32),
            shape_of((lowers, block, block), F32),
            shape_of((lowers, block, block), F32),
        ],
        in_specs=[SMEM, VMEM, VMEM, VMEM, VMEM],
        out_specs=[VMEM] * 3,
        name="blocks",
    )(parents, sums, upper_diagonal, lower_diagonal, parent_panel)
    return (
        upper_columns[:, None, None],
        upper_blocks,
        lower_columns[:, None, None],
        lower_cross,
        lower_blocks,
    )


def solution(mesh):
    return jax.shard_map(
        per_device,
        mesh=mesh,
        in_specs=(
            P("row", None, None, "col", None, None),
            P(None, "row", "col", None, None),
            P(None, "row", "col"),
            P(),
            P(None, "row", "col", None, None),
            P(None, "row", "col"),
            P(),
            P(),
            P(),
        ),
        out_specs=(
            P(None, "row", "col", None, None),
            P(),
            P(None, "row", "col", None, None),
            P(),
            P(),
        ),
        check_vma=False,
    )
```

```python
import functools

import jax
import jax.numpy as jnp
import numpy as np
from jax import lax
from jax.experimental import pallas as pl
from jax.experimental.pallas import tpu as pltpu
from jax.sharding import PartitionSpec as P

F32 = jnp.float32
WIRE = jnp.bfloat16
VMEM = pl.BlockSpec(memory_space=pltpu.VMEM)
SMEM = pl.BlockSpec(memory_space=pltpu.SMEM)


def shape_of(dims, kind):
    return jax.ShapeDtypeStruct(dims, kind)


def flip(value, axis, mask):
    size = lax.axis_size(axis)
    return lax.ppermute(value, axis, [(i, i ^ mask) for i in range(size)])


def shift(value, axis, step):
    size = lax.axis_size(axis)
    return lax.ppermute(value, axis, [(i, (i + step) % size) for i in range(size)])


def ceil_to(value, step):
    return -(-value // step) * step


def params(refs):
    size = sum(int(np.prod(r.shape)) * np.dtype(r.dtype).itemsize for r in refs)
    return pltpu.CompilerParams(vmem_limit_bytes=ceil_to(size * 5 // 4, 1 << 20) + (4 << 20))


def call(kernel, name, scalars, arrays, outs, scratch=()):
    return pl.pallas_call(
        kernel,
        out_shape=outs,
        in_specs=[SMEM] * len(scalars) + [VMEM] * len(arrays),
        out_specs=[VMEM] * len(outs),
        scratch_shapes=[pltpu.VMEM(r.shape, r.dtype) for r in scratch],
        compiler_params=params([*arrays, *outs, *scratch]),
        name=name,
    )(*scalars, *arrays)


def mask_kernel(upper_pattern, lower_pattern, upper_panel, lower_panel, masked):
    uppers, lowers = upper_panel.shape[0], lower_panel.shape[0]
    for k in range(uppers):
        masked[k] = upper_panel[k] * upper_pattern[k].astype(F32).astype(jnp.bfloat16)
    for m in range(lowers):
        masked[uppers + m] = lower_panel[m] * lower_pattern[m].astype(F32).astype(jnp.bfloat16)


def turn_kernel(masked, turned):
    for k in range(masked.shape[0]):
        turned[k] = masked[k].T


def top_kernel(top, panel, out, panel_turned):
    depth, width, block, _ = top.shape
    row, col = lax.axis_index("row"), lax.axis_index("col")

    def step(m, carry):
        for o in range(depth):
            tile = top[lax.rem(col + o, depth), row ^ m].T
            out[pl.ds(pl.multiple_of(m * block, block), block), o * block : (o + 1) * block] = tile
        return carry

    lax.fori_loop(0, width, step, 0)
    for m in range(panel.shape[0]):
        panel_turned[m] = panel[m].T


def product_kernel(depth, width, uppers, parents, top, *refs):
    own, ups, downs = refs[0], refs[1:depth], refs[depth : 2 * depth - 1]
    near, far, keep, away, sums_keep, sums_away, both, forms = refs[2 * depth - 1 :]
    total, block = own.shape[0], own.shape[-1]
    lowers = total - uppers
    chunk = block // width
    row, col = lax.axis_index("row"), lax.axis_index("col")

    def piece(o, k):
        if o == 0:
            return own[k]
        return jnp.where(col + o < depth, downs[o - 1][k], ups[depth - o - 1][k])

    def columns(pair, carry):
        first = 2 * pair
        second = jnp.minimum(first + 1, total - 1)
        right = jnp.concatenate(
            [jnp.concatenate([piece(o, first), piece(o, second)], axis=1) for o in range(depth)],
            axis=0,
        )
        value = jnp.dot(top[...], right, preferred_element_type=F32)
        for half, k in enumerate((first, second)):
            part = value[:, half * block : (half + 1) * block]
            for m in range(width):
                tile = part[m * block : (m + 1) * block]
                (away if m & 1 else keep)[m // 2, k] = tile
            high = part.astype(jnp.bfloat16)
            both[k, :, :block] = high
            both[k, :, block:] = (part - high.astype(F32)).astype(jnp.bfloat16)
        return carry

    lax.fori_loop(0, ceil_to(total, 2) // 2, columns, 0)

    def fold(rows, k):
        value = jnp.dot(rows, both[k], preferred_element_type=F32)
        return value[:, :block] + value[:, block:]

    def row_of(k):
        return jnp.concatenate([(far if m & 1 else near)[m // 2, k] for m in range(width)], axis=1)

    def spread(slot, i):
        for m in range(width):
            start = pl.multiple_of((row ^ m) * chunk, chunk)
            (sums_away if m & 1 else sums_keep)[m // 2, i] = forms[slot, pl.ds(start, chunk)]

    def upper_step(k, carry):
        forms[0] = fold(row_of(k), k)
        spread(0, k)
        return carry

    def lower_step(m, carry):
        rows = jnp.concatenate([row_of(uppers + m), row_of(parents[m])], axis=0)
        value = fold(rows, uppers + m)
        forms[0] = value[:block]
        forms[1] = value[block:]
        spread(0, uppers + lowers + m)
        spread(1, uppers + m)
        return carry

    lax.fori_loop(0, uppers, upper_step, 0)
    lax.fori_loop(0, lowers, lower_step, 0)


def middle_kernel(
    depth, width, parents, upper_pattern, lower_pattern, panel, keep, *refs
):
    count = width // 2 - 1
    got, parts = refs[:count], refs[count : count + depth]
    upper_out, lower_out, total_out, order, product = refs[count + depth :]
    col = lax.axis_index("col")
    for o in range(depth):
        order[lax.rem(col + o, depth)] = parts[o][...].astype(F32)
    total = order[0]
    for c in range(1, depth):
        total = total + order[c]
    total_out[...] = total.astype(total_out.dtype)
    value = keep[...]
    for piece in got:
        value = value + piece[...].astype(F32)
    product[...] = value
    uppers, lowers = upper_out.shape[0], lower_out.shape[0]
    for k in range(uppers):
        upper_out[k] = (-product[k] * upper_pattern[k].astype(F32)).astype(jnp.bfloat16)
    for m in range(lowers):
        extension = jnp.dot(upper_out[parents[m]], panel[m], preferred_element_type=F32)
        value = -(product[uppers + m] + extension) * lower_pattern[m].astype(F32)
        lower_out[m] = value.astype(jnp.bfloat16)


def split(wide):
    high = wide.astype(jnp.bfloat16)
    return high, (wide - high.astype(F32)).astype(jnp.bfloat16)


def blocks_kernel(
    width,
    parents,
    near,
    far,
    upper_diagonal,
    lower_diagonal,
    panel,
    panel_turned,
    upper_out,
    cross_out,
    lower_out,
    sums,
    halves,
):
    uppers, lowers = upper_out.shape[0], lower_out.shape[0]
    block = panel.shape[-1]
    chunk = block // width
    row = lax.axis_index("row")
    for m in range(width):
        start = pl.multiple_of((row ^ m) * chunk, chunk)
        sums[:, pl.ds(start, chunk)] = (far if m & 1 else near)[m // 2].astype(F32)
    for k in range(uppers):
        value = upper_diagonal[k] + sums[k]
        upper_out[k] = value
        halves[k, :block], halves[k, block:] = split(value)
    for m in range(lowers):
        forms = sums[uppers + m]
        value = jnp.dot(halves[parents[m]], panel[m], preferred_element_type=F32)
        cross = forms - (value[:block] + value[block:])
        cross_out[m] = cross
        right = jnp.concatenate([forms.astype(jnp.bfloat16), *split(cross)], axis=1)
        value = jnp.dot(panel_turned[m], right, preferred_element_type=F32)
        back = value[:, :block].T + value[:, block : 2 * block] + value[:, 2 * block :]
        lower_out[m] = lower_diagonal[m] + sums[uppers + lowers + m] - back


def gather_shifts(value, axis):
    size = lax.axis_size(axis)
    return [value] + [shift(value, axis, -o) for o in range(1, size)]


def gather_line(value, axis):
    size = lax.axis_size(axis)
    ups, downs = [value], [value]
    for s in range(1, size):
        ups.append(lax.ppermute(ups[-1], axis, [(i, i + 1) for i in range(s - 1, size - 1)]))
        downs.append(lax.ppermute(downs[-1], axis, [(i + 1, i) for i in range(size - s)]))
    return ups[1:] + downs[1:]


def gather_near(value, axis):
    masks = range(2, lax.axis_size(axis), 2)
    return jnp.stack([value] + [flip(value, axis, m) for m in masks])


def tie(*values):
    return lax.optimization_barrier(values)


def scatter_flips(value, axis):
    masks = range(2, lax.axis_size(axis), 2)
    return [flip(value[m // 2].astype(WIRE), axis, m) for m in masks]


def per_device(
    top_inverse,
    upper_panel,
    upper_pattern,
    upper_diagonal,
    lower_panel,
    lower_pattern,
    parents,
    parent_panel,
    lower_diagonal,
):
    uppers, block = upper_panel.shape[0], upper_panel.shape[-1]
    lowers = lower_panel.shape[0]
    total = uppers + lowers
    sums_n = total + lowers
    width, depth = lax.axis_size("row"), lax.axis_size("col")
    half, chunk = width // 2, block // width
    bf16 = jnp.bfloat16
    upper_pattern, lower_pattern = upper_pattern.reshape(-1), lower_pattern.reshape(-1)

    (masked,) = call(
        mask_kernel,
        "mask",
        (upper_pattern, lower_pattern),
        (upper_panel.reshape(-1, block, block), lower_panel.reshape(-1, block, block)),
        [shape_of((total, block, block), bf16)],
    )
    pieces = gather_line(masked, "col")
    (turned,) = call(turn_kernel, "turn", (), (masked,), [shape_of(masked.shape, bf16)])
    near = gather_near(turned, "row")
    near, *pieces[depth - 3 :: depth - 1] = tie(near, *pieces[depth - 3 :: depth - 1])
    far = flip(near, "row", 1)
    top, panel_turned = call(
        top_kernel,
        "top",
        (),
        (top_inverse[0, :, :, 0], parent_panel),
        [shape_of((width * block, depth * block), bf16), shape_of(parent_panel.shape, bf16)],
    )

    keep, away, sums_keep, sums_away = call(
        functools.partial(product_kernel, depth, width, uppers),
        "product",
        (parents,),
        (top, masked, *pieces, near, far),
        [shape_of((half, total, block, block), F32)] * 2
        + [shape_of((half, sums_n, chunk, block), F32)] * 2,
        [
            shape_of((total, width * block, 2 * block), bf16),
            shape_of((2, block, block), F32),
        ],
    )

    other, away = tie(flip(sums_away, "row", 1), away)
    sums = sums_keep + other
    part = sums[0]
    for piece in scatter_flips(sums, "row"):
        part = part + piece.astype(F32)
    parts = gather_shifts(part.astype(WIRE), "col")

    product = keep + flip(away, "row", 1)
    got = scatter_flips(product, "row")
    upper_columns, lower_columns, part = call(
        functools.partial(middle_kernel, depth, width),
        "middle",
        (parents, upper_pattern, lower_pattern),
        (parent_panel, product[0], *got, *parts),
        [
            shape_of((uppers, block, block), bf16),
            shape_of((lowers, block, block), bf16),
            shape_of((sums_n, chunk, block), WIRE),
        ],
        [shape_of((depth, sums_n, chunk, block), F32), shape_of((total, block, block), F32)],
    )
    near = gather_near(part, "row")
    far = flip(near, "row", 1)

    upper_blocks, lower_cross, lower_blocks = call(
        functools.partial(blocks_kernel, width),
        "blocks",
        (parents,),
        (near, far, upper_diagonal, lower_diagonal, parent_panel, panel_turned),
        [
            shape_of((uppers, block, block), F32),
            shape_of((lowers, block, block), F32),
            shape_of((lowers, block, block), F32),
        ],
        [shape_of((sums_n, block, block), F32), shape_of((uppers, 2 * block, block), bf16)],
    )
    return (
        upper_columns[:, None, None],
        upper_blocks,
        lower_columns[:, None, None],
        lower_cross,
        lower_blocks,
    )


def solution(mesh):
    return jax.shard_map(
        per_device,
        mesh=mesh,
        in_specs=(
            P("row", None, None, "col", None, None),
            P(None, "row", "col", None, None),
            P(None, "row", "col"),
            P(),
            P(None, "row", "col", None, None),
            P(None, "row", "col"),
            P(),
            P(),
            P(),
        ),
        out_specs=(
            P(None, "row", "col", None, None),
            P(),
            P(None, "row", "col", None, None),
            P(),
            P(),
        ),
        check_vma=False,
    )
```

```python
import functools

import jax
import jax.numpy as jnp
import numpy as np
from jax import lax
from jax.experimental import pallas as pl
from jax.experimental.pallas import tpu as pltpu
from jax.sharding import PartitionSpec as P

F32 = jnp.float32
WIRE = jnp.bfloat16
VMEM = pl.BlockSpec(memory_space=pltpu.VMEM)
SMEM = pl.BlockSpec(memory_space=pltpu.SMEM)


def shape_of(dims, kind):
    return jax.ShapeDtypeStruct(dims, kind)


def flip(value, axis, mask):
    size = lax.axis_size(axis)
    return lax.ppermute(value, axis, [(i, i ^ mask) for i in range(size)])


def shift(value, axis, step):
    size = lax.axis_size(axis)
    return lax.ppermute(value, axis, [(i, (i + step) % size) for i in range(size)])


def ceil_to(value, step):
    return -(-value // step) * step


def params(refs, limit):
    size = sum(int(np.prod(r.shape)) * np.dtype(r.dtype).itemsize for r in refs)
    return pltpu.CompilerParams(vmem_limit_bytes=limit or ceil_to(size * 5 // 4, 1 << 20) + (4 << 20))


def call(kernel, name, scalars, arrays, outs, scratch=(), limit=0):
    return pl.pallas_call(
        kernel,
        out_shape=outs,
        in_specs=[SMEM] * len(scalars) + [VMEM] * len(arrays),
        out_specs=[VMEM] * len(outs),
        scratch_shapes=[pltpu.VMEM(r.shape, r.dtype) for r in scratch],
        compiler_params=params([*arrays, *outs, *scratch], limit),
        name=name,
    )(*scalars, *arrays)


def mask_kernel(upper_pattern, lower_pattern, upper_panel, lower_panel, masked):
    uppers, lowers = upper_panel.shape[0], lower_panel.shape[0]
    for k in range(uppers):
        masked[k] = upper_panel[k] * upper_pattern[k].astype(F32).astype(jnp.bfloat16)
    for m in range(lowers):
        masked[uppers + m] = lower_panel[m] * lower_pattern[m].astype(F32).astype(jnp.bfloat16)


def turn_kernel(*refs):
    pieces, turned = refs[:-1], refs[-1]
    total, block = pieces[0].shape[0], pieces[0].shape[-1]
    for k in range(total):
        for o, piece in enumerate(pieces):
            turned[k, :, o * block : (o + 1) * block] = piece[k].T


def top_kernel(top, panel, out, panel_turned):
    depth, width, block, _ = top.shape
    row, col = lax.axis_index("row"), lax.axis_index("col")
    half = width // 2

    def step(o, carry):
        start = pl.multiple_of(o * block, block)
        for i in range(width):
            m = 2 * (i % half) + i // half
            tile = top[lax.rem(col + o, depth), row ^ m]
            out[i // half, pl.ds(start, block), (i % half) * block : (i % half + 1) * block] = tile
        return carry

    lax.fori_loop(0, depth, step, 0)
    for m in range(panel.shape[0]):
        panel_turned[m] = panel[m].T


def dot_pair(left, pieces, first, second):
    right = [
        jnp.concatenate([pieces[i, first], pieces[i, second]], axis=1)
        for i in range(pieces.shape[0])
    ]
    return jnp.dot(left, jnp.concatenate(right), preferred_element_type=F32)


def first_kernel(top, near, out):
    total = near.shape[1]
    for first in range(0, total, 2):
        out[first // 2] = dot_pair(top[0], near, first, min(first + 1, total - 1))


def second_kernel(uppers, parents, top, far, start, turned, *refs):
    own, returns, (sums_keep, sums_away, both, forms) = refs[0], refs[1:-4], refs[-4:]
    total, block, reach = turned.shape
    lowers = total - uppers
    half, _, chunk, _ = sums_keep.shape
    row = lax.axis_index("row")

    for first in range(0, total, 2):
        second = min(first + 1, total - 1)
        value = start[first // 2] + dot_pair(top[1], far, first, second)
        for lane, k in enumerate(range(first, second + 1)):
            part = value[:, lane * block : (lane + 1) * block]
            own[k] = part[:block]
            for o, out in enumerate(returns):
                out[k] = part[(o + 1) * block : (o + 2) * block].astype(WIRE)
            part = jnp.concatenate([0.5 * part[:block], part[block:reach]])
            high = part.astype(jnp.bfloat16)
            both[k, :, :block] = high
            both[k, :, block:] = (part - high.astype(F32)).astype(jnp.bfloat16)

    def fold(rows, k):
        value = jnp.dot(rows, both[k], preferred_element_type=F32)
        return value[:, :block] + value[:, block:]

    def spread(slot, index):
        for m in range(2 * half):
            place = pl.multiple_of((row ^ m) * chunk, chunk)
            (sums_away if m & 1 else sums_keep)[m // 2, index] = forms[slot, pl.ds(place, chunk)]

    for k in range(uppers):
        forms[k] = fold(turned[k], k)
        spread(k, k)
    for m in range(lowers):
        own_row, parent = turned[uppers + m], parents[m]
        value = fold(jnp.concatenate([own_row, turned[parent]], axis=0), uppers + m)
        slot = uppers + 2 * m
        forms[slot] = value[:block]
        forms[slot + 1] = value[block:] + fold(own_row, parent).T
        spread(slot, total + m)
        spread(slot + 1, uppers + m)


def line_kernel(*refs):
    parts, (total_out, order) = refs[:-2], refs[-2:]
    depth, col = len(parts), lax.axis_index("col")
    for o in range(depth):
        order[lax.rem(col + o, depth)] = parts[o][...].astype(F32)
    total = order[0]
    for c in range(1, depth):
        total = total + order[c]
    total_out[...] = total.astype(total_out.dtype)


def columns_kernel(parents, upper_pattern, lower_pattern, panel, own, *refs):
    got, (upper_out, lower_out) = refs[:-2], refs[-2:]
    uppers, lowers = upper_out.shape[0], lower_out.shape[0]

    def product(k):
        value = own[k]
        for piece in got:
            value = value + piece[k].astype(F32)
        return value

    for k in range(uppers):
        upper_out[k] = (-product(k) * upper_pattern[k].astype(F32)).astype(jnp.bfloat16)
    for m in range(lowers):
        extension = jnp.dot(upper_out[parents[m]], panel[m], preferred_element_type=F32)
        value = -(product(uppers + m) + extension) * lower_pattern[m].astype(F32)
        lower_out[m] = value.astype(jnp.bfloat16)


def split(wide):
    high = wide.astype(jnp.bfloat16)
    return high, (wide - high.astype(F32)).astype(jnp.bfloat16)


def blocks_kernel(
    width,
    parents,
    near,
    far,
    upper_diagonal,
    lower_diagonal,
    panel,
    panel_turned,
    upper_out,
    cross_out,
    lower_out,
    sums,
    halves,
):
    uppers, lowers = upper_out.shape[0], lower_out.shape[0]
    block = panel.shape[-1]
    chunk = block // width
    row = lax.axis_index("row")
    for m in range(width):
        start = pl.multiple_of((row ^ m) * chunk, chunk)
        sums[:, pl.ds(start, chunk)] = (far if m & 1 else near)[m // 2].astype(F32)
    for k in range(uppers):
        value = upper_diagonal[k] + (sums[k] + sums[k].T)
        upper_out[k] = value
        halves[k, :block], halves[k, block:] = split(value)
    for m in range(lowers):
        forms = sums[uppers + m]
        value = jnp.dot(halves[parents[m]], panel[m], preferred_element_type=F32)
        cross = forms - (value[:block] + value[block:])
        cross_out[m] = cross
        right = jnp.concatenate([forms.astype(jnp.bfloat16), *split(cross)], axis=1)
        value = jnp.dot(panel_turned[m], right, preferred_element_type=F32)
        back = value[:, :block].T + value[:, block : 2 * block] + value[:, 2 * block :]
        square = sums[uppers + lowers + m]
        lower_out[m] = lower_diagonal[m] + (square + square.T) - back


def gather_shifts(value, axis):
    size = lax.axis_size(axis)
    return [value] + [shift(value, axis, -o) for o in range(1, size)]


def gather_pairs(value, axis):
    size = lax.axis_size(axis)
    pieces = [value]
    for o in range(1, size // 2 + 1):
        takers = range(size)
        if 2 * o == size:
            takers = [c if c % 2 == 0 else c + o for c in range(o)]
        pieces.append(lax.ppermute(value, axis, [((c + o) % size, c) for c in takers]))
    return pieces


def gather_near(value, axis):
    masks = range(2, lax.axis_size(axis), 2)
    return jnp.stack([value] + [flip(value, axis, m) for m in masks])


def scatter_flips(value, axis):
    masks = range(2, lax.axis_size(axis), 2)
    return [flip(value[m // 2].astype(WIRE), axis, m) for m in masks]


def tie(*values):
    return lax.optimization_barrier(values)


def per_device(
    top_inverse,
    upper_panel,
    upper_pattern,
    upper_diagonal,
    lower_panel,
    lower_pattern,
    parents,
    parent_panel,
    lower_diagonal,
):
    uppers, block = upper_panel.shape[0], upper_panel.shape[-1]
    lowers = lower_panel.shape[0]
    total = uppers + lowers
    sums_n = total + lowers
    width, depth = lax.axis_size("row"), lax.axis_size("col")
    half, chunk = width // 2, block // width
    bf16 = jnp.bfloat16
    upper_pattern, lower_pattern = upper_pattern.reshape(-1), lower_pattern.reshape(-1)

    (masked,) = call(
        mask_kernel,
        "mask",
        (upper_pattern, lower_pattern),
        (upper_panel.reshape(-1, block, block), lower_panel.reshape(-1, block, block)),
        [shape_of((total, block, block), bf16)],
        limit=60 << 20,
    )
    near, *pieces = tie(gather_near(masked, "row"), *gather_pairs(masked, "col"))
    far = flip(near, "row", 1)
    top, panel_turned = call(
        top_kernel,
        "top",
        (),
        (top_inverse[0, :, :, 0], parent_panel),
        [shape_of((2, depth * block, half * block), bf16), shape_of(parent_panel.shape, bf16)],
    )
    reach = len(pieces) * block
    (turned,) = call(turn_kernel, "turn", (), pieces, [shape_of((total, block, reach), bf16)])
    pairs = ceil_to(total, 2) // 2
    (start,) = call(
        first_kernel, "first", (), (top, near), [shape_of((pairs, depth * block, 2 * block), F32)]
    )
    own, *rest = call(
        functools.partial(second_kernel, uppers),
        "second",
        (parents,),
        (top, far, start, turned),
        [shape_of((total, block, block), F32)]
        + [shape_of((total, block, block), WIRE)] * (depth - 1)
        + [shape_of((half, sums_n, chunk, block), F32)] * 2,
        [shape_of((total, reach, 2 * block), bf16), shape_of((sums_n, block, block), F32)],
    )
    returns, (sums_keep, sums_away) = rest[:-2], rest[-2:]

    other, *returns = tie(flip(sums_away, "row", 1), *returns)
    sums = sums_keep + other
    middle = depth // 2
    part = sums[0]
    for piece in scatter_flips(sums, "row"):
        part = part + piece.astype(F32)
    parts = gather_shifts(part.astype(WIRE), "col")
    got = [shift(returns[o - 1], "col", o) for o in range(1, depth) if o == middle]
    tied = tie(*parts, *got)
    parts, got = tied[:depth], tied[depth:]
    (part,) = call(
        line_kernel,
        "line",
        (),
        parts,
        [shape_of((sums_n, chunk, block), WIRE)],
        [shape_of((depth, sums_n, chunk, block), F32)],
    )
    near = gather_near(part, "row")
    near, *more = tie(near, *[shift(returns[o - 1], "col", o) for o in range(1, middle)])
    part, *returns = tie(part, *returns)
    got = [*got, *more, *[shift(returns[o - 1], "col", o) for o in range(middle + 1, depth)]]
    far = flip(near, "row", 1)

    upper_columns, lower_columns = call(
        columns_kernel,
        "columns",
        (parents, upper_pattern, lower_pattern),
        (parent_panel, own, *got),
        [
            shape_of((uppers, block, block), bf16),
            shape_of((lowers, block, block), bf16),
        ],
    )
    upper_blocks, lower_cross, lower_blocks = call(
        functools.partial(blocks_kernel, width),
        "blocks",
        (parents,),
        (near, far, upper_diagonal, lower_diagonal, parent_panel, panel_turned),
        [
            shape_of((uppers, block, block), F32),
            shape_of((lowers, block, block), F32),
            shape_of((lowers, block, block), F32),
        ],
        [shape_of((sums_n, block, block), F32), shape_of((uppers, 2 * block, block), bf16)],
    )
    return (
        upper_columns[:, None, None],
        upper_blocks,
        lower_columns[:, None, None],
        lower_cross,
        lower_blocks,
    )


def solution(mesh):
    return jax.shard_map(
        per_device,
        mesh=mesh,
        in_specs=(
            P("row", None, None, "col", None, None),
            P(None, "row", "col", None, None),
            P(None, "row", "col"),
            P(),
            P(None, "row", "col", None, None),
            P(None, "row", "col"),
            P(),
            P(),
            P(),
        ),
        out_specs=(
            P(None, "row", "col", None, None),
            P(),
            P(None, "row", "col", None, None),
            P(),
            P(),
        ),
        check_vma=False,
    )
```

```python
import functools

import jax
import jax.numpy as jnp
import numpy as np
from jax import lax
from jax.experimental import pallas as pl
from jax.experimental.pallas import tpu as pltpu
from jax.sharding import PartitionSpec as P

F32 = jnp.float32
WIRE = jnp.bfloat16
VMEM = pl.BlockSpec(memory_space=pltpu.VMEM)
SMEM = pl.BlockSpec(memory_space=pltpu.SMEM)


def shape_of(dims, kind):
    return jax.ShapeDtypeStruct(dims, kind)


def flip(value, axis, mask):
    size = lax.axis_size(axis)
    return lax.ppermute(value, axis, [(i, i ^ mask) for i in range(size)])


def shift(value, axis, step):
    size = lax.axis_size(axis)
    return lax.ppermute(value, axis, [(i, (i + step) % size) for i in range(size)])


def ceil_to(value, step):
    return -(-value // step) * step


def params(refs, limit):
    size = sum(int(np.prod(r.shape)) * np.dtype(r.dtype).itemsize for r in refs)
    return pltpu.CompilerParams(vmem_limit_bytes=limit or ceil_to(size * 5 // 4, 1 << 20) + (4 << 20))


def call(kernel, name, scalars, arrays, outs, scratch=(), limit=0, cost=0):
    return pl.pallas_call(
        kernel,
        out_shape=outs,
        in_specs=[SMEM] * len(scalars) + [VMEM] * len(arrays),
        out_specs=[VMEM] * len(outs),
        scratch_shapes=[pltpu.VMEM(r.shape, r.dtype) for r in scratch],
        compiler_params=params([*arrays, *outs, *scratch], limit),
        cost_estimate=pl.CostEstimate(flops=cost, bytes_accessed=cost, transcendentals=0) if cost else None,
        name=name,
    )(*scalars, *arrays)


def stack_kernel(*refs):
    for i, piece in enumerate(refs[:-2]):
        refs[-1][i] = piece[...]


def mask_kernel(*refs):
    sources, masked, stages, sems = refs[:4], refs[4], refs[5:9], refs[9]
    copies = [
        pltpu.make_async_copy(source, stage, sems.at[i])
        for i, (source, stage) in enumerate(zip(sources, stages))
    ]
    for copy in copies:
        copy.start()
    for copy in copies:
        copy.wait()
    upper_pattern, lower_pattern, upper_panel, lower_panel = stages
    uppers, lowers = upper_panel.shape[0], lower_panel.shape[0]
    for k in range(uppers):
        masked[k] = upper_panel[k] * upper_pattern[k].astype(F32).astype(jnp.bfloat16)
    for m in range(lowers):
        masked[uppers + m] = lower_panel[m] * lower_pattern[m].astype(F32).astype(jnp.bfloat16)


def mask(*arrays):
    total, block = arrays[2].shape[0] + arrays[3].shape[0], arrays[2].shape[-1]
    return pl.pallas_call(
        mask_kernel,
        out_shape=shape_of((total, block, block), jnp.bfloat16),
        in_specs=[pl.BlockSpec(memory_space=pltpu.HBM)] * 4,
        out_specs=VMEM,
        scratch_shapes=[
            *[pltpu.SMEM(a.shape, a.dtype) for a in arrays[:2]],
            *[pltpu.VMEM(a.shape, a.dtype) for a in arrays[2:]],
            pltpu.SemaphoreType.DMA((4,)),
        ],
        compiler_params=params(arrays, 0),
        name="mask",
    )(*arrays)


def turn_kernel(*refs):
    pieces, turned = refs[:-1], refs[-1]
    total, block = pieces[0].shape[0], pieces[0].shape[-1]
    for k in range(total):
        for o, piece in enumerate(pieces):
            turned[k, :, o * block : (o + 1) * block] = piece[k].T


def top_kernel(top, panel, out, panel_turned):
    depth, width, block, _ = top.shape
    row, col = lax.axis_index("row"), lax.axis_index("col")
    half = width // 2

    def step(o, carry):
        start = pl.multiple_of(o * block, block)
        for i in range(width):
            m = 2 * (i % half) + i // half
            tile = top[lax.rem(col + o, depth), row ^ m]
            out[i // half, pl.ds(start, block), (i % half) * block : (i % half + 1) * block] = tile
        return carry

    lax.fori_loop(0, depth, step, 0)
    for m in range(panel.shape[0]):
        panel_turned[m] = panel[m].T


def dot_pair(left, pieces, first, second):
    right = [
        jnp.concatenate([pieces[i, first], pieces[i, second]], axis=1)
        for i in range(pieces.shape[0])
    ]
    return jnp.dot(left, jnp.concatenate(right), preferred_element_type=F32)


def first_kernel(top, near, out):
    total = near.shape[1]
    for first in range(0, total, 2):
        out[first // 2] = dot_pair(top[0], near, first, min(first + 1, total - 1))


def second_kernel(uppers, parents, top, far, start, turned, *refs):
    own, returns, (sums_keep, sums_away, both, forms) = refs[0], refs[1:-4], refs[-4:]
    total, block, reach = turned.shape
    lowers = total - uppers
    half, _, chunk, _ = sums_keep.shape
    row = lax.axis_index("row")

    for first in range(0, total, 2):
        second = min(first + 1, total - 1)
        value = start[first // 2] + dot_pair(top[1], far, first, second)
        for lane, k in enumerate(range(first, second + 1)):
            part = value[:, lane * block : (lane + 1) * block]
            own[k] = part[:block]
            for o, out in enumerate(returns):
                out[k] = part[(o + 1) * block : (o + 2) * block].astype(WIRE)
            part = jnp.concatenate([0.5 * part[:block], part[block:reach]])
            high = part.astype(jnp.bfloat16)
            both[k, :, :block] = high
            both[k, :, block:] = (part - high.astype(F32)).astype(jnp.bfloat16)

    def fold(rows, k):
        value = jnp.dot(rows, both[k], preferred_element_type=F32)
        return value[:, :block] + value[:, block:]

    def spread(slot, index):
        for m in range(2 * half):
            place = pl.multiple_of((row ^ m) * chunk, chunk)
            (sums_away if m & 1 else sums_keep)[m // 2, index] = forms[slot, pl.ds(place, chunk)]

    for k in range(uppers):
        forms[k] = fold(turned[k], k)
        spread(k, k)
    for m in range(lowers):
        own_row, parent = turned[uppers + m], parents[m]
        value = fold(jnp.concatenate([own_row, turned[parent]], axis=0), uppers + m)
        slot = uppers + 2 * m
        forms[slot] = value[:block]
        forms[slot + 1] = value[block:] + fold(own_row, parent).T
        spread(slot, total + m)
        spread(slot + 1, uppers + m)


def line_kernel(*refs):
    parts, (total_out, order) = refs[:-2], refs[-2:]
    depth, col = len(parts), lax.axis_index("col")
    for o in range(depth):
        order[lax.rem(col + o, depth)] = parts[o][...].astype(F32)
    total = order[0]
    for c in range(1, depth):
        total = total + order[c]
    total_out[...] = total.astype(total_out.dtype)


def columns_kernel(parents, upper_pattern, lower_pattern, panel, own, *refs):
    got, (upper_out, lower_out) = refs[:-2], refs[-2:]
    uppers, lowers = upper_out.shape[0], lower_out.shape[0]

    def product(k):
        value = own[k]
        for piece in got:
            value = value + piece[k].astype(F32)
        return value

    for k in range(uppers):
        upper_out[k] = (-product(k) * upper_pattern[k].astype(F32)).astype(jnp.bfloat16)
    for m in range(lowers):
        extension = jnp.dot(upper_out[parents[m]], panel[m], preferred_element_type=F32)
        value = -(product(uppers + m) + extension) * lower_pattern[m].astype(F32)
        lower_out[m] = value.astype(jnp.bfloat16)


def split(wide):
    high = wide.astype(jnp.bfloat16)
    return high, (wide - high.astype(F32)).astype(jnp.bfloat16)


def blocks_kernel(
    width,
    parents,
    near,
    far,
    upper_diagonal,
    lower_diagonal,
    panel,
    panel_turned,
    upper_out,
    cross_out,
    lower_out,
    sums,
    halves,
):
    uppers, lowers = upper_out.shape[0], lower_out.shape[0]
    block = panel.shape[-1]
    chunk = block // width
    row = lax.axis_index("row")
    for m in range(width):
        start = pl.multiple_of((row ^ m) * chunk, chunk)
        sums[:, pl.ds(start, chunk)] = (far if m & 1 else near)[m // 2].astype(F32)
    for k in range(uppers):
        value = upper_diagonal[k] + (sums[k] + sums[k].T)
        upper_out[k] = value
        halves[k, :block], halves[k, block:] = split(value)
    for m in range(lowers):
        forms = sums[uppers + m]
        value = jnp.dot(halves[parents[m]], panel[m], preferred_element_type=F32)
        cross = forms - (value[:block] + value[block:])
        cross_out[m] = cross
        right = jnp.concatenate([forms.astype(jnp.bfloat16), *split(cross)], axis=1)
        value = jnp.dot(panel_turned[m], right, preferred_element_type=F32)
        back = value[:, :block].T + value[:, block : 2 * block] + value[:, 2 * block :]
        square = sums[uppers + lowers + m]
        lower_out[m] = lower_diagonal[m] + (square + square.T) - back


def gather_shifts(value, axis):
    size = lax.axis_size(axis)
    return [value] + [shift(value, axis, -o) for o in range(1, size)]


def gather_pairs(value, axis):
    size = lax.axis_size(axis)
    pieces = [value]
    for o in range(1, size // 2 + 1):
        takers = range(size)
        if 2 * o == size:
            takers = [c if c % 2 == 0 else c + o for c in range(o)]
        pieces.append(lax.ppermute(value, axis, [((c + o) % size, c) for c in takers]))
    return pieces


def gather_near(value, axis):
    masks = range(2, lax.axis_size(axis), 2)
    return [value] + [flip(value, axis, m) for m in masks]


def scatter_flips(value, axis):
    masks = range(2, lax.axis_size(axis), 2)
    return [flip(value[m // 2].astype(WIRE), axis, m) for m in masks]


def tie(*values):
    return lax.optimization_barrier(values)


def per_device(
    top_inverse,
    upper_panel,
    upper_pattern,
    upper_diagonal,
    lower_panel,
    lower_pattern,
    parents,
    parent_panel,
    lower_diagonal,
):
    uppers, block = upper_panel.shape[0], upper_panel.shape[-1]
    lowers = lower_panel.shape[0]
    total = uppers + lowers
    sums_n = total + lowers
    width, depth = lax.axis_size("row"), lax.axis_size("col")
    half, chunk = width // 2, block // width
    bf16 = jnp.bfloat16
    upper_pattern, lower_pattern = upper_pattern.reshape(-1), lower_pattern.reshape(-1)

    masked = mask(
        upper_pattern,
        lower_pattern,
        upper_panel.reshape(-1, block, block),
        lower_panel.reshape(-1, block, block),
    )
    reach = (depth // 2 + 1) * block
    (turned,) = call(
        turn_kernel,
        "turn",
        (),
        gather_pairs(masked, "col"),
        [shape_of((total, block, reach), bf16)],
        cost=0,
    )
    (near,) = call(
        stack_kernel,
        "stack",
        (),
        (*gather_near(masked, "row"), turned),
        [shape_of((half, total, block, block), bf16)],
    )
    far = flip(near, "row", 1)
    top, panel_turned = call(
        top_kernel,
        "top",
        (),
        (top_inverse[0, :, :, 0], parent_panel),
        [shape_of((2, depth * block, half * block), bf16), shape_of(parent_panel.shape, bf16)],
    )
    pairs = ceil_to(total, 2) // 2
    (start,) = call(
        first_kernel, "first", (), (top, near), [shape_of((pairs, depth * block, 2 * block), F32)]
    )
    own, *rest = call(
        functools.partial(second_kernel, uppers),
        "second",
        (parents,),
        (top, far, start, turned),
        [shape_of((total, block, block), F32)]
        + [shape_of((total, block, block), WIRE)] * (depth - 1)
        + [shape_of((half, sums_n, chunk, block), F32)] * 2,
        [shape_of((total, reach, 2 * block), bf16), shape_of((sums_n, block, block), F32)],
    )
    returns, (sums_keep, sums_away) = rest[:-2], rest[-2:]

    other, *returns = tie(flip(sums_away, "row", 1), *returns)
    sums = sums_keep + other
    part = sums[0]
    for piece in scatter_flips(sums, "row"):
        part = part + piece.astype(F32)
    parts = gather_shifts(part.astype(WIRE), "col")
    early = [o for o in range(1, depth) if min(o, depth - o) <= depth // 4]
    late = [o for o in range(1, depth) if o not in early]
    tied = tie(*parts, *[shift(returns[o - 1], "col", o) for o in early])
    parts, got = tied[:depth], tied[depth:]
    (part,) = call(
        line_kernel,
        "line",
        (),
        parts,
        [shape_of((sums_n, chunk, block), WIRE)],
        [shape_of((depth, sums_n, chunk, block), F32)],
    )
    part, *returns = tie(part, *returns)
    got = [*got, *[shift(returns[o - 1], "col", o) for o in late]]
    near = jnp.stack(gather_near(part, "row"))
    far = flip(near, "row", 1)

    upper_columns, lower_columns = call(
        columns_kernel,
        "columns",
        (parents, upper_pattern, lower_pattern),
        (parent_panel, own, *got),
        [
            shape_of((uppers, block, block), bf16),
            shape_of((lowers, block, block), bf16),
        ],
    )
    upper_blocks, lower_cross, lower_blocks = call(
        functools.partial(blocks_kernel, width),
        "blocks",
        (parents,),
        (near, far, upper_diagonal, lower_diagonal, parent_panel, panel_turned),
        [
            shape_of((uppers, block, block), F32),
            shape_of((lowers, block, block), F32),
            shape_of((lowers, block, block), F32),
        ],
        [shape_of((sums_n, block, block), F32), shape_of((uppers, 2 * block, block), bf16)],
    )
    return (
        upper_columns[:, None, None],
        upper_blocks,
        lower_columns[:, None, None],
        lower_cross,
        lower_blocks,
    )


def solution(mesh):
    return jax.shard_map(
        per_device,
        mesh=mesh,
        in_specs=(
            P("row", None, None, "col", None, None),
            P(None, "row", "col", None, None),
            P(None, "row", "col"),
            P(),
            P(None, "row", "col", None, None),
            P(None, "row", "col"),
            P(),
            P(),
            P(),
        ),
        out_specs=(
            P(None, "row", "col", None, None),
            P(),
            P(None, "row", "col", None, None),
            P(),
            P(),
        ),
        check_vma=False,
    )
```

```python
import functools

import jax
import jax.numpy as jnp
import numpy as np
from jax import lax
from jax.experimental import pallas as pl
from jax.experimental.pallas import tpu as pltpu
from jax.sharding import PartitionSpec as P

F32 = jnp.float32
WIRE = jnp.bfloat16
VMEM = pl.BlockSpec(memory_space=pltpu.VMEM)
SMEM = pl.BlockSpec(memory_space=pltpu.SMEM)


def shape_of(dims, kind):
    return jax.ShapeDtypeStruct(dims, kind)


def flip(value, axis, mask):
    size = lax.axis_size(axis)
    return lax.ppermute(value, axis, [(i, i ^ mask) for i in range(size)])


def shift(value, axis, step):
    size = lax.axis_size(axis)
    return lax.ppermute(value, axis, [(i, (i + step) % size) for i in range(size)])


def ceil_to(value, step):
    return -(-value // step) * step


def params(refs, limit):
    size = sum(int(np.prod(r.shape)) * np.dtype(r.dtype).itemsize for r in refs)
    return pltpu.CompilerParams(vmem_limit_bytes=limit or ceil_to(size * 5 // 4, 1 << 20) + (4 << 20))


def call(kernel, name, scalars, arrays, outs, scratch=(), limit=0, cost=0):
    return pl.pallas_call(
        kernel,
        out_shape=outs,
        in_specs=[SMEM] * len(scalars) + [VMEM] * len(arrays),
        out_specs=[VMEM] * len(outs),
        scratch_shapes=[pltpu.VMEM(r.shape, r.dtype) for r in scratch],
        compiler_params=params([*arrays, *outs, *scratch], limit),
        cost_estimate=pl.CostEstimate(flops=cost, bytes_accessed=cost, transcendentals=0) if cost else None,
        name=name,
    )(*scalars, *arrays)


def stack_kernel(*refs):
    for i, piece in enumerate(refs[:-2]):
        refs[-1][i] = piece[...]


def mask_kernel(upper_pattern, lower_pattern, upper_panel, lower_panel, masked):
    uppers, lowers = upper_panel.shape[0], lower_panel.shape[0]
    for k in range(uppers):
        masked[k] = upper_panel[k] * upper_pattern[k].astype(F32).astype(jnp.bfloat16)
    for m in range(lowers):
        masked[uppers + m] = lower_panel[m] * lower_pattern[m].astype(F32).astype(jnp.bfloat16)


def turn_kernel(*refs):
    pieces, turned = refs[:-1], refs[-1]
    total, block = pieces[0].shape[0], pieces[0].shape[-1]
    for k in range(total):
        for o, piece in enumerate(pieces):
            turned[k, :, o * block : (o + 1) * block] = piece[k].T


def top_kernel(top, panel, out, out_turned, panel_turned):
    depth, width, block, _ = top.shape
    row, col = lax.axis_index("row"), lax.axis_index("col")
    half = width // 2

    def tile(o, i):
        return top[lax.rem(col + o, depth), row ^ (2 * (i % half) + i // half)]

    for o in range(out.shape[1] // block):
        rows = slice(o * block, (o + 1) * block)
        for i in range(width):
            out[i // half, rows, (i % half) * block : (i % half + 1) * block] = tile(o, i)

    for o in range(1, out.shape[1] // block):
        lanes = slice((o - 1) * block, o * block)
        for i in range(width):
            out_turned[i * block : (i + 1) * block, lanes] = tile(o, i).T
    for m in range(panel.shape[0]):
        panel_turned[m] = panel[m].T


def partial_kernel(top, *refs):
    pieces, (keep, away) = refs[:-2], refs[-2:]
    half, total, block, _ = keep.shape
    for first in range(0, total, 2):
        second = min(first + 1, total - 1)
        right = [jnp.concatenate([p[first], p[second]], axis=1) for p in pieces]
        value = jnp.dot(top[...], jnp.concatenate(right), preferred_element_type=F32)
        for lane, k in enumerate(range(first, second + 1)):
            for i in range(half):
                lanes = slice(lane * block, (lane + 1) * block)
                keep[i, k] = value[i * block : (i + 1) * block, lanes]
                far = value[(half + i) * block : (half + i + 1) * block, lanes]
                away[i, k] = far.astype(away.dtype)


def dot_pair(left, pieces, first, second):
    right = [
        jnp.concatenate([pieces[i, first], pieces[i, second]], axis=1)
        for i in range(pieces.shape[0])
    ]
    return jnp.dot(left, jnp.concatenate(right), preferred_element_type=F32)


def first_kernel(top, near, out):
    total = near.shape[1]
    for first in range(0, total, 2):
        out[first // 2] = dot_pair(top[0], near, first, min(first + 1, total - 1))


def second_kernel(uppers, parents, top, far, start, turned, *refs):
    own, returns, (sums_keep, sums_away, both, forms) = refs[0], refs[1:-4], refs[-4:]
    total, block, reach = turned.shape
    lowers = total - uppers
    half, _, chunk, _ = sums_keep.shape
    row = lax.axis_index("row")

    for first in range(0, total, 2):
        second = min(first + 1, total - 1)
        value = start[first // 2] + dot_pair(top[1], far, first, second)
        for lane, k in enumerate(range(first, second + 1)):
            part = value[:, lane * block : (lane + 1) * block]
            own[k] = part[:block]
            for o, out in enumerate(returns):
                out[k] = part[(o + 1) * block : (o + 2) * block].astype(WIRE)
            part = jnp.concatenate([0.5 * part[:block], part[block:reach]])
            high = part.astype(jnp.bfloat16)
            both[k, :, :block] = high
            both[k, :, block:] = (part - high.astype(F32)).astype(jnp.bfloat16)

    def fold(rows, k):
        value = jnp.dot(rows, both[k], preferred_element_type=F32)
        return value[:, :block] + value[:, block:]

    def spread(slot, index):
        for m in range(2 * half):
            place = pl.multiple_of((row ^ m) * chunk, chunk)
            (sums_away if m & 1 else sums_keep)[m // 2, index] = forms[slot, pl.ds(place, chunk)]

    for k in range(uppers):
        forms[k] = fold(turned[k], k)
        spread(k, k)
    for m in range(lowers):
        own_row, parent = turned[uppers + m], parents[m]
        value = fold(jnp.concatenate([own_row, turned[parent]], axis=0), uppers + m)
        slot = uppers + 2 * m
        forms[slot] = value[:block]
        forms[slot + 1] = value[block:] + fold(own_row, parent).T
        spread(slot, total + m)
        spread(slot + 1, uppers + m)


def line_kernel(*refs):
    parts, (total_out, order) = refs[:-2], refs[-2:]
    depth, col = len(parts), lax.axis_index("col")
    for o in range(depth):
        order[lax.rem(col + o, depth)] = parts[o][...].astype(F32)
    total = order[0]
    for c in range(1, depth):
        total = total + order[c]
    total_out[...] = total.astype(total_out.dtype)


def columns_kernel(parents, upper_pattern, lower_pattern, panel, own, front, back, *refs):
    got, (upper_out, lower_out) = refs[:-2], refs[-2:]
    uppers, lowers, middle = upper_out.shape[0], lower_out.shape[0], front.shape[0]

    def product(k):
        value = own[k] + (front[k] if k < middle else back[k - middle])
        for piece in got:
            value = value + piece[k].astype(F32)
        return value

    for k in range(uppers):
        upper_out[k] = (-product(k) * upper_pattern[k].astype(F32)).astype(jnp.bfloat16)
    for m in range(lowers):
        extension = jnp.dot(upper_out[parents[m]], panel[m], preferred_element_type=F32)
        value = -(product(uppers + m) + extension) * lower_pattern[m].astype(F32)
        lower_out[m] = value.astype(jnp.bfloat16)


def split(wide):
    high = wide.astype(jnp.bfloat16)
    return high, (wide - high.astype(F32)).astype(jnp.bfloat16)


def blocks_kernel(
    width,
    parents,
    near,
    far,
    upper_diagonal,
    lower_diagonal,
    panel,
    panel_turned,
    upper_out,
    cross_out,
    lower_out,
    sums,
    halves,
):
    uppers, lowers = upper_out.shape[0], lower_out.shape[0]
    block = panel.shape[-1]
    chunk = block // width
    row = lax.axis_index("row")
    for m in range(width):
        start = pl.multiple_of((row ^ m) * chunk, chunk)
        sums[:, pl.ds(start, chunk)] = (far if m & 1 else near)[m // 2].astype(F32)
    for k in range(uppers):
        value = upper_diagonal[k] + (sums[k] + sums[k].T)
        upper_out[k] = value
        halves[k, :block], halves[k, block:] = split(value)
    for m in range(lowers):
        forms = sums[uppers + m]
        value = jnp.dot(halves[parents[m]], panel[m], preferred_element_type=F32)
        cross = forms - (value[:block] + value[block:])
        cross_out[m] = cross
        right = jnp.concatenate([forms.astype(jnp.bfloat16), *split(cross)], axis=1)
        value = jnp.dot(panel_turned[m], right, preferred_element_type=F32)
        back = value[:, :block].T + value[:, block : 2 * block] + value[:, 2 * block :]
        square = sums[uppers + lowers + m]
        lower_out[m] = lower_diagonal[m] + (square + square.T) - back


def gather_shifts(value, axis):
    size = lax.axis_size(axis)
    return [value] + [shift(value, axis, -o) for o in range(1, size)]


def pairs(size, offset):
    takers = range(size)
    if 2 * offset == size:
        takers = [c if c % 2 == 0 else c + offset for c in range(offset)]
    return [(c, (c + offset) % size) for c in takers]


def gather_pair(value, axis, offset):
    return lax.ppermute(value, axis, [(b, c) for c, b in pairs(lax.axis_size(axis), offset)])


def return_pair(value, axis, offset):
    return lax.ppermute(value, axis, pairs(lax.axis_size(axis), offset))


def halve(value, axis, bit, left):
    place = sorted(left, reverse=True).index(bit)
    value = value.reshape((2,) * len(left) + value.shape[-3:])
    away = lax.index_in_dim(value, 1, place, keepdims=False).astype(WIRE)
    keep = lax.index_in_dim(value, 0, place, keepdims=False)
    return keep, flip(away, axis, 1 << bit)


def gather_doubles(value, axis):
    value = value[None]
    for bit in range(1, lax.axis_size(axis).bit_length() - 1):
        value = jnp.concatenate([value, flip(value, axis, 1 << bit)])
    return value


def gather_near(value, axis):
    masks = range(2, lax.axis_size(axis), 2)
    return [value] + [flip(value, axis, m) for m in masks]


def scatter_flips(value, axis):
    masks = range(2, lax.axis_size(axis), 2)
    return [flip(value[m // 2].astype(WIRE), axis, m) for m in masks]


def tie(*values):
    return lax.optimization_barrier(values)


def per_device(
    top_inverse,
    upper_panel,
    upper_pattern,
    upper_diagonal,
    lower_panel,
    lower_pattern,
    parents,
    parent_panel,
    lower_diagonal,
):
    uppers, block = upper_panel.shape[0], upper_panel.shape[-1]
    lowers = lower_panel.shape[0]
    total = uppers + lowers
    sums_n = total + lowers
    width, depth = lax.axis_size("row"), lax.axis_size("col")
    half, chunk = width // 2, block // width
    bf16 = jnp.bfloat16
    upper_pattern, lower_pattern = upper_pattern.reshape(-1), lower_pattern.reshape(-1)

    (masked,) = call(
        mask_kernel,
        "mask",
        (upper_pattern, lower_pattern),
        (upper_panel.reshape(-1, block, block), lower_panel.reshape(-1, block, block)),
        [shape_of((total, block, block), bf16)],
        limit=60 << 20,
    )
    reach = depth // 2
    pieces = [gather_pair(masked, "col", o) for o in range(1, reach + 1)]
    (turned,) = call(
        turn_kernel,
        "turn",
        (),
        (masked, *pieces),
        [shape_of((total, block, (reach + 1) * block), bf16)],
    )
    (near,) = call(
        stack_kernel,
        "stack",
        (),
        (*gather_near(masked, "row"), turned),
        [shape_of((half, total, block, block), bf16)],
    )
    far = flip(near, "row", 1)
    top, top_turned, panel_turned = call(
        top_kernel,
        "top",
        (),
        (top_inverse[0, :, :, 0], parent_panel),
        [
            shape_of((2, (reach + 1) * block, half * block), bf16),
            shape_of((width * block, reach * block), bf16),
            shape_of(parent_panel.shape, bf16),
        ],
    )
    keep, away = call(
        partial_kernel,
        "partial",
        (),
        (top_turned, *pieces),
        [
            shape_of((half, total, block, block), F32),
            shape_of((half, total, block, block), WIRE),
        ],
    )
    columns_n = ceil_to(total, 2) // 2
    (start,) = call(
        first_kernel,
        "first",
        (),
        (top, near),
        [shape_of((columns_n, (reach + 1) * block, 2 * block), F32)],
    )
    own, *rest = call(
        functools.partial(second_kernel, uppers),
        "second",
        (parents,),
        (top, far, start, turned),
        [shape_of((total, block, block), F32)]
        + [shape_of((total, block, block), WIRE)] * reach
        + [shape_of((half, sums_n, chunk, block), F32)] * 2,
        [
            shape_of((total, (reach + 1) * block, 2 * block), bf16),
            shape_of((sums_n, block, block), F32),
        ],
    )
    returns, (sums_keep, sums_away) = rest[:-2], rest[-2:]

    other, across, *returns = tie(
        flip(sums_away, "row", 1), flip(away, "row", 1), *returns
    )
    sums = sums_keep + other
    part = sums[0]
    for piece in scatter_flips(sums, "row"):
        part = part + piece.astype(F32)
    early = [return_pair(returns[o - 1], "col", o) for o in range(1, reach)]
    part, keep, *early = tie(part, keep, *early)
    value = keep + across.astype(F32)
    middle = total // 2
    bits = list(range(1, width.bit_length() - 1))
    lefts, sides = [bits, bits], [value[:, :middle], value[:, middle:]]
    halves = [
        halve(side, "row", bit, left) for side, bit, left in zip(sides, (bits[0], bits[-1]), lefts)
    ]
    parts = gather_shifts(part.astype(WIRE), "col")
    tied = tie(*parts, *[got for _, got in halves])
    (part,) = call(
        line_kernel,
        "line",
        (),
        tied[:depth],
        [shape_of((sums_n, chunk, block), WIRE)],
        [shape_of((depth, sums_n, chunk, block), F32)],
    )
    sides = [keep + got.astype(F32) for (keep, _), got in zip(halves, tied[depth:])]
    part, last, *sides = tie(part, returns[-1], *sides)
    near = gather_doubles(part, "row")
    far = flip(near, "row", 1)
    got = [*early, return_pair(last, "col", reach)]
    front, back = sides
    for i in range(1, len(bits)):
        keep, across = halve(front, "row", bits[i], bits[i:])
        front = keep + across.astype(F32)
        keep, across = halve(back, "row", bits[-1 - i], bits[: len(bits) - i])
        back = keep + across.astype(F32)
    front, back = [side.reshape(-1, block, block) for side in (front, back)]

    upper_columns, lower_columns = call(
        columns_kernel,
        "columns",
        (parents, upper_pattern, lower_pattern),
        (parent_panel, own, front, back, *got),
        [
            shape_of((uppers, block, block), bf16),
            shape_of((lowers, block, block), bf16),
        ],
    )
    upper_blocks, lower_cross, lower_blocks = call(
        functools.partial(blocks_kernel, width),
        "blocks",
        (parents,),
        (near, far, upper_diagonal, lower_diagonal, parent_panel, panel_turned),
        [
            shape_of((uppers, block, block), F32),
            shape_of((lowers, block, block), F32),
            shape_of((lowers, block, block), F32),
        ],
        [shape_of((sums_n, block, block), F32), shape_of((uppers, 2 * block, block), bf16)],
    )
    return (
        upper_columns[:, None, None],
        upper_blocks,
        lower_columns[:, None, None],
        lower_cross,
        lower_blocks,
    )


def solution(mesh):
    return jax.shard_map(
        per_device,
        mesh=mesh,
        in_specs=(
            P("row", None, None, "col", None, None),
            P(None, "row", "col", None, None),
            P(None, "row", "col"),
            P(),
            P(None, "row", "col", None, None),
            P(None, "row", "col"),
            P(),
            P(),
            P(),
        ),
        out_specs=(
            P(None, "row", "col", None, None),
            P(),
            P(None, "row", "col", None, None),
            P(),
            P(),
        ),
        check_vma=False,
    )
```

```python
import functools

import jax
import jax.numpy as jnp
import numpy as np
from jax import lax
from jax.experimental import pallas as pl
from jax.experimental.pallas import tpu as pltpu
from jax.sharding import PartitionSpec as P

F32 = jnp.float32
WIRE = jnp.bfloat16
VMEM = pl.BlockSpec(memory_space=pltpu.VMEM)
SMEM = pl.BlockSpec(memory_space=pltpu.SMEM)


def shape_of(dims, kind):
    return jax.ShapeDtypeStruct(dims, kind)


def flip(value, axis, mask):
    size = lax.axis_size(axis)
    return lax.ppermute(value, axis, [(i, i ^ mask) for i in range(size)])


def shift(value, axis, step):
    size = lax.axis_size(axis)
    return lax.ppermute(value, axis, [(i, (i + step) % size) for i in range(size)])


def ceil_to(value, step):
    return -(-value // step) * step


def params(refs, limit):
    size = sum(int(np.prod(r.shape)) * np.dtype(r.dtype).itemsize for r in refs)
    return pltpu.CompilerParams(vmem_limit_bytes=limit or ceil_to(size * 5 // 4, 1 << 20) + (4 << 20))


def call(kernel, name, scalars, arrays, outs, scratch=(), limit=0, cost=0):
    return pl.pallas_call(
        kernel,
        out_shape=outs,
        in_specs=[SMEM] * len(scalars) + [VMEM] * len(arrays),
        out_specs=[VMEM] * len(outs),
        scratch_shapes=[pltpu.VMEM(r.shape, r.dtype) for r in scratch],
        compiler_params=params([*arrays, *outs, *scratch], limit),
        cost_estimate=pl.CostEstimate(flops=cost, bytes_accessed=cost, transcendentals=0) if cost else None,
        name=name,
    )(*scalars, *arrays)


def stack_kernel(*refs):
    for i, piece in enumerate(refs[:-2]):
        refs[-1][i] = piece[...]


def mask_kernel(upper_pattern, lower_pattern, upper_panel, lower_panel, masked):
    uppers, lowers = upper_panel.shape[0], lower_panel.shape[0]
    for k in range(uppers):
        masked[k] = upper_panel[k] * upper_pattern[k].astype(F32).astype(jnp.bfloat16)
    for m in range(lowers):
        masked[uppers + m] = lower_panel[m] * lower_pattern[m].astype(F32).astype(jnp.bfloat16)


def turn_kernel(*refs):
    pieces, turned = refs[:-1], refs[-1]
    total, block = pieces[0].shape[0], pieces[0].shape[-1]
    for k in range(total):
        for o, piece in enumerate(pieces):
            turned[k, :, o * block : (o + 1) * block] = piece[k].T


def top_kernel(top, panel, out, out_turned, panel_turned):
    depth, width, block, _ = top.shape
    row, col = lax.axis_index("row"), lax.axis_index("col")
    half = width // 2

    def tile(o, i):
        return top[lax.rem(col + o, depth), row ^ (2 * (i % half) + i // half)]

    for o in range(out.shape[1] // block):
        rows = slice(o * block, (o + 1) * block)
        for i in range(width):
            out[i // half, rows, (i % half) * block : (i % half + 1) * block] = tile(o, i)

    for o in range(1, out.shape[1] // block):
        lanes = slice((o - 1) * block, o * block)
        for i in range(width):
            out_turned[i * block : (i + 1) * block, lanes] = tile(o, i).T
    for m in range(panel.shape[0]):
        panel_turned[m] = panel[m].T


def partial_kernel(top, *refs):
    pieces, (keep, away) = refs[:-2], refs[-2:]
    half, total, block, _ = keep.shape
    for first in range(0, total, 2):
        second = min(first + 1, total - 1)
        right = [jnp.concatenate([p[first], p[second]], axis=1) for p in pieces]
        value = jnp.dot(top[...], jnp.concatenate(right), preferred_element_type=F32)
        for lane, k in enumerate(range(first, second + 1)):
            for i in range(half):
                lanes = slice(lane * block, (lane + 1) * block)
                keep[i, k] = value[i * block : (i + 1) * block, lanes]
                far = value[(half + i) * block : (half + i + 1) * block, lanes]
                away[i, k] = far.astype(away.dtype)


def dot_pair(left, pieces, first, second):
    right = [
        jnp.concatenate([pieces[i, first], pieces[i, second]], axis=1)
        for i in range(pieces.shape[0])
    ]
    return jnp.dot(left, jnp.concatenate(right), preferred_element_type=F32)


def first_kernel(top, near, out):
    total = near.shape[1]
    for first in range(0, total, 2):
        out[first // 2] = dot_pair(top[0], near, first, min(first + 1, total - 1))


def second_kernel(uppers, parents, top, far, start, turned, *refs):
    own, returns, (sums_keep, sums_away, both, forms) = refs[0], refs[1:-4], refs[-4:]
    total, block, reach = turned.shape
    lowers = total - uppers
    half, _, chunk, _ = sums_keep.shape
    row = lax.axis_index("row")

    for first in range(0, total, 2):
        second = min(first + 1, total - 1)
        value = start[first // 2] + dot_pair(top[1], far, first, second)
        for lane, k in enumerate(range(first, second + 1)):
            part = value[:, lane * block : (lane + 1) * block]
            own[k] = part[:block]
            for o, out in enumerate(returns):
                out[k] = part[(o + 1) * block : (o + 2) * block].astype(WIRE)
            part = jnp.concatenate([0.5 * part[:block], part[block:reach]])
            high = part.astype(jnp.bfloat16)
            both[k, :, :block] = high
            both[k, :, block:] = (part - high.astype(F32)).astype(jnp.bfloat16)

    def fold(rows, k):
        value = jnp.dot(rows, both[k], preferred_element_type=F32)
        return value[:, :block] + value[:, block:]

    def spread(slot, index):
        for m in range(2 * half):
            place = pl.multiple_of((row ^ m) * chunk, chunk)
            (sums_away if m & 1 else sums_keep)[m // 2, index] = forms[slot, pl.ds(place, chunk)]

    for k in range(uppers):
        forms[k] = fold(turned[k], k)
        spread(k, k)
    for m in range(lowers):
        own_row, parent = turned[uppers + m], parents[m]
        value = fold(jnp.concatenate([own_row, turned[parent]], axis=0), uppers + m)
        slot = uppers + 2 * m
        forms[slot] = value[:block]
        forms[slot + 1] = value[block:] + fold(own_row, parent).T
        spread(slot, total + m)
        spread(slot + 1, uppers + m)


def line_kernel(*refs):
    parts, (total_out, order) = refs[:-2], refs[-2:]
    depth, col = len(parts), lax.axis_index("col")
    for o in range(depth):
        order[lax.rem(col + o, depth)] = parts[o][...].astype(F32)
    total = order[0]
    for c in range(1, depth):
        total = total + order[c]
    total_out[...] = total.astype(total_out.dtype)


def columns_kernel(parents, upper_pattern, lower_pattern, panel, own, front, back, *refs):
    got, (upper_out, lower_out) = refs[:-2], refs[-2:]
    uppers, lowers, middle = upper_out.shape[0], lower_out.shape[0], front.shape[0]

    def product(k):
        value = own[k] + (front[k] if k < middle else back[k - middle])
        for piece in got:
            value = value + piece[k].astype(F32)
        return value

    for k in range(uppers):
        upper_out[k] = (-product(k) * upper_pattern[k].astype(F32)).astype(jnp.bfloat16)
    extensions = [
        jnp.dot(upper_out[parents[m]], panel[m], preferred_element_type=F32) for m in range(lowers)
    ]
    for m in range(lowers):
        value = -(product(uppers + m) + extensions[m]) * lower_pattern[m].astype(F32)
        lower_out[m] = value.astype(jnp.bfloat16)


def split(wide):
    high = wide.astype(jnp.bfloat16)
    return high, (wide - high.astype(F32)).astype(jnp.bfloat16)


def blocks_kernel(
    width,
    parents,
    near,
    far,
    upper_diagonal,
    lower_diagonal,
    panel,
    panel_turned,
    upper_out,
    cross_out,
    lower_out,
    sums,
    halves,
):
    uppers, lowers = upper_out.shape[0], lower_out.shape[0]
    block = panel.shape[-1]
    chunk = block // width
    row = lax.axis_index("row")
    for m in range(width):
        start = pl.multiple_of((row ^ m) * chunk, chunk)
        sums[:, pl.ds(start, chunk)] = (far if m & 1 else near)[m // 2].astype(F32)
    for k in range(uppers):
        value = upper_diagonal[k] + (sums[k] + sums[k].T)
        upper_out[k] = value
        halves[k, :block], halves[k, block:] = split(value)
    products = [
        jnp.dot(halves[parents[m]], panel[m], preferred_element_type=F32) for m in range(lowers)
    ]
    rights = []
    for m in range(lowers):
        forms = sums[uppers + m]
        cross = forms - (products[m][:block] + products[m][block:])
        cross_out[m] = cross
        rights.append(jnp.concatenate([forms.astype(jnp.bfloat16), *split(cross)], axis=1))
    backs = [
        jnp.dot(panel_turned[m], rights[m], preferred_element_type=F32) for m in range(lowers)
    ]
    for m in range(lowers):
        value = backs[m]
        square = sums[uppers + lowers + m]
        turned = (square - value[:, :block]).T
        rest = value[:, block : 2 * block] + value[:, 2 * block :]
        lower_out[m] = lower_diagonal[m] + (square - rest) + turned


def gather_shifts(value, axis):
    size = lax.axis_size(axis)
    return [value] + [shift(value, axis, -o) for o in range(1, size)]


def pairs(size, offset):
    takers = range(size)
    if 2 * offset == size:
        takers = [c if c % 2 == 0 else c + offset for c in range(offset)]
    return [(c, (c + offset) % size) for c in takers]


def gather_pair(value, axis, offset):
    return lax.ppermute(value, axis, [(b, c) for c, b in pairs(lax.axis_size(axis), offset)])


def return_pair(value, axis, offset):
    return lax.ppermute(value, axis, pairs(lax.axis_size(axis), offset))


def halve(value, axis, bit, left):
    place = sorted(left, reverse=True).index(bit)
    value = value.reshape((2,) * len(left) + value.shape[-3:])
    away = lax.index_in_dim(value, 1, place, keepdims=False).astype(WIRE)
    keep = lax.index_in_dim(value, 0, place, keepdims=False)
    return keep, flip(away, axis, 1 << bit)


def gather_doubles(value, axis):
    value = value[None]
    for bit in range(1, lax.axis_size(axis).bit_length() - 1):
        value = jnp.concatenate([value, flip(value, axis, 1 << bit)])
    return value


def gather_near(value, axis):
    masks = range(2, lax.axis_size(axis), 2)
    return [value] + [flip(value, axis, m) for m in masks]


def scatter_flips(value, axis):
    masks = range(2, lax.axis_size(axis), 2)
    return [flip(value[m // 2].astype(WIRE), axis, m) for m in masks]


def tie(*values):
    return lax.optimization_barrier(values)


def per_device(
    top_inverse,
    upper_panel,
    upper_pattern,
    upper_diagonal,
    lower_panel,
    lower_pattern,
    parents,
    parent_panel,
    lower_diagonal,
):
    uppers, block = upper_panel.shape[0], upper_panel.shape[-1]
    lowers = lower_panel.shape[0]
    total = uppers + lowers
    sums_n = total + lowers
    width, depth = lax.axis_size("row"), lax.axis_size("col")
    half, chunk = width // 2, block // width
    bf16 = jnp.bfloat16
    upper_pattern, lower_pattern = upper_pattern.reshape(-1), lower_pattern.reshape(-1)

    (masked,) = call(
        mask_kernel,
        "mask",
        (upper_pattern, lower_pattern),
        (upper_panel.reshape(-1, block, block), lower_panel.reshape(-1, block, block)),
        [shape_of((total, block, block), bf16)],
        limit=60 << 20,
    )
    reach = depth // 2
    pieces = [gather_pair(masked, "col", o) for o in range(1, reach + 1)]
    (turned,) = call(
        turn_kernel,
        "turn",
        (),
        (masked, *pieces),
        [shape_of((total, block, (reach + 1) * block), bf16)],
    )
    (near,) = call(
        stack_kernel,
        "stack",
        (),
        (*gather_near(masked, "row"), turned),
        [shape_of((half, total, block, block), bf16)],
    )
    far = flip(near, "row", 1)
    top, top_turned, panel_turned = call(
        top_kernel,
        "top",
        (),
        (top_inverse[0, :, :, 0], parent_panel),
        [
            shape_of((2, (reach + 1) * block, half * block), bf16),
            shape_of((width * block, reach * block), bf16),
            shape_of(parent_panel.shape, bf16),
        ],
    )
    keep, away = call(
        partial_kernel,
        "partial",
        (),
        (top_turned, *pieces),
        [
            shape_of((half, total, block, block), F32),
            shape_of((half, total, block, block), WIRE),
        ],
    )
    columns_n = ceil_to(total, 2) // 2
    (start,) = call(
        first_kernel,
        "first",
        (),
        (top, near),
        [shape_of((columns_n, (reach + 1) * block, 2 * block), F32)],
    )
    own, *rest = call(
        functools.partial(second_kernel, uppers),
        "second",
        (parents,),
        (top, far, start, turned),
        [shape_of((total, block, block), F32)]
        + [shape_of((total, block, block), WIRE)] * reach
        + [shape_of((half, sums_n, chunk, block), F32)] * 2,
        [
            shape_of((total, (reach + 1) * block, 2 * block), bf16),
            shape_of((sums_n, block, block), F32),
        ],
    )
    returns, (sums_keep, sums_away) = rest[:-2], rest[-2:]

    other, across = tie(flip(sums_away, "row", 1), flip(away, "row", 1))
    sums = sums_keep + other
    pieces = scatter_flips(sums, "row")
    pieces[0], value = tie(pieces[0], keep + across.astype(F32))
    middle = total // 2
    bits = list(range(1, width.bit_length() - 1))
    sides = [value[:, :middle], value[:, middle:]]
    halves = [halve(side, "row", bit, bits) for side, bit in zip(sides, (bits[0], bits[-1]))]
    part = sums[0]
    for piece in pieces:
        part = part + piece.astype(F32)
    part = part.astype(WIRE)
    early = [return_pair(returns[o - 1], "col", o) for o in range(1, reach)]
    parts = gather_shifts(part, "col")
    tied = tie(*parts, *[got for _, got in halves], *early)
    early = tied[depth + 2 :]
    (part,) = call(
        line_kernel,
        "line",
        (),
        tied[:depth],
        [shape_of((sums_n, chunk, block), WIRE)],
        [shape_of((depth, sums_n, chunk, block), F32)],
    )
    sides = [keep + got.astype(F32) for (keep, _), got in zip(halves, tied[depth : depth + 2])]
    part, last, *sides = tie(part, returns[-1], *sides)
    near = gather_doubles(part, "row")
    far = flip(near, "row", 1)
    got = [*early, return_pair(last, "col", reach)]
    front, back = sides
    for i in range(1, len(bits)):
        keep, across = halve(front, "row", bits[i], bits[i:])
        front = keep + across.astype(F32)
        keep, across = halve(back, "row", bits[-1 - i], bits[: len(bits) - i])
        back = keep + across.astype(F32)
    front, back = [side.reshape(-1, block, block) for side in (front, back)]

    upper_blocks, lower_cross, lower_blocks = call(
        functools.partial(blocks_kernel, width),
        "blocks",
        (parents,),
        (near, far, upper_diagonal, lower_diagonal, parent_panel, panel_turned),
        [
            shape_of((uppers, block, block), F32),
            shape_of((lowers, block, block), F32),
            shape_of((lowers, block, block), F32),
        ],
        [shape_of((sums_n, block, block), F32), shape_of((uppers, 2 * block, block), bf16)],
    )
    upper_blocks, *got = tie(upper_blocks, *got)
    upper_columns, lower_columns = call(
        columns_kernel,
        "columns",
        (parents, upper_pattern, lower_pattern),
        (parent_panel, own, front, back, *got),
        [
            shape_of((uppers, block, block), bf16),
            shape_of((lowers, block, block), bf16),
        ],
    )
    return (
        upper_columns[:, None, None],
        upper_blocks,
        lower_columns[:, None, None],
        lower_cross,
        lower_blocks,
    )


def solution(mesh):
    return jax.shard_map(
        per_device,
        mesh=mesh,
        in_specs=(
            P("row", None, None, "col", None, None),
            P(None, "row", "col", None, None),
            P(None, "row", "col"),
            P(),
            P(None, "row", "col", None, None),
            P(None, "row", "col"),
            P(),
            P(),
            P(),
        ),
        out_specs=(
            P(None, "row", "col", None, None),
            P(),
            P(None, "row", "col", None, None),
            P(),
            P(),
        ),
        check_vma=False,
    )
```

```python
import functools

import jax
import jax.numpy as jnp
import numpy as np
from jax import lax
from jax.experimental import pallas as pl
from jax.experimental.pallas import tpu as pltpu
from jax.sharding import PartitionSpec as P

F32 = jnp.float32
WIRE = jnp.bfloat16
VMEM = pl.BlockSpec(memory_space=pltpu.VMEM)
SMEM = pl.BlockSpec(memory_space=pltpu.SMEM)


def shape_of(dims, kind):
    return jax.ShapeDtypeStruct(dims, kind)


def flip(value, axis, mask):
    size = lax.axis_size(axis)
    return lax.ppermute(value, axis, [(i, i ^ mask) for i in range(size)])


def shift(value, axis, step):
    size = lax.axis_size(axis)
    return lax.ppermute(value, axis, [(i, (i + step) % size) for i in range(size)])


def ceil_to(value, step):
    return -(-value // step) * step


def params(refs, limit):
    size = sum(int(np.prod(r.shape)) * np.dtype(r.dtype).itemsize for r in refs)
    return pltpu.CompilerParams(vmem_limit_bytes=limit or ceil_to(size * 5 // 4, 1 << 20) + (4 << 20))


def call(kernel, name, scalars, arrays, outs, scratch=(), limit=0, cost=0):
    return pl.pallas_call(
        kernel,
        out_shape=outs,
        in_specs=[SMEM] * len(scalars) + [VMEM] * len(arrays),
        out_specs=[VMEM] * len(outs),
        scratch_shapes=[pltpu.VMEM(r.shape, r.dtype) for r in scratch],
        compiler_params=params([*arrays, *outs, *scratch], limit),
        cost_estimate=pl.CostEstimate(flops=cost, bytes_accessed=cost, transcendentals=0) if cost else None,
        name=name,
    )(*scalars, *arrays)


def stack_kernel(*refs):
    for i, piece in enumerate(refs[:-2]):
        refs[-1][i] = piece[...]


def mask_kernel(upper_pattern, lower_pattern, upper_panel, lower_panel, masked):
    uppers, lowers = upper_panel.shape[0], lower_panel.shape[0]
    for k in range(uppers):
        masked[k] = upper_panel[k] * upper_pattern[k].astype(F32).astype(jnp.bfloat16)
    for m in range(lowers):
        masked[uppers + m] = lower_panel[m] * lower_pattern[m].astype(F32).astype(jnp.bfloat16)


def turn_kernel(*refs):
    pieces, turned = refs[:-1], refs[-1]
    total, block = pieces[0].shape[0], pieces[0].shape[-1]
    for k in range(total):
        for o, piece in enumerate(pieces):
            turned[k, :, o * block : (o + 1) * block] = piece[k].T


def top_kernel(top, panel, out, out_turned, panel_turned):
    depth, width, block, _ = top.shape
    row, col = lax.axis_index("row"), lax.axis_index("col")
    half = width // 2

    def tile(o, i):
        return top[lax.rem(col + o, depth), row ^ (2 * (i % half) + i // half)]

    for o in range(out.shape[1] // block):
        rows = slice(o * block, (o + 1) * block)
        for i in range(width):
            out[i // half, rows, (i % half) * block : (i % half + 1) * block] = tile(o, i)

    for o in range(1, out.shape[1] // block):
        lanes = slice((o - 1) * block, o * block)
        for i in range(width):
            out_turned[i * block : (i + 1) * block, lanes] = tile(o, i).T
    for m in range(panel.shape[0]):
        panel_turned[m] = panel[m].T


def partial_kernel(top, *refs):
    pieces, (keep, away) = refs[:-2], refs[-2:]
    half, total, block, _ = keep.shape
    for first in range(0, total, 2):
        second = min(first + 1, total - 1)
        right = [jnp.concatenate([p[first], p[second]], axis=1) for p in pieces]
        value = jnp.dot(top[...], jnp.concatenate(right), preferred_element_type=F32)
        for lane, k in enumerate(range(first, second + 1)):
            for i in range(half):
                lanes = slice(lane * block, (lane + 1) * block)
                keep[i, k] = value[i * block : (i + 1) * block, lanes]
                far = value[(half + i) * block : (half + i + 1) * block, lanes]
                away[i, k] = far.astype(away.dtype)


def dot_pair(left, pieces, first, second):
    right = [
        jnp.concatenate([pieces[i, first], pieces[i, second]], axis=1)
        for i in range(pieces.shape[0])
    ]
    return jnp.dot(left, jnp.concatenate(right), preferred_element_type=F32)


def first_kernel(top, near, out):
    total = near.shape[1]
    for first in range(0, total, 2):
        out[first // 2] = dot_pair(top[0], near, first, min(first + 1, total - 1))


def triangle(block):
    rows = lax.broadcasted_iota(jnp.int32, (block, block), 0)
    lanes = lax.broadcasted_iota(jnp.int32, (block, block), 1)
    return rows < lanes, rows == lanes


def pack(squares, packed, start):
    total, block = squares.shape[:2]
    above, diagonal = triangle(block)
    for p in range(total // 2):
        first, second = [squares[k] + squares[k].T for k in (2 * p, 2 * p + 1)]
        packed[p * block : (p + 1) * block] = jnp.where(above, first, second)
        row = jnp.sum(jnp.where(diagonal, first, 0.0), axis=0, keepdims=True)
        packed[start + p : start + p + 1] = row
    if total % 2:
        packed[(total // 2) * block : (total // 2 + 1) * block] = squares[total - 1] + squares[total - 1].T


def unpack(packed, total, block, start):
    above, diagonal = triangle(block)
    squares = []
    for p in range(total // 2):
        value = packed[p * block : (p + 1) * block]
        turned = value.T
        row = packed[start + p : start + p + 1]
        squares.append(jnp.where(above, value, jnp.where(diagonal, row, turned)))
        squares.append(jnp.where(above, turned, value))
    if total % 2:
        squares.append(packed[(total // 2) * block : (total // 2 + 1) * block])
    return squares


def second_kernel(uppers, parents, top, far, start, turned, *refs):
    own, returns, (sums_keep, sums_away, both, squares, packed) = refs[0], refs[1:-5], refs[-5:]
    total, block, reach = turned.shape
    lowers = total - uppers
    half, chunk, _ = sums_keep.shape
    row = lax.axis_index("row")

    for first in range(0, total, 2):
        second = min(first + 1, total - 1)
        value = start[first // 2] + dot_pair(top[1], far, first, second)
        for lane, k in enumerate(range(first, second + 1)):
            part = value[:, lane * block : (lane + 1) * block]
            own[k] = part[:block]
            for o, out in enumerate(returns):
                out[k] = part[(o + 1) * block : (o + 2) * block].astype(WIRE)
            part = jnp.concatenate([0.5 * part[:block], part[block:reach]])
            high = part.astype(jnp.bfloat16)
            both[k, :, :block] = high
            both[k, :, block:] = (part - high.astype(F32)).astype(jnp.bfloat16)

    def fold(rows, k):
        value = jnp.dot(rows, both[k], preferred_element_type=F32)
        return value[:, :block] + value[:, block:]

    base = (total + 1) // 2 * block
    for k in range(uppers):
        squares[k] = fold(turned[k], k)
    for m in range(lowers):
        own_row, parent = turned[uppers + m], parents[m]
        value = fold(jnp.concatenate([own_row, turned[parent]], axis=0), uppers + m)
        squares[uppers + m] = value[:block]
        place = base + m * block
        packed[place : place + block] = value[block:] + fold(own_row, parent).T
    end = base + lowers * block
    packed[end:] = jnp.zeros((packed.shape[0] - end, block), F32)
    pack(squares, packed, end)
    for m in range(2 * half):
        place = pl.multiple_of((row ^ m) * chunk, chunk)
        (sums_away if m & 1 else sums_keep)[m // 2] = packed[pl.ds(place, chunk)]


def line_kernel(*refs):
    parts, (total_out, order) = refs[:-2], refs[-2:]
    depth, col = len(parts), lax.axis_index("col")
    for o in range(depth):
        order[lax.rem(col + o, depth)] = parts[o][...].astype(F32)
    total = order[0]
    for c in range(1, depth):
        total = total + order[c]
    total_out[...] = total.astype(total_out.dtype)


def columns_kernel(parents, upper_pattern, lower_pattern, panel, own, front, back, *refs):
    got, (upper_out, lower_out) = refs[:-2], refs[-2:]
    uppers, lowers, middle = upper_out.shape[0], lower_out.shape[0], front.shape[0]

    def product(k):
        value = own[k] + (front[k] if k < middle else back[k - middle])
        for piece in got:
            value = value + piece[k].astype(F32)
        return value

    for k in range(uppers):
        upper_out[k] = (-product(k) * upper_pattern[k].astype(F32)).astype(jnp.bfloat16)
    extensions = [
        jnp.dot(upper_out[parents[m]], panel[m], preferred_element_type=F32) for m in range(lowers)
    ]
    for m in range(lowers):
        value = -(product(uppers + m) + extensions[m]) * lower_pattern[m].astype(F32)
        lower_out[m] = value.astype(jnp.bfloat16)


def split(wide):
    high = wide.astype(jnp.bfloat16)
    return high, (wide - high.astype(F32)).astype(jnp.bfloat16)


def blocks_kernel(
    width,
    parents,
    near,
    far,
    upper_diagonal,
    lower_diagonal,
    panel,
    panel_turned,
    upper_out,
    cross_out,
    lower_out,
    packed,
    halves,
):
    uppers, lowers = upper_out.shape[0], lower_out.shape[0]
    block = panel.shape[-1]
    chunk = near.shape[1]
    row = lax.axis_index("row")
    for m in range(width):
        place = pl.multiple_of((row ^ m) * chunk, chunk)
        packed[pl.ds(place, chunk)] = (far if m & 1 else near)[m // 2].astype(F32)
    base = (uppers + lowers + 1) // 2 * block
    squares = unpack(packed, uppers + lowers, block, base + lowers * block)
    for k in range(uppers):
        value = upper_diagonal[k] + squares[k]
        upper_out[k] = value
        halves[k, :block], halves[k, block:] = split(value)
    products = [
        jnp.dot(halves[parents[m]], panel[m], preferred_element_type=F32) for m in range(lowers)
    ]
    rights = []
    for m in range(lowers):
        forms = packed[base + m * block : base + (m + 1) * block]
        cross = forms - (products[m][:block] + products[m][block:])
        cross_out[m] = cross
        rights.append(jnp.concatenate([forms.astype(jnp.bfloat16), *split(cross)], axis=1))
    backs = [
        jnp.dot(panel_turned[m], rights[m], preferred_element_type=F32) for m in range(lowers)
    ]
    for m in range(lowers):
        value = backs[m]
        rest = value[:, block : 2 * block] + value[:, 2 * block :]
        lower_out[m] = lower_diagonal[m] + squares[uppers + m] - rest - value[:, :block].T


def gather_shifts(value, axis):
    size = lax.axis_size(axis)
    return [value] + [shift(value, axis, -o) for o in range(1, size)]


def pairs(size, offset):
    takers = range(size)
    if 2 * offset == size:
        takers = [c if c % 2 == 0 else c + offset for c in range(offset)]
    return [(c, (c + offset) % size) for c in takers]


def gather_pair(value, axis, offset):
    return lax.ppermute(value, axis, [(b, c) for c, b in pairs(lax.axis_size(axis), offset)])


def return_pair(value, axis, offset):
    return lax.ppermute(value, axis, pairs(lax.axis_size(axis), offset))


def halve(value, axis, bit, left):
    place = sorted(left, reverse=True).index(bit)
    value = value.reshape((2,) * len(left) + value.shape[-3:])
    away = lax.index_in_dim(value, 1, place, keepdims=False).astype(WIRE)
    keep = lax.index_in_dim(value, 0, place, keepdims=False)
    return keep, flip(away, axis, 1 << bit)


def gather_doubles(value, axis):
    value = value[None]
    for bit in range(1, lax.axis_size(axis).bit_length() - 1):
        value = jnp.concatenate([value, flip(value, axis, 1 << bit)])
    return value


def gather_near(value, axis):
    masks = range(2, lax.axis_size(axis), 2)
    return [value] + [flip(value, axis, m) for m in masks]


def scatter_flips(value, axis):
    masks = range(2, lax.axis_size(axis), 2)
    return [flip(value[m // 2].astype(WIRE), axis, m) for m in masks]


def tie(*values):
    return lax.optimization_barrier(values)


def per_device(
    top_inverse,
    upper_panel,
    upper_pattern,
    upper_diagonal,
    lower_panel,
    lower_pattern,
    parents,
    parent_panel,
    lower_diagonal,
):
    uppers, block = upper_panel.shape[0], upper_panel.shape[-1]
    lowers = lower_panel.shape[0]
    total = uppers + lowers
    width, depth = lax.axis_size("row"), lax.axis_size("col")
    half = width // 2
    packed_n = (total + 1) // 2 * block + lowers * block + total // 2
    chunk = ceil_to(packed_n, 16 * width) // width
    bf16 = jnp.bfloat16
    upper_pattern, lower_pattern = upper_pattern.reshape(-1), lower_pattern.reshape(-1)

    (masked,) = call(
        mask_kernel,
        "mask",
        (upper_pattern, lower_pattern),
        (upper_panel.reshape(-1, block, block), lower_panel.reshape(-1, block, block)),
        [shape_of((total, block, block), bf16)],
        limit=60 << 20,
    )
    reach = depth // 2
    pieces = [gather_pair(masked, "col", o) for o in range(1, reach + 1)]
    (turned,) = call(
        turn_kernel,
        "turn",
        (),
        (masked, *pieces),
        [shape_of((total, block, (reach + 1) * block), bf16)],
    )
    (near,) = call(
        stack_kernel,
        "stack",
        (),
        (*gather_near(masked, "row"), turned),
        [shape_of((half, total, block, block), bf16)],
    )
    far = flip(near, "row", 1)
    top, top_turned, panel_turned = call(
        top_kernel,
        "top",
        (),
        (top_inverse[0, :, :, 0], parent_panel),
        [
            shape_of((2, (reach + 1) * block, half * block), bf16),
            shape_of((width * block, reach * block), bf16),
            shape_of(parent_panel.shape, bf16),
        ],
    )
    keep, away = call(
        partial_kernel,
        "partial",
        (),
        (top_turned, *pieces),
        [
            shape_of((half, total, block, block), F32),
            shape_of((half, total, block, block), WIRE),
        ],
    )
    columns_n = ceil_to(total, 2) // 2
    (start,) = call(
        first_kernel,
        "first",
        (),
        (top, near),
        [shape_of((columns_n, (reach + 1) * block, 2 * block), F32)],
    )
    own, *rest = call(
        functools.partial(second_kernel, uppers),
        "second",
        (parents,),
        (top, far, start, turned),
        [shape_of((total, block, block), F32)]
        + [shape_of((total, block, block), WIRE)] * reach
        + [shape_of((half, chunk, block), F32)] * 2,
        [
            shape_of((total, (reach + 1) * block, 2 * block), bf16),
            shape_of((total, block, block), F32),
            shape_of((width * chunk, block), F32),
        ],
    )
    returns, (sums_keep, sums_away) = rest[:-2], rest[-2:]

    other, across = tie(flip(sums_away, "row", 1), flip(away, "row", 1))
    sums = sums_keep + other
    pieces = scatter_flips(sums, "row")
    pieces[0], value = tie(pieces[0], keep + across.astype(F32))
    middle = total // 2
    bits = list(range(1, width.bit_length() - 1))
    sides = [value[:, :middle], value[:, middle:]]
    halves = [halve(side, "row", bit, bits) for side, bit in zip(sides, (bits[0], bits[-1]))]
    part = sums[0]
    for piece in pieces:
        part = part + piece.astype(F32)
    part = part.astype(WIRE)
    early = [return_pair(returns[o - 1], "col", o) for o in range(1, reach)]
    parts = gather_shifts(part, "col")
    tied = tie(*parts, *[got for _, got in halves], *early)
    early = tied[depth + 2 :]
    (part,) = call(
        line_kernel,
        "line",
        (),
        tied[:depth],
        [shape_of((chunk, block), WIRE)],
        [shape_of((depth, chunk, block), F32)],
    )
    sides = [keep + got.astype(F32) for (keep, _), got in zip(halves, tied[depth : depth + 2])]
    part, last, *sides = tie(part, returns[-1], *sides)
    near = gather_doubles(part, "row")
    far, last = tie(flip(near, "row", 1), return_pair(last, "col", reach))
    got = [*early, last]
    front, back = sides
    for i in range(1, len(bits)):
        keep, across = halve(front, "row", bits[i], bits[i:])
        front = keep + across.astype(F32)
        keep, across = halve(back, "row", bits[-1 - i], bits[: len(bits) - i])
        back = keep + across.astype(F32)
    front, back = [side.reshape(-1, block, block) for side in (front, back)]

    upper_blocks, lower_cross, lower_blocks = call(
        functools.partial(blocks_kernel, width),
        "blocks",
        (parents,),
        (near, far, upper_diagonal, lower_diagonal, parent_panel, panel_turned),
        [
            shape_of((uppers, block, block), F32),
            shape_of((lowers, block, block), F32),
            shape_of((lowers, block, block), F32),
        ],
        [shape_of((width * chunk, block), F32), shape_of((uppers, 2 * block, block), bf16)],
    )
    upper_columns, lower_columns = call(
        columns_kernel,
        "columns",
        (parents, upper_pattern, lower_pattern),
        (parent_panel, own, front, back, *got),
        [
            shape_of((uppers, block, block), bf16),
            shape_of((lowers, block, block), bf16),
        ],
    )
    return (
        upper_columns[:, None, None],
        upper_blocks,
        lower_columns[:, None, None],
        lower_cross,
        lower_blocks,
    )


def solution(mesh):
    return jax.shard_map(
        per_device,
        mesh=mesh,
        in_specs=(
            P("row", None, None, "col", None, None),
            P(None, "row", "col", None, None),
            P(None, "row", "col"),
            P(),
            P(None, "row", "col", None, None),
            P(None, "row", "col"),
            P(),
            P(),
            P(),
        ),
        out_specs=(
            P(None, "row", "col", None, None),
            P(),
            P(None, "row", "col", None, None),
            P(),
            P(),
        ),
        check_vma=False,
    )
```

```python
import functools

import jax
import jax.numpy as jnp
import numpy as np
from jax import lax
from jax.experimental import pallas as pl
from jax.experimental.pallas import tpu as pltpu
from jax.sharding import PartitionSpec as P

F32 = jnp.float32
WIRE = jnp.bfloat16
VMEM = pl.BlockSpec(memory_space=pltpu.VMEM)
SMEM = pl.BlockSpec(memory_space=pltpu.SMEM)


def shape_of(dims, kind):
    return jax.ShapeDtypeStruct(dims, kind)


def flip(value, axis, mask):
    size = lax.axis_size(axis)
    return lax.ppermute(value, axis, [(i, i ^ mask) for i in range(size)])


def shift(value, axis, step):
    size = lax.axis_size(axis)
    return lax.ppermute(value, axis, [(i, (i + step) % size) for i in range(size)])


def ceil_to(value, step):
    return -(-value // step) * step


def params(refs, limit):
    size = sum(int(np.prod(r.shape)) * np.dtype(r.dtype).itemsize for r in refs)
    return pltpu.CompilerParams(vmem_limit_bytes=limit or ceil_to(size * 5 // 4, 1 << 20) + (4 << 20))


def call(kernel, name, scalars, arrays, outs, scratch=(), limit=0, cost=0):
    return pl.pallas_call(
        kernel,
        out_shape=outs,
        in_specs=[SMEM] * len(scalars) + [VMEM] * len(arrays),
        out_specs=[VMEM] * len(outs),
        scratch_shapes=[pltpu.VMEM(r.shape, r.dtype) for r in scratch],
        compiler_params=params([*arrays, *outs, *scratch], limit),
        cost_estimate=pl.CostEstimate(flops=cost, bytes_accessed=cost, transcendentals=0) if cost else None,
        name=name,
    )(*scalars, *arrays)


def stack_kernel(*refs):
    for i, piece in enumerate(refs[:-2]):
        refs[-1][i] = piece[...]


def mask_kernel(upper_pattern, lower_pattern, upper_panel, lower_panel, masked):
    uppers, lowers = upper_panel.shape[0], lower_panel.shape[0]
    for k in range(uppers):
        masked[k] = upper_panel[k] * upper_pattern[k].astype(F32).astype(jnp.bfloat16)
    for m in range(lowers):
        masked[uppers + m] = lower_panel[m] * lower_pattern[m].astype(F32).astype(jnp.bfloat16)


def turn_kernel(*refs):
    pieces, turned = refs[:-1], refs[-1]
    total, block = pieces[0].shape[0], pieces[0].shape[-1]
    for k in range(total):
        for o, piece in enumerate(pieces):
            turned[k, :, o * block : (o + 1) * block] = piece[k].T


def top_kernel(top, panel, out, out_turned, panel_turned):
    depth, width, block, _ = top.shape
    row, col = lax.axis_index("row"), lax.axis_index("col")
    half = width // 2

    def tile(o, i):
        return top[lax.rem(col + o, depth), row ^ (2 * (i % half) + i // half)]

    for o in range(out.shape[1] // block):
        rows = slice(o * block, (o + 1) * block)
        for i in range(width):
            out[i // half, rows, (i % half) * block : (i % half + 1) * block] = tile(o, i)

    for o in range(1, out.shape[1] // block):
        lanes = slice((o - 1) * block, o * block)
        for i in range(width):
            out_turned[i * block : (i + 1) * block, lanes] = tile(o, i).T
    for m in range(panel.shape[0]):
        panel_turned[m] = panel[m].T


def partial_kernel(top, *refs):
    pieces, (keep, away) = refs[:-2], refs[-2:]
    half, total, block, _ = keep.shape
    for first in range(0, total, 2):
        second = min(first + 1, total - 1)
        right = [jnp.concatenate([p[first], p[second]], axis=1) for p in pieces]
        value = jnp.dot(top[...], jnp.concatenate(right), preferred_element_type=F32)
        for lane, k in enumerate(range(first, second + 1)):
            for i in range(half):
                lanes = slice(lane * block, (lane + 1) * block)
                keep[i, k] = value[i * block : (i + 1) * block, lanes]
                far = value[(half + i) * block : (half + i + 1) * block, lanes]
                away[i, k] = far.astype(away.dtype)


def dot_pair(left, pieces, first, second):
    right = [
        jnp.concatenate([pieces[i, first], pieces[i, second]], axis=1)
        for i in range(pieces.shape[0])
    ]
    return jnp.dot(left, jnp.concatenate(right), preferred_element_type=F32)


def first_kernel(top, near, out):
    total = near.shape[1]
    for first in range(0, total, 2):
        out[first // 2] = dot_pair(top[0], near, first, min(first + 1, total - 1))


def triangle(block):
    rows = lax.broadcasted_iota(jnp.int32, (block, block), 0)
    lanes = lax.broadcasted_iota(jnp.int32, (block, block), 1)
    return rows < lanes, rows == lanes


def pack(squares, packed, start):
    total, block = squares.shape[:2]
    above, diagonal = triangle(block)
    for p in range(total // 2):
        first, second = [squares[k] + squares[k].T for k in (2 * p, 2 * p + 1)]
        packed[p * block : (p + 1) * block] = jnp.where(above, first, second)
        row = jnp.sum(jnp.where(diagonal, first, 0.0), axis=0, keepdims=True)
        packed[start + p : start + p + 1] = row
    if total % 2:
        packed[(total // 2) * block : (total // 2 + 1) * block] = squares[total - 1] + squares[total - 1].T


def unpack(packed, total, block, start):
    above, diagonal = triangle(block)
    squares = []
    for p in range(total // 2):
        value = packed[p * block : (p + 1) * block]
        turned = value.T
        row = packed[start + p : start + p + 1]
        squares.append(jnp.where(above, value, jnp.where(diagonal, row, turned)))
        squares.append(jnp.where(above, turned, value))
    if total % 2:
        squares.append(packed[(total // 2) * block : (total // 2 + 1) * block])
    return squares


def second_kernel(uppers, parents, top, far, start, turned, *refs):
    own, returns, (sums_keep, sums_away, both, squares, packed) = refs[0], refs[1:-5], refs[-5:]
    total, block, reach = turned.shape
    lowers = total - uppers
    half, chunk, _ = sums_keep.shape
    row = lax.axis_index("row")

    for first in range(0, total, 2):
        second = min(first + 1, total - 1)
        value = start[first // 2] + dot_pair(top[1], far, first, second)
        for lane, k in enumerate(range(first, second + 1)):
            part = value[:, lane * block : (lane + 1) * block]
            own[k] = part[:block]
            for o, out in enumerate(returns):
                out[k] = part[(o + 1) * block : (o + 2) * block].astype(WIRE)
            part = jnp.concatenate([0.5 * part[:block], part[block:reach]])
            high = part.astype(jnp.bfloat16)
            both[k, :, :block] = high
            both[k, :, block:] = (part - high.astype(F32)).astype(jnp.bfloat16)

    def fold(rows, k):
        value = jnp.dot(rows, both[k], preferred_element_type=F32)
        return value[:, :block] + value[:, block:]

    base = (total + 1) // 2 * block
    for k in range(uppers):
        squares[k] = fold(turned[k], k)
    for m in range(lowers):
        own_row, parent = turned[uppers + m], parents[m]
        value = fold(jnp.concatenate([own_row, turned[parent]], axis=0), uppers + m)
        squares[uppers + m] = value[:block]
        place = base + m * block
        packed[place : place + block] = value[block:] + fold(own_row, parent).T
    end = base + lowers * block
    packed[end:] = jnp.zeros((packed.shape[0] - end, block), F32)
    pack(squares, packed, end)
    for m in range(2 * half):
        place = pl.multiple_of((row ^ m) * chunk, chunk)
        (sums_away if m & 1 else sums_keep)[m // 2] = packed[pl.ds(place, chunk)]


def line_kernel(*refs):
    parts, (total_out, order) = refs[:-2], refs[-2:]
    depth, col = len(parts), lax.axis_index("col")
    for o in range(depth):
        order[lax.rem(col + o, depth)] = parts[o][...].astype(F32)
    total = order[0]
    for c in range(1, depth):
        total = total + order[c]
    total_out[...] = total.astype(total_out.dtype)


def columns_kernel(parents, upper_pattern, lower_pattern, panel, own, *refs):
    front, back, got, (upper_out, lower_out) = refs[0:4:2], refs[1:4:2], refs[4:-2], refs[-2:]
    uppers, lowers, middle = upper_out.shape[0], lower_out.shape[0], front[0].shape[0]

    def product(k):
        value = own[k]
        for piece in front if k < middle else back:
            value = value + piece[k - (0 if k < middle else middle)].astype(F32)
        for piece in got:
            value = value + piece[k].astype(F32)
        return value

    for k in range(uppers):
        upper_out[k] = (-product(k) * upper_pattern[k].astype(F32)).astype(jnp.bfloat16)
    extensions = [
        jnp.dot(upper_out[parents[m]], panel[m], preferred_element_type=F32) for m in range(lowers)
    ]
    for m in range(lowers):
        value = -(product(uppers + m) + extensions[m]) * lower_pattern[m].astype(F32)
        lower_out[m] = value.astype(jnp.bfloat16)


def split(wide):
    high = wide.astype(jnp.bfloat16)
    return high, (wide - high.astype(F32)).astype(jnp.bfloat16)


def blocks_kernel(
    width,
    parents,
    near,
    far,
    upper_diagonal,
    lower_diagonal,
    panel,
    panel_turned,
    upper_out,
    cross_out,
    lower_out,
    packed,
    halves,
):
    uppers, lowers = upper_out.shape[0], lower_out.shape[0]
    block = panel.shape[-1]
    chunk = near.shape[1]
    row = lax.axis_index("row")
    for m in range(width):
        place = pl.multiple_of((row ^ m) * chunk, chunk)
        packed[pl.ds(place, chunk)] = (far if m & 1 else near)[m // 2].astype(F32)
    base = (uppers + lowers + 1) // 2 * block
    squares = unpack(packed, uppers + lowers, block, base + lowers * block)
    for k in range(uppers):
        value = upper_diagonal[k] + squares[k]
        upper_out[k] = value
        halves[k, :block], halves[k, block:] = split(value)
    products = [
        jnp.dot(halves[parents[m]], panel[m], preferred_element_type=F32) for m in range(lowers)
    ]
    rights = []
    for m in range(lowers):
        forms = packed[base + m * block : base + (m + 1) * block]
        cross = forms - (products[m][:block] + products[m][block:])
        cross_out[m] = cross
        rights.append(jnp.concatenate([forms.astype(jnp.bfloat16), *split(cross)], axis=1))
    backs = [
        jnp.dot(panel_turned[m], rights[m], preferred_element_type=F32) for m in range(lowers)
    ]
    for m in range(lowers):
        value = backs[m]
        rest = value[:, block : 2 * block] + value[:, 2 * block :]
        lower_out[m] = lower_diagonal[m] + squares[uppers + m] - rest - value[:, :block].T


def gather_shifts(value, axis):
    size = lax.axis_size(axis)
    return [value] + [shift(value, axis, -o) for o in range(1, size)]


def pairs(size, offset):
    takers = range(size)
    if 2 * offset == size:
        takers = [c if c % 2 == 0 else c + offset for c in range(offset)]
    return [(c, (c + offset) % size) for c in takers]


def gather_pair(value, axis, offset):
    return lax.ppermute(value, axis, [(b, c) for c, b in pairs(lax.axis_size(axis), offset)])


def return_pair(value, axis, offset):
    return lax.ppermute(value, axis, pairs(lax.axis_size(axis), offset))


def halve(value, axis, bit, left):
    place = sorted(left, reverse=True).index(bit)
    value = value.reshape((2,) * len(left) + value.shape[-3:])
    away = lax.index_in_dim(value, 1, place, keepdims=False).astype(WIRE)
    keep = lax.index_in_dim(value, 0, place, keepdims=False)
    return keep, flip(away, axis, 1 << bit)


def gather_near(value, axis):
    masks = range(2, lax.axis_size(axis), 2)
    return [value] + [flip(value, axis, m) for m in masks]


def scatter_flips(value, axis):
    masks = range(2, lax.axis_size(axis), 2)
    return [flip(value[m // 2].astype(WIRE), axis, m) for m in masks]


def tie(*values):
    return lax.optimization_barrier(values)


def per_device(
    top_inverse,
    upper_panel,
    upper_pattern,
    upper_diagonal,
    lower_panel,
    lower_pattern,
    parents,
    parent_panel,
    lower_diagonal,
):
    uppers, block = upper_panel.shape[0], upper_panel.shape[-1]
    lowers = lower_panel.shape[0]
    total = uppers + lowers
    width, depth = lax.axis_size("row"), lax.axis_size("col")
    half = width // 2
    packed_n = (total + 1) // 2 * block + lowers * block + total // 2
    chunk = ceil_to(packed_n, 16 * width) // width
    bf16 = jnp.bfloat16
    upper_pattern, lower_pattern = upper_pattern.reshape(-1), lower_pattern.reshape(-1)

    (masked,) = call(
        mask_kernel,
        "mask",
        (upper_pattern, lower_pattern),
        (upper_panel.reshape(-1, block, block), lower_panel.reshape(-1, block, block)),
        [shape_of((total, block, block), bf16)],
        limit=60 << 20,
    )
    reach = depth // 2
    pieces = [gather_pair(masked, "col", o) for o in range(1, reach + 1)]
    (turned,) = call(
        turn_kernel,
        "turn",
        (),
        (masked, *pieces),
        [shape_of((total, block, (reach + 1) * block), bf16)],
    )
    (near,) = call(
        stack_kernel,
        "stack",
        (),
        (*gather_near(masked, "row"), turned),
        [shape_of((half, total, block, block), bf16)],
    )
    far = flip(near, "row", 1)
    top, top_turned, panel_turned = call(
        top_kernel,
        "top",
        (),
        (top_inverse[0, :, :, 0], parent_panel),
        [
            shape_of((2, (reach + 1) * block, half * block), bf16),
            shape_of((width * block, reach * block), bf16),
            shape_of(parent_panel.shape, bf16),
        ],
    )
    keep, away = call(
        partial_kernel,
        "partial",
        (),
        (top_turned, *pieces),
        [
            shape_of((half, total, block, block), F32),
            shape_of((half, total, block, block), WIRE),
        ],
    )
    columns_n = ceil_to(total, 2) // 2
    (start,) = call(
        first_kernel,
        "first",
        (),
        (top, near),
        [shape_of((columns_n, (reach + 1) * block, 2 * block), F32)],
    )
    own, *rest = call(
        functools.partial(second_kernel, uppers),
        "second",
        (parents,),
        (top, far, start, turned),
        [shape_of((total, block, block), F32)]
        + [shape_of((total, block, block), WIRE)] * reach
        + [shape_of((half, chunk, block), F32)] * 2,
        [
            shape_of((total, (reach + 1) * block, 2 * block), bf16),
            shape_of((total, block, block), F32),
            shape_of((width * chunk, block), F32),
        ],
    )
    returns, (sums_keep, sums_away) = rest[:-2], rest[-2:]

    other, across = tie(flip(sums_away, "row", 1), flip(away, "row", 1))
    sums = sums_keep + other
    pieces = scatter_flips(sums, "row")
    pieces[0], value = tie(pieces[0], keep + across.astype(F32))
    middle = total // 2
    bits = list(range(1, width.bit_length() - 1))
    sides = [value[:, :middle], value[:, middle:]]
    halves = [halve(side, "row", bit, bits) for side, bit in zip(sides, (bits[0], bits[-1]))]
    part = sums[0]
    for piece in pieces:
        part = part + piece.astype(F32)
    part = part.astype(WIRE)
    early = [return_pair(returns[o - 1], "col", o) for o in range(1, reach)]
    parts = gather_shifts(part, "col")
    tied = tie(*parts, *[got for _, got in halves], *early)
    early = tied[depth + 2 :]
    (part,) = call(
        line_kernel,
        "line",
        (),
        tied[:depth],
        [shape_of((chunk, block), WIRE)],
        [shape_of((depth, chunk, block), F32)],
    )
    sides = [keep + got.astype(F32) for (keep, _), got in zip(halves, tied[depth : depth + 2])]
    part, last, *sides = tie(part, returns[-1], *sides)
    nears = gather_near(part, "row")
    nears[-1], *sides = tie(nears[-1], *sides)
    near = jnp.stack(nears)
    far = flip(near, "row", 1)
    got = [*early, return_pair(last, "col", reach)]
    for i in range(1, len(bits)):
        keeps, across = zip(
            halve(sides[0], "row", bits[i], bits[i:]),
            halve(sides[1], "row", bits[-1 - i], bits[: len(bits) - i]),
        )
        if i == len(bits) - 1:
            got += across
            sides = keeps
        else:
            sides = [keep + piece.astype(F32) for keep, piece in zip(keeps, across)]
    front, back = [side.reshape(-1, block, block) for side in sides]

    upper_blocks, lower_cross, lower_blocks = call(
        functools.partial(blocks_kernel, width),
        "blocks",
        (parents,),
        (near, far, upper_diagonal, lower_diagonal, parent_panel, panel_turned),
        [
            shape_of((uppers, block, block), F32),
            shape_of((lowers, block, block), F32),
            shape_of((lowers, block, block), F32),
        ],
        [shape_of((width * chunk, block), F32), shape_of((uppers, 2 * block, block), bf16)],
    )
    upper_blocks, *got = tie(upper_blocks, *got)
    across = [piece.reshape(-1, block, block) for piece in got[reach:]]
    upper_columns, lower_columns = call(
        columns_kernel,
        "columns",
        (parents, upper_pattern, lower_pattern),
        (parent_panel, own, front, back, *across, *got[:reach]),
        [
            shape_of((uppers, block, block), bf16),
            shape_of((lowers, block, block), bf16),
        ],
    )
    return (
        upper_columns[:, None, None],
        upper_blocks,
        lower_columns[:, None, None],
        lower_cross,
        lower_blocks,
    )


def solution(mesh):
    return jax.shard_map(
        per_device,
        mesh=mesh,
        in_specs=(
            P("row", None, None, "col", None, None),
            P(None, "row", "col", None, None),
            P(None, "row", "col"),
            P(),
            P(None, "row", "col", None, None),
            P(None, "row", "col"),
            P(),
            P(),
            P(),
        ),
        out_specs=(
            P(None, "row", "col", None, None),
            P(),
            P(None, "row", "col", None, None),
            P(),
            P(),
        ),
        check_vma=False,
    )
```

```python
import functools

import jax
import jax.numpy as jnp
import numpy as np
from jax import lax
from jax.experimental import pallas as pl
from jax.experimental.pallas import tpu as pltpu
from jax.sharding import PartitionSpec as P

F32 = jnp.float32
WIRE = jnp.bfloat16
VMEM = pl.BlockSpec(memory_space=pltpu.VMEM)
SMEM = pl.BlockSpec(memory_space=pltpu.SMEM)


def shape_of(dims, kind):
    return jax.ShapeDtypeStruct(dims, kind)


def flip(value, axis, mask):
    size = lax.axis_size(axis)
    return lax.ppermute(value, axis, [(i, i ^ mask) for i in range(size)])


def shift(value, axis, step):
    size = lax.axis_size(axis)
    return lax.ppermute(value, axis, [(i, (i + step) % size) for i in range(size)])


def ceil_to(value, step):
    return -(-value // step) * step


def params(refs, limit):
    size = sum(int(np.prod(r.shape)) * np.dtype(r.dtype).itemsize for r in refs)
    return pltpu.CompilerParams(vmem_limit_bytes=limit or ceil_to(size * 5 // 4, 1 << 20) + (4 << 20))


def call(kernel, name, scalars, arrays, outs, scratch=(), limit=0, cost=0):
    return pl.pallas_call(
        kernel,
        out_shape=outs,
        in_specs=[SMEM] * len(scalars) + [VMEM] * len(arrays),
        out_specs=[VMEM] * len(outs),
        scratch_shapes=[pltpu.VMEM(r.shape, r.dtype) for r in scratch],
        compiler_params=params([*arrays, *outs, *scratch], limit),
        cost_estimate=pl.CostEstimate(flops=cost, bytes_accessed=cost, transcendentals=0) if cost else None,
        name=name,
    )(*scalars, *arrays)


def stack_kernel(*refs):
    for i, piece in enumerate(refs[:-2]):
        refs[-1][i] = piece[...]


def mask_kernel(upper_pattern, lower_pattern, upper_panel, lower_panel, masked):
    uppers, lowers = upper_panel.shape[0], lower_panel.shape[0]
    for k in range(uppers):
        masked[k] = upper_panel[k] * upper_pattern[k].astype(F32).astype(jnp.bfloat16)
    for m in range(lowers):
        masked[uppers + m] = lower_panel[m] * lower_pattern[m].astype(F32).astype(jnp.bfloat16)


def turn_kernel(*refs):
    pieces, turned = refs[:-1], refs[-1]
    total, block = pieces[0].shape[0], pieces[0].shape[-1]
    for k in range(total):
        for o, piece in enumerate(pieces):
            turned[k, :, o * block : (o + 1) * block] = piece[k].T


def top_kernel(top, panel, out, out_turned, panel_turned):
    depth, width, block, _ = top.shape
    row, col = lax.axis_index("row"), lax.axis_index("col")
    half = width // 2

    def tile(o, i):
        return top[lax.rem(col + o, depth), row ^ (2 * (i % half) + i // half)]

    for o in range(out.shape[1] // block):
        rows = slice(o * block, (o + 1) * block)
        for i in range(width):
            out[i // half, rows, (i % half) * block : (i % half + 1) * block] = tile(o, i)

    for o in range(1, out.shape[1] // block):
        lanes = slice((o - 1) * block, o * block)
        for i in range(width):
            out_turned[i * block : (i + 1) * block, lanes] = tile(o, i).T
    for m in range(panel.shape[0]):
        panel_turned[m] = panel[m].T


def partial_kernel(top, *refs):
    pieces, (keep, away) = refs[:-2], refs[-2:]
    half, total, block, _ = keep.shape
    for first in range(0, total, 2):
        second = min(first + 1, total - 1)
        right = [jnp.concatenate([p[first], p[second]], axis=1) for p in pieces]
        value = jnp.dot(top[...], jnp.concatenate(right), preferred_element_type=F32)
        for lane, k in enumerate(range(first, second + 1)):
            for i in range(half):
                lanes = slice(lane * block, (lane + 1) * block)
                keep[i, k] = value[i * block : (i + 1) * block, lanes]
                far = value[(half + i) * block : (half + i + 1) * block, lanes]
                away[i, k] = far.astype(away.dtype)


def dot_pair(left, pieces, first, second):
    right = [
        jnp.concatenate([pieces[i, first], pieces[i, second]], axis=1)
        for i in range(pieces.shape[0])
    ]
    return jnp.dot(left, jnp.concatenate(right), preferred_element_type=F32)


def first_kernel(top, near, out):
    total = near.shape[1]
    for first in range(0, total, 2):
        out[first // 2] = dot_pair(top[0], near, first, min(first + 1, total - 1))


def triangle(block):
    rows = lax.broadcasted_iota(jnp.int32, (block, block), 0)
    lanes = lax.broadcasted_iota(jnp.int32, (block, block), 1)
    return rows < lanes, rows == lanes


def pack(squares, packed, start):
    total, block = squares.shape[:2]
    above, diagonal = triangle(block)
    for p in range(total // 2):
        first, second = [squares[k] + squares[k].T for k in (2 * p, 2 * p + 1)]
        packed[p * block : (p + 1) * block] = jnp.where(above, first, second)
        row = jnp.sum(jnp.where(diagonal, first, 0.0), axis=0, keepdims=True)
        packed[start + p : start + p + 1] = row
    if total % 2:
        packed[(total // 2) * block : (total // 2 + 1) * block] = squares[total - 1] + squares[total - 1].T


def unpack(packed, total, block, start):
    above, diagonal = triangle(block)
    squares = []
    for p in range(total // 2):
        value = packed[p * block : (p + 1) * block]
        turned = value.T
        row = packed[start + p : start + p + 1]
        squares.append(jnp.where(above, value, jnp.where(diagonal, row, turned)))
        squares.append(jnp.where(above, turned, value))
    if total % 2:
        squares.append(packed[(total // 2) * block : (total // 2 + 1) * block])
    return squares


def second_kernel(uppers, parents, top, far, start, turned, *refs):
    own, returns, (sums_keep, sums_away, both, squares, packed) = refs[0], refs[1:-5], refs[-5:]
    total, block, reach = turned.shape
    lowers = total - uppers
    half, chunk, _ = sums_keep.shape
    row = lax.axis_index("row")

    for first in range(0, total, 2):
        second = min(first + 1, total - 1)
        value = start[first // 2] + dot_pair(top[1], far, first, second)
        for lane, k in enumerate(range(first, second + 1)):
            part = value[:, lane * block : (lane + 1) * block]
            own[k] = part[:block]
            for o, out in enumerate(returns):
                out[k] = part[(o + 1) * block : (o + 2) * block].astype(WIRE)
            part = jnp.concatenate([0.5 * part[:block], part[block:reach]])
            high = part.astype(jnp.bfloat16)
            both[k, :, :block] = high
            both[k, :, block:] = (part - high.astype(F32)).astype(jnp.bfloat16)

    def fold(rows, k):
        value = jnp.dot(rows, both[k], preferred_element_type=F32)
        return value[:, :block] + value[:, block:]

    base = (total + 1) // 2 * block
    for k in range(uppers):
        squares[k] = fold(turned[k], k)
    for m in range(lowers):
        own_row, parent = turned[uppers + m], parents[m]
        value = fold(jnp.concatenate([own_row, turned[parent]], axis=0), uppers + m)
        squares[uppers + m] = value[:block]
        place = base + m * block
        packed[place : place + block] = value[block:] + fold(own_row, parent).T
    end = base + lowers * block
    packed[end:] = jnp.zeros((packed.shape[0] - end, block), F32)
    pack(squares, packed, end)
    for m in range(2 * half):
        place = pl.multiple_of((row ^ m) * chunk, chunk)
        (sums_away if m & 1 else sums_keep)[m // 2] = packed[pl.ds(place, chunk)]


def line_kernel(*refs):
    parts, (total_out, order) = refs[:-2], refs[-2:]
    depth, col = len(parts), lax.axis_index("col")
    for o in range(depth):
        order[lax.rem(col + o, depth)] = parts[o][...].astype(F32)
    total = order[0]
    for c in range(1, depth):
        total = total + order[c]
    total_out[...] = total.astype(total_out.dtype)


def columns_kernel(parents, upper_pattern, lower_pattern, panel, own, front, back, *refs):
    got, (upper_out, lower_out) = refs[:-2], refs[-2:]
    uppers, lowers, middle = upper_out.shape[0], lower_out.shape[0], front.shape[0]

    def product(k):
        value = own[k] + (front[k] if k < middle else back[k - middle])
        for piece in got:
            value = value + piece[k].astype(F32)
        return value

    for k in range(uppers):
        upper_out[k] = (-product(k) * upper_pattern[k].astype(F32)).astype(jnp.bfloat16)
    extensions = [
        jnp.dot(upper_out[parents[m]], panel[m], preferred_element_type=F32) for m in range(lowers)
    ]
    for m in range(lowers):
        value = -(product(uppers + m) + extensions[m]) * lower_pattern[m].astype(F32)
        lower_out[m] = value.astype(jnp.bfloat16)


def split(wide):
    high = wide.astype(jnp.bfloat16)
    return high, (wide - high.astype(F32)).astype(jnp.bfloat16)


def blocks_kernel(
    width,
    parents,
    near,
    far,
    upper_diagonal,
    lower_diagonal,
    panel,
    panel_turned,
    upper_out,
    cross_out,
    lower_out,
    packed,
    halves,
):
    uppers, lowers = upper_out.shape[0], lower_out.shape[0]
    block = panel.shape[-1]
    chunk = near.shape[1]
    row = lax.axis_index("row")
    for m in range(width):
        place = pl.multiple_of((row ^ m) * chunk, chunk)
        packed[pl.ds(place, chunk)] = (far if m & 1 else near)[m // 2].astype(F32)
    base = (uppers + lowers + 1) // 2 * block
    squares = unpack(packed, uppers + lowers, block, base + lowers * block)
    for k in range(uppers):
        value = upper_diagonal[k] + squares[k]
        upper_out[k] = value
        halves[k, :block], halves[k, block:] = split(value)
    products = [
        jnp.dot(halves[parents[m]], panel[m], preferred_element_type=F32) for m in range(lowers)
    ]
    rights = []
    for m in range(lowers):
        forms = packed[base + m * block : base + (m + 1) * block]
        cross = forms - (products[m][:block] + products[m][block:])
        cross_out[m] = cross
        rights.append(jnp.concatenate([forms.astype(jnp.bfloat16), *split(cross)], axis=1))
    backs = [
        jnp.dot(panel_turned[m], rights[m], preferred_element_type=F32) for m in range(lowers)
    ]
    for m in range(lowers):
        value = backs[m]
        rest = value[:, block : 2 * block] + value[:, 2 * block :]
        lower_out[m] = lower_diagonal[m] + squares[uppers + m] - rest - value[:, :block].T


def gather_shifts(value, axis):
    size = lax.axis_size(axis)
    return [value] + [shift(value, axis, -o) for o in range(1, size)]


def pairs(size, offset):
    takers = range(size)
    if 2 * offset == size:
        takers = [c if c % 2 == 0 else c + offset for c in range(offset)]
    return [(c, (c + offset) % size) for c in takers]


def gather_pair(value, axis, offset):
    return lax.ppermute(value, axis, [(b, c) for c, b in pairs(lax.axis_size(axis), offset)])


def return_pair(value, axis, offset):
    return lax.ppermute(value, axis, pairs(lax.axis_size(axis), offset))


def halve(value, axis, bit, left):
    place = sorted(left, reverse=True).index(bit)
    value = value.reshape((2,) * len(left) + value.shape[-3:])
    away = lax.index_in_dim(value, 1, place, keepdims=False).astype(WIRE)
    keep = lax.index_in_dim(value, 0, place, keepdims=False)
    return keep, flip(away, axis, 1 << bit)


def gather_near(value, axis):
    masks = range(2, lax.axis_size(axis), 2)
    return [value] + [flip(value, axis, m) for m in masks]


def scatter_flips(value, axis):
    masks = range(2, lax.axis_size(axis), 2)
    return [flip(value[m // 2].astype(WIRE), axis, m) for m in masks]


def tie(*values):
    return lax.optimization_barrier(values)


def per_device(
    top_inverse,
    upper_panel,
    upper_pattern,
    upper_diagonal,
    lower_panel,
    lower_pattern,
    parents,
    parent_panel,
    lower_diagonal,
):
    uppers, block = upper_panel.shape[0], upper_panel.shape[-1]
    lowers = lower_panel.shape[0]
    total = uppers + lowers
    width, depth = lax.axis_size("row"), lax.axis_size("col")
    half = width // 2
    packed_n = (total + 1) // 2 * block + lowers * block + total // 2
    chunk = ceil_to(packed_n, 16 * width) // width
    bf16 = jnp.bfloat16
    upper_pattern, lower_pattern = upper_pattern.reshape(-1), lower_pattern.reshape(-1)

    (masked,) = call(
        mask_kernel,
        "mask",
        (upper_pattern, lower_pattern),
        (upper_panel.reshape(-1, block, block), lower_panel.reshape(-1, block, block)),
        [shape_of((total, block, block), bf16)],
        limit=60 << 20,
    )
    reach = depth // 2
    pieces = [gather_pair(masked, "col", o) for o in range(1, reach + 1)]
    (turned,) = call(
        turn_kernel,
        "turn",
        (),
        (masked, *pieces),
        [shape_of((total, block, (reach + 1) * block), bf16)],
    )
    (near,) = call(
        stack_kernel,
        "stack",
        (),
        (*gather_near(masked, "row"), turned),
        [shape_of((half, total, block, block), bf16)],
    )
    far = flip(near, "row", 1)
    top, top_turned, panel_turned = call(
        top_kernel,
        "top",
        (),
        (top_inverse[0, :, :, 0], parent_panel),
        [
            shape_of((2, (reach + 1) * block, half * block), bf16),
            shape_of((width * block, reach * block), bf16),
            shape_of(parent_panel.shape, bf16),
        ],
    )
    keep, away = call(
        partial_kernel,
        "partial",
        (),
        (top_turned, *pieces),
        [
            shape_of((half, total, block, block), F32),
            shape_of((half, total, block, block), WIRE),
        ],
    )
    columns_n = ceil_to(total, 2) // 2
    (start,) = call(
        first_kernel,
        "first",
        (),
        (top, near),
        [shape_of((columns_n, (reach + 1) * block, 2 * block), F32)],
    )
    own, *rest = call(
        functools.partial(second_kernel, uppers),
        "second",
        (parents,),
        (top, far, start, turned),
        [shape_of((total, block, block), F32)]
        + [shape_of((total, block, block), WIRE)] * reach
        + [shape_of((half, chunk, block), F32)] * 2,
        [
            shape_of((total, (reach + 1) * block, 2 * block), bf16),
            shape_of((total, block, block), F32),
            shape_of((width * chunk, block), F32),
        ],
    )
    returns, (sums_keep, sums_away) = rest[:-2], rest[-2:]

    other, across = tie(flip(sums_away, "row", 1), flip(away, "row", 1))
    sums = sums_keep + other
    pieces = scatter_flips(sums, "row")
    pieces[0], value = tie(pieces[0], keep + across.astype(F32))
    middle = total // 2
    bits = list(range(1, width.bit_length() - 1))
    sides = [value[:, :middle], value[:, middle:]]
    halves = [halve(side, "row", bit, bits) for side, bit in zip(sides, (bits[0], bits[-1]))]
    part = sums[0]
    for piece in pieces:
        part = part + piece.astype(F32)
    part = part.astype(WIRE)
    early = [return_pair(returns[o - 1], "col", o) for o in range(1, reach)]
    parts = gather_shifts(part, "col")
    tied = tie(*parts, *[got for _, got in halves], *early)
    early = tied[depth + 2 :]
    (part,) = call(
        line_kernel,
        "line",
        (),
        tied[:depth],
        [shape_of((chunk, block), WIRE)],
        [shape_of((depth, chunk, block), F32)],
    )
    sides = [keep + got.astype(F32) for (keep, _), got in zip(halves, tied[depth : depth + 2])]
    part, *sides = tie(part, *sides)
    last = returns[-1]
    nears = gather_near(part, "row")
    near = jnp.stack(nears)
    far = flip(near, "row", 1)
    got = [*early, return_pair(last, "col", reach)]
    front, back = sides
    for i in range(1, len(bits)):
        keep, across = halve(front, "row", bits[i], bits[i:])
        front = keep + across.astype(F32)
        keep, across = halve(back, "row", bits[-1 - i], bits[: len(bits) - i])
        back = keep + across.astype(F32)
    front, back = [side.reshape(-1, block, block) for side in (front, back)]

    upper_blocks, lower_cross, lower_blocks = call(
        functools.partial(blocks_kernel, width),
        "blocks",
        (parents,),
        (near, far, upper_diagonal, lower_diagonal, parent_panel, panel_turned),
        [
            shape_of((uppers, block, block), F32),
            shape_of((lowers, block, block), F32),
            shape_of((lowers, block, block), F32),
        ],
        [shape_of((width * chunk, block), F32), shape_of((uppers, 2 * block, block), bf16)],
    )
    upper_blocks, *got = tie(upper_blocks, *got)
    upper_columns, lower_columns = call(
        columns_kernel,
        "columns",
        (parents, upper_pattern, lower_pattern),
        (parent_panel, own, front, back, *got),
        [
            shape_of((uppers, block, block), bf16),
            shape_of((lowers, block, block), bf16),
        ],
    )
    return (
        upper_columns[:, None, None],
        upper_blocks,
        lower_columns[:, None, None],
        lower_cross,
        lower_blocks,
    )


def solution(mesh):
    return jax.shard_map(
        per_device,
        mesh=mesh,
        in_specs=(
            P("row", None, None, "col", None, None),
            P(None, "row", "col", None, None),
            P(None, "row", "col"),
            P(),
            P(None, "row", "col", None, None),
            P(None, "row", "col"),
            P(),
            P(),
            P(),
        ),
        out_specs=(
            P(None, "row", "col", None, None),
            P(),
            P(None, "row", "col", None, None),
            P(),
            P(),
        ),
        check_vma=False,
    )
```

```python
import functools

import jax
import jax.numpy as jnp
import numpy as np
from jax import lax
from jax.experimental import pallas as pl
from jax.experimental.pallas import tpu as pltpu
from jax.sharding import PartitionSpec as P

F32 = jnp.float32
WIRE = jnp.bfloat16
VMEM = pl.BlockSpec(memory_space=pltpu.VMEM)
SMEM = pl.BlockSpec(memory_space=pltpu.SMEM)


def shape_of(dims, kind):
    return jax.ShapeDtypeStruct(dims, kind)


def flip(value, axis, mask):
    size = lax.axis_size(axis)
    return lax.ppermute(value, axis, [(i, i ^ mask) for i in range(size)])


def shift(value, axis, step):
    size = lax.axis_size(axis)
    return lax.ppermute(value, axis, [(i, (i + step) % size) for i in range(size)])


def ceil_to(value, step):
    return -(-value // step) * step


def params(refs, limit):
    size = sum(int(np.prod(r.shape)) * np.dtype(r.dtype).itemsize for r in refs)
    return pltpu.CompilerParams(vmem_limit_bytes=limit or ceil_to(size * 5 // 4, 1 << 20) + (4 << 20))


def call(kernel, name, scalars, arrays, outs, scratch=(), limit=0, cost=0):
    return pl.pallas_call(
        kernel,
        out_shape=outs,
        in_specs=[SMEM] * len(scalars) + [VMEM] * len(arrays),
        out_specs=[VMEM] * len(outs),
        scratch_shapes=[pltpu.VMEM(r.shape, r.dtype) for r in scratch],
        compiler_params=params([*arrays, *outs, *scratch], limit),
        cost_estimate=pl.CostEstimate(flops=cost, bytes_accessed=cost, transcendentals=0) if cost else None,
        name=name,
    )(*scalars, *arrays)


def stack_kernel(*refs):
    for i, piece in enumerate(refs[:-2]):
        refs[-1][i] = piece[...]


def mask_kernel(upper_pattern, lower_pattern, upper_panel, lower_panel, masked):
    uppers, lowers = upper_panel.shape[0], lower_panel.shape[0]
    for k in range(uppers):
        masked[k] = upper_panel[k] * upper_pattern[k].astype(F32).astype(jnp.bfloat16)
    for m in range(lowers):
        masked[uppers + m] = lower_panel[m] * lower_pattern[m].astype(F32).astype(jnp.bfloat16)


def turn_kernel(*refs):
    pieces, turned = refs[:-1], refs[-1]
    total, block = pieces[0].shape[0], pieces[0].shape[-1]
    for k in range(total):
        for o, piece in enumerate(pieces):
            turned[k, :, o * block : (o + 1) * block] = piece[k].T


def top_kernel(top, panel, out, out_turned, panel_turned):
    depth, width, block, _ = top.shape
    row, col = lax.axis_index("row"), lax.axis_index("col")
    half = width // 2

    def tile(o, i):
        return top[lax.rem(col + o, depth), row ^ (2 * (i % half) + i // half)]

    for o in range(out.shape[1] // block):
        rows = slice(o * block, (o + 1) * block)
        for i in range(width):
            out[i // half, rows, (i % half) * block : (i % half + 1) * block] = tile(o, i)

    for o in range(1, out.shape[1] // block):
        lanes = slice((o - 1) * block, o * block)
        for i in range(width):
            out_turned[i * block : (i + 1) * block, lanes] = tile(o, i).T
    for m in range(panel.shape[0]):
        panel_turned[m] = panel[m].T


def partial_kernel(top, *refs):
    pieces, (keep, away) = refs[:-2], refs[-2:]
    half, total, block, _ = keep.shape
    for first in range(0, total, 2):
        second = min(first + 1, total - 1)
        right = [jnp.concatenate([p[first], p[second]], axis=1) for p in pieces]
        value = jnp.dot(top[...], jnp.concatenate(right), preferred_element_type=F32)
        for lane, k in enumerate(range(first, second + 1)):
            for i in range(half):
                lanes = slice(lane * block, (lane + 1) * block)
                keep[i, k] = value[i * block : (i + 1) * block, lanes]
                far = value[(half + i) * block : (half + i + 1) * block, lanes]
                away[i, k] = far.astype(away.dtype)


def dot_pair(left, pieces, first, second):
    right = [
        jnp.concatenate([pieces[i, first], pieces[i, second]], axis=1)
        for i in range(pieces.shape[0])
    ]
    return jnp.dot(left, jnp.concatenate(right), preferred_element_type=F32)


def first_kernel(top, near, out):
    total = near.shape[1]
    for first in range(0, total, 2):
        out[first // 2] = dot_pair(top[0], near, first, min(first + 1, total - 1))


def triangle(block):
    rows = lax.broadcasted_iota(jnp.int32, (block, block), 0)
    lanes = lax.broadcasted_iota(jnp.int32, (block, block), 1)
    return rows < lanes, rows == lanes


def pack(squares, packed, start):
    total, block = squares.shape[:2]
    above, diagonal = triangle(block)
    for p in range(total // 2):
        first, second = [squares[k] + squares[k].T for k in (2 * p, 2 * p + 1)]
        packed[p * block : (p + 1) * block] = jnp.where(above, first, second)
        row = jnp.sum(jnp.where(diagonal, first, 0.0), axis=0, keepdims=True)
        packed[start + p : start + p + 1] = row
    if total % 2:
        packed[(total // 2) * block : (total // 2 + 1) * block] = squares[total - 1] + squares[total - 1].T


def unpack(packed, total, block, start):
    above, diagonal = triangle(block)
    squares = []
    for p in range(total // 2):
        value = packed[p * block : (p + 1) * block]
        turned = value.T
        row = packed[start + p : start + p + 1]
        squares.append(jnp.where(above, value, jnp.where(diagonal, row, turned)))
        squares.append(jnp.where(above, turned, value))
    if total % 2:
        squares.append(packed[(total // 2) * block : (total // 2 + 1) * block])
    return squares


def second_kernel(uppers, parents, top, far, start, turned, *refs):
    own, returns, (sums_keep, sums_away, both, squares, packed) = refs[0], refs[1:-5], refs[-5:]
    total, block, reach = turned.shape
    lowers = total - uppers
    half, chunk, _ = sums_keep.shape
    row = lax.axis_index("row")

    for first in range(0, total, 2):
        second = min(first + 1, total - 1)
        value = start[first // 2] + dot_pair(top[1], far, first, second)
        for lane, k in enumerate(range(first, second + 1)):
            part = value[:, lane * block : (lane + 1) * block]
            own[k] = part[:block]
            for o, out in enumerate(returns):
                out[k] = part[(o + 1) * block : (o + 2) * block].astype(WIRE)
            part = jnp.concatenate([0.5 * part[:block], part[block:reach]])
            high = part.astype(jnp.bfloat16)
            both[k, :, :block] = high
            both[k, :, block:] = (part - high.astype(F32)).astype(jnp.bfloat16)

    def fold(rows, k):
        value = jnp.dot(rows, both[k], preferred_element_type=F32)
        return value[:, :block] + value[:, block:]

    base = (total + 1) // 2 * block
    for k in range(uppers):
        squares[k] = fold(turned[k], k)
    for m in range(lowers):
        own_row, parent = turned[uppers + m], parents[m]
        value = fold(jnp.concatenate([own_row, turned[parent]], axis=0), uppers + m)
        squares[uppers + m] = value[:block]
        place = base + m * block
        packed[place : place + block] = value[block:] + fold(own_row, parent).T
    end = base + lowers * block
    packed[end:] = jnp.zeros((packed.shape[0] - end, block), F32)
    pack(squares, packed, end)
    for m in range(2 * half):
        place = pl.multiple_of((row ^ m) * chunk, chunk)
        (sums_away if m & 1 else sums_keep)[m // 2] = packed[pl.ds(place, chunk)]


def line_kernel(*refs):
    parts, (total_out, order) = refs[:-2], refs[-2:]
    depth, col = len(parts), lax.axis_index("col")
    for o in range(depth):
        order[lax.rem(col + o, depth)] = parts[o][...].astype(F32)
    total = order[0]
    for c in range(1, depth):
        total = total + order[c]
    total_out[...] = total.astype(total_out.dtype)


def columns_kernel(parents, upper_pattern, lower_pattern, panel, own, front, back, *refs):
    got, (upper_out, lower_out) = refs[:-2], refs[-2:]
    uppers, lowers, middle = upper_out.shape[0], lower_out.shape[0], front.shape[0]

    def product(k):
        value = own[k] + (front[k] if k < middle else back[k - middle])
        for piece in got:
            value = value + piece[k].astype(F32)
        return value

    for k in range(uppers):
        upper_out[k] = (-product(k) * upper_pattern[k].astype(F32)).astype(jnp.bfloat16)
    extensions = [
        jnp.dot(upper_out[parents[m]], panel[m], preferred_element_type=F32) for m in range(lowers)
    ]
    for m in range(lowers):
        value = -(product(uppers + m) + extensions[m]) * lower_pattern[m].astype(F32)
        lower_out[m] = value.astype(jnp.bfloat16)


def split(wide):
    high = wide.astype(jnp.bfloat16)
    return high, (wide - high.astype(F32)).astype(jnp.bfloat16)


def blocks_kernel(
    width,
    parents,
    near,
    far,
    upper_diagonal,
    lower_diagonal,
    panel,
    panel_turned,
    upper_out,
    cross_out,
    lower_out,
    packed,
    halves,
):
    uppers, lowers = upper_out.shape[0], lower_out.shape[0]
    block = panel.shape[-1]
    chunk = near.shape[1]
    row = lax.axis_index("row")
    for m in range(width):
        place = pl.multiple_of((row ^ m) * chunk, chunk)
        packed[pl.ds(place, chunk)] = (far if m & 1 else near)[m // 2].astype(F32)
    base = (uppers + lowers + 1) // 2 * block
    squares = unpack(packed, uppers + lowers, block, base + lowers * block)
    for k in range(uppers):
        value = upper_diagonal[k] + squares[k]
        upper_out[k] = value
        halves[k, :block], halves[k, block:] = split(value)
    products = [
        jnp.dot(halves[parents[m]], panel[m], preferred_element_type=F32) for m in range(lowers)
    ]
    rights = []
    for m in range(lowers):
        forms = packed[base + m * block : base + (m + 1) * block]
        cross = forms - (products[m][:block] + products[m][block:])
        cross_out[m] = cross
        rights.append(jnp.concatenate([forms.astype(jnp.bfloat16), *split(cross)], axis=1))
    backs = [
        jnp.dot(panel_turned[m], rights[m], preferred_element_type=F32) for m in range(lowers)
    ]
    for m in range(lowers):
        value = backs[m]
        rest = value[:, block : 2 * block] + value[:, 2 * block :]
        lower_out[m] = lower_diagonal[m] + squares[uppers + m] - rest - value[:, :block].T


def gather_shifts(value, axis):
    size = lax.axis_size(axis)
    return [value] + [shift(value, axis, -o) for o in range(1, size)]


def pairs(size, offset):
    takers = range(size)
    if 2 * offset == size:
        takers = [c if c % 2 == 0 else c + offset for c in range(offset)]
    return [(c, (c + offset) % size) for c in takers]


def gather_pair(value, axis, offset):
    return lax.ppermute(value, axis, [(b, c) for c, b in pairs(lax.axis_size(axis), offset)])


def return_pair(value, axis, offset):
    return lax.ppermute(value, axis, pairs(lax.axis_size(axis), offset))


def halve(value, axis, bit, left):
    place = sorted(left, reverse=True).index(bit)
    value = value.reshape((2,) * len(left) + value.shape[-3:])
    away = lax.index_in_dim(value, 1, place, keepdims=False).astype(WIRE)
    keep = lax.index_in_dim(value, 0, place, keepdims=False)
    return keep, flip(away, axis, 1 << bit)


def gather_near(value, axis):
    masks = range(2, lax.axis_size(axis), 2)
    return [value] + [flip(value, axis, m) for m in masks]


def scatter_flips(value, axis):
    masks = range(2, lax.axis_size(axis), 2)
    return [flip(value[m // 2].astype(WIRE), axis, m) for m in masks]


def tie(*values):
    return lax.optimization_barrier(values)


def per_device(
    top_inverse,
    upper_panel,
    upper_pattern,
    upper_diagonal,
    lower_panel,
    lower_pattern,
    parents,
    parent_panel,
    lower_diagonal,
):
    uppers, block = upper_panel.shape[0], upper_panel.shape[-1]
    lowers = lower_panel.shape[0]
    total = uppers + lowers
    width, depth = lax.axis_size("row"), lax.axis_size("col")
    half = width // 2
    packed_n = (total + 1) // 2 * block + lowers * block + total // 2
    chunk = ceil_to(packed_n, 16 * width) // width
    bf16 = jnp.bfloat16
    upper_pattern, lower_pattern = upper_pattern.reshape(-1), lower_pattern.reshape(-1)

    (masked,) = call(
        mask_kernel,
        "mask",
        (upper_pattern, lower_pattern),
        (upper_panel.reshape(-1, block, block), lower_panel.reshape(-1, block, block)),
        [shape_of((total, block, block), bf16)],
        limit=60 << 20,
    )
    reach = depth // 2
    pieces = [gather_pair(masked, "col", o) for o in range(1, reach + 1)]
    (turned,) = call(
        turn_kernel,
        "turn",
        (),
        (masked, *pieces),
        [shape_of((total, block, (reach + 1) * block), bf16)],
    )
    (near,) = call(
        stack_kernel,
        "stack",
        (),
        (*gather_near(masked, "row"), turned),
        [shape_of((half, total, block, block), bf16)],
    )
    far = flip(near, "row", 1)
    top, top_turned, panel_turned = call(
        top_kernel,
        "top",
        (),
        (top_inverse[0, :, :, 0], parent_panel),
        [
            shape_of((2, (reach + 1) * block, half * block), bf16),
            shape_of((width * block, reach * block), bf16),
            shape_of(parent_panel.shape, bf16),
        ],
    )
    keep, away = call(
        partial_kernel,
        "partial",
        (),
        (top_turned, *pieces),
        [
            shape_of((half, total, block, block), F32),
            shape_of((half, total, block, block), WIRE),
        ],
    )
    columns_n = ceil_to(total, 2) // 2
    (start,) = call(
        first_kernel,
        "first",
        (),
        (top, near),
        [shape_of((columns_n, (reach + 1) * block, 2 * block), F32)],
    )
    own, *rest = call(
        functools.partial(second_kernel, uppers),
        "second",
        (parents,),
        (top, far, start, turned),
        [shape_of((total, block, block), F32)]
        + [shape_of((total, block, block), WIRE)] * reach
        + [shape_of((half, chunk, block), F32)] * 2,
        [
            shape_of((total, (reach + 1) * block, 2 * block), bf16),
            shape_of((total, block, block), F32),
            shape_of((width * chunk, block), F32),
        ],
    )
    returns, (sums_keep, sums_away) = rest[:-2], rest[-2:]

    other, across = tie(flip(sums_away, "row", 1), flip(away, "row", 1))
    sums = sums_keep + other
    pieces = scatter_flips(sums, "row")
    pieces[0], value = tie(pieces[0], keep + across.astype(F32))
    middle = total // 2
    bits = list(range(1, width.bit_length() - 1))
    sides = [value[:, :middle], value[:, middle:]]
    halves = [halve(side, "row", bit, bits) for side, bit in zip(sides, (bits[0], bits[-1]))]
    part = sums[0]
    for piece in pieces:
        part = part + piece.astype(F32)
    part = part.astype(WIRE)
    early = [return_pair(returns[o - 1], "col", o) for o in range(1, reach)]
    parts = gather_shifts(part, "col")
    tied = tie(*parts, *[got for _, got in halves], *early)
    early = tied[depth + 2 :]
    (part,) = call(
        line_kernel,
        "line",
        (),
        tied[:depth],
        [shape_of((chunk, block), WIRE)],
        [shape_of((depth, chunk, block), F32)],
    )
    sides = [keep + got.astype(F32) for (keep, _), got in zip(halves, tied[depth : depth + 2])]
    part, last, *sides = tie(part, returns[-1], *sides)
    nears = gather_near(part, "row")
    near = jnp.stack(nears)
    far = flip(near, "row", 1)
    got = [*early, return_pair(last, "col", reach)]
    front, back = sides
    for i in range(1, len(bits)):
        keep, across = halve(front, "row", bits[i], bits[i:])
        front = keep + across.astype(F32)
        keep, across = halve(back, "row", bits[-1 - i], bits[: len(bits) - i])
        back = keep + across.astype(F32)
    front, back = [side.reshape(-1, block, block) for side in (front, back)]

    upper_blocks, lower_cross, lower_blocks = call(
        functools.partial(blocks_kernel, width),
        "blocks",
        (parents,),
        (near, far, upper_diagonal, lower_diagonal, parent_panel, panel_turned),
        [
            shape_of((uppers, block, block), F32),
            shape_of((lowers, block, block), F32),
            shape_of((lowers, block, block), F32),
        ],
        [shape_of((width * chunk, block), F32), shape_of((uppers, 2 * block, block), bf16)],
    )
    upper_blocks, *got = tie(upper_blocks, *got)
    upper_columns, lower_columns = call(
        columns_kernel,
        "columns",
        (parents, upper_pattern, lower_pattern),
        (parent_panel, own, front, back, *got),
        [
            shape_of((uppers, block, block), bf16),
            shape_of((lowers, block, block), bf16),
        ],
    )
    return (
        upper_columns[:, None, None],
        upper_blocks,
        lower_columns[:, None, None],
        lower_cross,
        lower_blocks,
    )


def solution(mesh):
    return jax.shard_map(
        per_device,
        mesh=mesh,
        in_specs=(
            P("row", None, None, "col", None, None),
            P(None, "row", "col", None, None),
            P(None, "row", "col"),
            P(),
            P(None, "row", "col", None, None),
            P(None, "row", "col"),
            P(),
            P(),
            P(),
        ),
        out_specs=(
            P(None, "row", "col", None, None),
            P(),
            P(None, "row", "col", None, None),
            P(),
            P(),
        ),
        check_vma=False,
    )
```

```python
import functools

import jax
import jax.numpy as jnp
import numpy as np
from jax import lax
from jax.experimental import pallas as pl
from jax.experimental.pallas import tpu as pltpu
from jax.sharding import PartitionSpec as P

F32 = jnp.float32
WIRE = jnp.bfloat16
VMEM = pl.BlockSpec(memory_space=pltpu.VMEM)
SMEM = pl.BlockSpec(memory_space=pltpu.SMEM)


def shape_of(dims, kind):
    return jax.ShapeDtypeStruct(dims, kind)


def flip(value, axis, mask):
    size = lax.axis_size(axis)
    return lax.ppermute(value, axis, [(i, i ^ mask) for i in range(size)])


def shift(value, axis, step):
    size = lax.axis_size(axis)
    return lax.ppermute(value, axis, [(i, (i + step) % size) for i in range(size)])


def ceil_to(value, step):
    return -(-value // step) * step


def params(refs, limit):
    size = sum(int(np.prod(r.shape)) * np.dtype(r.dtype).itemsize for r in refs)
    return pltpu.CompilerParams(vmem_limit_bytes=limit or ceil_to(size * 5 // 4, 1 << 20) + (4 << 20))


def call(kernel, name, scalars, arrays, outs, scratch=(), limit=0, cost=0):
    return pl.pallas_call(
        kernel,
        out_shape=outs,
        in_specs=[SMEM] * len(scalars) + [VMEM] * len(arrays),
        out_specs=[VMEM] * len(outs),
        scratch_shapes=[pltpu.VMEM(r.shape, r.dtype) for r in scratch],
        compiler_params=params([*arrays, *outs, *scratch], limit),
        cost_estimate=pl.CostEstimate(flops=cost, bytes_accessed=cost, transcendentals=0) if cost else None,
        name=name,
    )(*scalars, *arrays)


def stack_kernel(*refs):
    for i, piece in enumerate(refs[:-3]):
        refs[-1][i] = piece[...]


def mask_kernel(upper_pattern, lower_pattern, upper_panel, lower_panel, masked):
    uppers, lowers = upper_panel.shape[0], lower_panel.shape[0]
    for k in range(uppers):
        masked[k] = upper_panel[k] * upper_pattern[k].astype(F32).astype(jnp.bfloat16)
    for m in range(lowers):
        masked[uppers + m] = lower_panel[m] * lower_pattern[m].astype(F32).astype(jnp.bfloat16)


def turn_kernel(*refs):
    pieces, turned = refs[:-1], refs[-1]
    total, block = pieces[0].shape[0], pieces[0].shape[-1]
    for k in range(total):
        for o, piece in enumerate(pieces):
            turned[k, :, o * block : (o + 1) * block] = piece[k].T


def top_kernel(top, panel, out, out_turned, panel_turned):
    depth, width, block, _ = top.shape
    row, col = lax.axis_index("row"), lax.axis_index("col")
    half = width // 2

    def tile(o, i):
        return top[lax.rem(col + o, depth), row ^ (2 * (i % half) + i // half)]

    for o in range(out.shape[1] // block):
        rows = slice(o * block, (o + 1) * block)
        for i in range(width):
            out[i // half, rows, (i % half) * block : (i % half + 1) * block] = tile(o, i)

    for o in range(1, out.shape[1] // block):
        lanes = slice((o - 1) * block, o * block)
        for i in range(width):
            out_turned[i * block : (i + 1) * block, lanes] = tile(o, i).T
    for m in range(panel.shape[0]):
        panel_turned[m] = panel[m].T


def partial_kernel(top, *refs):
    pieces, (keep, away) = refs[:-2], refs[-2:]
    half, total, block, _ = keep.shape
    for first in range(0, total, 2):
        second = min(first + 1, total - 1)
        right = [jnp.concatenate([p[first], p[second]], axis=1) for p in pieces]
        value = jnp.dot(top[...], jnp.concatenate(right), preferred_element_type=F32)
        for lane, k in enumerate(range(first, second + 1)):
            for i in range(half):
                lanes = slice(lane * block, (lane + 1) * block)
                keep[i, k] = value[i * block : (i + 1) * block, lanes]
                far = value[(half + i) * block : (half + i + 1) * block, lanes]
                away[i, k] = far.astype(away.dtype)


def dot_pair(left, own, others, first, second):
    pieces = [own, *[others.at[i] for i in range(others.shape[0])]]
    right = [jnp.concatenate([piece[first], piece[second]], axis=1) for piece in pieces]
    return jnp.dot(left, jnp.concatenate(right), preferred_element_type=F32)


def first_kernel(top, own, near, out):
    total = own.shape[0]
    for first in range(0, total, 2):
        out[first // 2] = dot_pair(top[0], own, near, first, min(first + 1, total - 1))


def triangle(block):
    rows = lax.broadcasted_iota(jnp.int32, (block, block), 0)
    lanes = lax.broadcasted_iota(jnp.int32, (block, block), 1)
    return rows < lanes, rows == lanes


def pack(squares, packed, start):
    total, block = len(squares), squares[0].shape[0]
    above, diagonal = triangle(block)
    for p in range(total // 2):
        first, second = [squares[k] + squares[k].T for k in (2 * p, 2 * p + 1)]
        packed[p * block : (p + 1) * block] = jnp.where(above, first, second)
        row = jnp.sum(jnp.where(diagonal, first, 0.0), axis=0, keepdims=True)
        packed[start + p : start + p + 1] = row
    if total % 2:
        packed[(total // 2) * block : (total // 2 + 1) * block] = squares[total - 1] + squares[total - 1].T


def unpack(packed, total, block, start):
    above, diagonal = triangle(block)
    squares = []
    for p in range(total // 2):
        value = packed[p * block : (p + 1) * block]
        turned = value.T
        row = packed[start + p : start + p + 1]
        squares.append(jnp.where(above, value, jnp.where(diagonal, row, turned)))
        squares.append(jnp.where(above, turned, value))
    if total % 2:
        squares.append(packed[(total // 2) * block : (total // 2 + 1) * block])
    return squares


def second_kernel(uppers, parents, top, far_own, far, start, turned, *refs):
    own, returns, (sums_keep, sums_away, both, packed) = refs[0], refs[1:-4], refs[-4:]
    total, block, reach = turned.shape
    lowers = total - uppers
    half, chunk, _ = sums_keep.shape
    row = lax.axis_index("row")

    for first in range(0, total, 2):
        second = min(first + 1, total - 1)
        value = start[first // 2] + dot_pair(top[1], far_own, far, first, second)
        for lane, k in enumerate(range(first, second + 1)):
            part = value[:, lane * block : (lane + 1) * block]
            own[k] = part[:block]
            for o, out in enumerate(returns):
                out[k] = part[(o + 1) * block : (o + 2) * block].astype(WIRE)
            part = jnp.concatenate([0.5 * part[:block], part[block:reach]])
            high = part.astype(jnp.bfloat16)
            both[k, :, :block] = high
            both[k, :, block:] = (part - high.astype(F32)).astype(jnp.bfloat16)

    def fold(rows, k):
        value = jnp.dot(rows, both[k], preferred_element_type=F32)
        return value[:, :block] + value[:, block:]

    base = (total + 1) // 2 * block
    squares = [fold(turned[k], k) for k in range(uppers)]
    crossed = [fold(turned[uppers + m], parents[m]) for m in range(lowers)]
    for m in range(lowers):
        rows = jnp.concatenate([turned[uppers + m], turned[parents[m]]], axis=0)
        value = fold(rows, uppers + m)
        squares.append(value[:block])
        place = base + m * block
        packed[place : place + block] = value[block:] + crossed[m].T
    end = base + lowers * block
    packed[end:] = jnp.zeros((packed.shape[0] - end, block), F32)
    pack(squares, packed, end)
    for m in range(2 * half):
        place = pl.multiple_of((row ^ m) * chunk, chunk)
        (sums_away if m & 1 else sums_keep)[m // 2] = packed[pl.ds(place, chunk)]


def line_kernel(*refs):
    parts, (total_out, order) = refs[:-2], refs[-2:]
    depth, col = len(parts), lax.axis_index("col")
    for o in range(depth):
        order[lax.rem(col + o, depth)] = parts[o][...].astype(F32)
    total = order[0]
    for c in range(1, depth):
        total = total + order[c]
    total_out[...] = total.astype(total_out.dtype)


def columns_kernel(parents, upper_pattern, lower_pattern, panel, own, front, back, *refs):
    got, (upper_out, lower_out) = refs[:-2], refs[-2:]
    uppers, lowers, middle = upper_out.shape[0], lower_out.shape[0], front.shape[0]

    def product(k):
        value = own[k] + (front[k] if k < middle else back[k - middle])
        for piece in got:
            value = value + piece[k].astype(F32)
        return value

    for k in range(uppers):
        upper_out[k] = (-product(k) * upper_pattern[k].astype(F32)).astype(jnp.bfloat16)
    extensions = [
        jnp.dot(upper_out[parents[m]], panel[m], preferred_element_type=F32) for m in range(lowers)
    ]
    for m in range(lowers):
        value = -(product(uppers + m) + extensions[m]) * lower_pattern[m].astype(F32)
        lower_out[m] = value.astype(jnp.bfloat16)


def split(wide):
    high = wide.astype(jnp.bfloat16)
    return high, (wide - high.astype(F32)).astype(jnp.bfloat16)


def blocks_kernel(
    width,
    parents,
    near,
    far,
    upper_diagonal,
    lower_diagonal,
    panel,
    panel_turned,
    upper_out,
    cross_out,
    lower_out,
    packed,
    halves,
):
    uppers, lowers = upper_out.shape[0], lower_out.shape[0]
    block = panel.shape[-1]
    chunk = near.shape[1]
    row = lax.axis_index("row")
    for m in range(width):
        place = pl.multiple_of((row ^ m) * chunk, chunk)
        packed[pl.ds(place, chunk)] = (far if m & 1 else near)[m // 2].astype(F32)
    base = (uppers + lowers + 1) // 2 * block
    squares = unpack(packed, uppers + lowers, block, base + lowers * block)
    for k in range(uppers):
        value = upper_diagonal[k] + squares[k]
        upper_out[k] = value
        halves[k, :block], halves[k, block:] = split(value)
    products = [
        jnp.dot(halves[parents[m]], panel[m], preferred_element_type=F32) for m in range(lowers)
    ]
    rights = []
    for m in range(lowers):
        forms = packed[base + m * block : base + (m + 1) * block]
        cross = forms - (products[m][:block] + products[m][block:])
        cross_out[m] = cross
        rights.append(jnp.concatenate([forms.astype(jnp.bfloat16), *split(cross)], axis=1))
    backs = [
        jnp.dot(panel_turned[m], rights[m], preferred_element_type=F32) for m in range(lowers)
    ]
    for m in range(lowers):
        value = backs[m]
        rest = value[:, block : 2 * block] + value[:, 2 * block :]
        lower_out[m] = lower_diagonal[m] + squares[uppers + m] - rest - value[:, :block].T


def gather_shifts(value, axis):
    size = lax.axis_size(axis)
    return [value] + [shift(value, axis, -o) for o in range(1, size)]


def pairs(size, offset):
    takers = range(size)
    if 2 * offset == size:
        takers = [c if c % 2 == 0 else c + offset for c in range(offset)]
    return [(c, (c + offset) % size) for c in takers]


def gather_pair(value, axis, offset):
    return lax.ppermute(value, axis, [(b, c) for c, b in pairs(lax.axis_size(axis), offset)])


def return_pair(value, axis, offset):
    return lax.ppermute(value, axis, pairs(lax.axis_size(axis), offset))


def halve(value, axis, bit, left):
    place = sorted(left, reverse=True).index(bit)
    value = value.reshape((2,) * len(left) + value.shape[-3:])
    away = lax.index_in_dim(value, 1, place, keepdims=False).astype(WIRE)
    keep = lax.index_in_dim(value, 0, place, keepdims=False)
    return keep, flip(away, axis, 1 << bit)


def gather_near(value, axis):
    masks = range(2, lax.axis_size(axis), 2)
    return [value] + [flip(value, axis, m) for m in masks]


def scatter_flips(value, axis):
    masks = range(2, lax.axis_size(axis), 2)
    return [flip(value[m // 2].astype(WIRE), axis, m) for m in masks]


def tie(*values):
    return lax.optimization_barrier(values)


def per_device(
    top_inverse,
    upper_panel,
    upper_pattern,
    upper_diagonal,
    lower_panel,
    lower_pattern,
    parents,
    parent_panel,
    lower_diagonal,
):
    uppers, block = upper_panel.shape[0], upper_panel.shape[-1]
    lowers = lower_panel.shape[0]
    total = uppers + lowers
    width, depth = lax.axis_size("row"), lax.axis_size("col")
    half = width // 2
    packed_n = (total + 1) // 2 * block + lowers * block + total // 2
    chunk = ceil_to(packed_n, 16 * width) // width
    bf16 = jnp.bfloat16
    upper_pattern, lower_pattern = upper_pattern.reshape(-1), lower_pattern.reshape(-1)

    (masked,) = call(
        mask_kernel,
        "mask",
        (upper_pattern, lower_pattern),
        (upper_panel.reshape(-1, block, block), lower_panel.reshape(-1, block, block)),
        [shape_of((total, block, block), bf16)],
        limit=60 << 20,
    )
    reach = depth // 2
    pieces = [gather_pair(masked, "col", o) for o in range(1, reach + 1)]
    (turned,) = call(
        turn_kernel,
        "turn",
        (),
        (masked, *pieces),
        [shape_of((total, block, (reach + 1) * block), bf16)],
    )
    far_own = flip(masked, "row", 1)
    (near,) = call(
        stack_kernel,
        "stack",
        (),
        (*gather_near(masked, "row")[1:], turned, far_own),
        [shape_of((half - 1, total, block, block), bf16)],
    )
    far = flip(near, "row", 1)
    top, top_turned, panel_turned = call(
        top_kernel,
        "top",
        (),
        (top_inverse[0, :, :, 0], parent_panel),
        [
            shape_of((2, (reach + 1) * block, half * block), bf16),
            shape_of((width * block, reach * block), bf16),
            shape_of(parent_panel.shape, bf16),
        ],
    )
    keep, away = call(
        partial_kernel,
        "partial",
        (),
        (top_turned, *pieces),
        [
            shape_of((half, total, block, block), F32),
            shape_of((half, total, block, block), WIRE),
        ],
    )
    columns_n = ceil_to(total, 2) // 2
    (start,) = call(
        first_kernel,
        "first",
        (),
        (top, masked, near),
        [shape_of((columns_n, (reach + 1) * block, 2 * block), F32)],
    )
    own, *rest = call(
        functools.partial(second_kernel, uppers),
        "second",
        (parents,),
        (top, far_own, far, start, turned),
        [shape_of((total, block, block), F32)]
        + [shape_of((total, block, block), WIRE)] * reach
        + [shape_of((half, chunk, block), F32)] * 2,
        [
            shape_of((total, (reach + 1) * block, 2 * block), bf16),
            shape_of((width * chunk, block), F32),
        ],
    )
    returns, (sums_keep, sums_away) = rest[:-2], rest[-2:]

    other, across = tie(flip(sums_away, "row", 1), flip(away, "row", 1))
    sums = sums_keep + other
    pieces = scatter_flips(sums, "row")
    pieces[0], value = tie(pieces[0], keep + across.astype(F32))
    middle = total // 2
    bits = list(range(1, width.bit_length() - 1))
    sides = [value[:, :middle], value[:, middle:]]
    halves = [halve(side, "row", bit, bits) for side, bit in zip(sides, (bits[0], bits[-1]))]
    part = sums[0]
    for piece in pieces:
        part = part + piece.astype(F32)
    part = part.astype(WIRE)
    early = [return_pair(returns[o - 1], "col", o) for o in range(1, reach)]
    parts = gather_shifts(part, "col")
    tied = tie(*parts, *[got for _, got in halves], *early)
    early = tied[depth + 2 :]
    (part,) = call(
        line_kernel,
        "line",
        (),
        tied[:depth],
        [shape_of((chunk, block), WIRE)],
        [shape_of((depth, chunk, block), F32)],
    )
    sides = [keep + got.astype(F32) for (keep, _), got in zip(halves, tied[depth : depth + 2])]
    part, last, *sides = tie(part, returns[-1], *sides)
    nears = gather_near(part, "row")
    near = jnp.stack(nears)
    far = flip(near, "row", 1)
    got = [*early, return_pair(last, "col", reach)]
    front, back = sides
    for i in range(1, len(bits)):
        keep, across = halve(front, "row", bits[i], bits[i:])
        front = keep + across.astype(F32)
        keep, across = halve(back, "row", bits[-1 - i], bits[: len(bits) - i])
        back = keep + across.astype(F32)
    front, back = [side.reshape(-1, block, block) for side in (front, back)]

    upper_blocks, lower_cross, lower_blocks = call(
        functools.partial(blocks_kernel, width),
        "blocks",
        (parents,),
        (near, far, upper_diagonal, lower_diagonal, parent_panel, panel_turned),
        [
            shape_of((uppers, block, block), F32),
            shape_of((lowers, block, block), F32),
            shape_of((lowers, block, block), F32),
        ],
        [shape_of((width * chunk, block), F32), shape_of((uppers, 2 * block, block), bf16)],
    )
    upper_blocks, *got = tie(upper_blocks, *got)
    upper_columns, lower_columns = call(
        columns_kernel,
        "columns",
        (parents, upper_pattern, lower_pattern),
        (parent_panel, own, front, back, *got),
        [
            shape_of((uppers, block, block), bf16),
            shape_of((lowers, block, block), bf16),
        ],
    )
    return (
        upper_columns[:, None, None],
        upper_blocks,
        lower_columns[:, None, None],
        lower_cross,
        lower_blocks,
    )


def solution(mesh):
    return jax.shard_map(
        per_device,
        mesh=mesh,
        in_specs=(
            P("row", None, None, "col", None, None),
            P(None, "row", "col", None, None),
            P(None, "row", "col"),
            P(),
            P(None, "row", "col", None, None),
            P(None, "row", "col"),
            P(),
            P(),
            P(),
        ),
        out_specs=(
            P(None, "row", "col", None, None),
            P(),
            P(None, "row", "col", None, None),
            P(),
            P(),
        ),
        check_vma=False,
    )
```

```python
import functools

import jax
import jax.numpy as jnp
import numpy as np
from jax import lax
from jax.experimental import pallas as pl
from jax.experimental.pallas import tpu as pltpu
from jax.sharding import PartitionSpec as P

F32 = jnp.float32
WIRE = jnp.bfloat16
VMEM = pl.BlockSpec(memory_space=pltpu.VMEM)
SMEM = pl.BlockSpec(memory_space=pltpu.SMEM)


def shape_of(dims, kind):
    return jax.ShapeDtypeStruct(dims, kind)


def flip(value, axis, mask):
    size = lax.axis_size(axis)
    return lax.ppermute(value, axis, [(i, i ^ mask) for i in range(size)])


def shift(value, axis, step):
    size = lax.axis_size(axis)
    return lax.ppermute(value, axis, [(i, (i + step) % size) for i in range(size)])


def ceil_to(value, step):
    return -(-value // step) * step


def params(refs, limit):
    size = sum(int(np.prod(r.shape)) * np.dtype(r.dtype).itemsize for r in refs)
    return pltpu.CompilerParams(vmem_limit_bytes=limit or ceil_to(size * 5 // 4, 1 << 20) + (4 << 20))


def call(kernel, name, scalars, arrays, outs, scratch=(), limit=0, cost=0):
    return pl.pallas_call(
        kernel,
        out_shape=outs,
        in_specs=[SMEM] * len(scalars) + [VMEM] * len(arrays),
        out_specs=[VMEM] * len(outs),
        scratch_shapes=[pltpu.VMEM(r.shape, r.dtype) for r in scratch],
        compiler_params=params([*arrays, *outs, *scratch], limit),
        cost_estimate=pl.CostEstimate(flops=cost, bytes_accessed=cost, transcendentals=0) if cost else None,
        name=name,
    )(*scalars, *arrays)


def stack_kernel(*refs):
    for i, piece in enumerate(refs[:-3]):
        refs[-1][i] = piece[...]


def mask_kernel(upper_pattern, lower_pattern, upper_panel, lower_panel, masked):
    uppers, lowers = upper_panel.shape[0], lower_panel.shape[0]
    for k in range(uppers):
        masked[k] = upper_panel[k] * upper_pattern[k].astype(F32).astype(jnp.bfloat16)
    for m in range(lowers):
        masked[uppers + m] = lower_panel[m] * lower_pattern[m].astype(F32).astype(jnp.bfloat16)


def turn_kernel(*refs):
    pieces, turned = refs[:-1], refs[-1]
    total, block = pieces[0].shape[0], pieces[0].shape[-1]
    for k in range(total):
        for o, piece in enumerate(pieces):
            turned[k, :, o * block : (o + 1) * block] = piece[k].T


def top_kernel(top, panel, out, out_turned, panel_turned):
    depth, width, block, _ = top.shape
    row, col = lax.axis_index("row"), lax.axis_index("col")
    half = width // 2

    def tile(o, i):
        return top[lax.rem(col + o, depth), row ^ (2 * (i % half) + i // half)]

    for o in range(out.shape[1] // block):
        rows = slice(o * block, (o + 1) * block)
        for i in range(width):
            out[i // half, rows, (i % half) * block : (i % half + 1) * block] = tile(o, i)

    for o in range(1, out.shape[1] // block):
        lanes = slice((o - 1) * block, o * block)
        for i in range(width):
            out_turned[i * block : (i + 1) * block, lanes] = tile(o, i).T
    for m in range(panel.shape[0]):
        panel_turned[m] = panel[m].T


def partial_kernel(top, *refs):
    pieces, (keep, away) = refs[:-2], refs[-2:]
    half, total, block, _ = keep.shape
    for first in range(0, total, 2):
        second = min(first + 1, total - 1)
        right = [jnp.concatenate([p[first], p[second]], axis=1) for p in pieces]
        value = jnp.dot(top[...], jnp.concatenate(right), preferred_element_type=F32)
        for lane, k in enumerate(range(first, second + 1)):
            for i in range(half):
                lanes = slice(lane * block, (lane + 1) * block)
                keep[i, k] = value[i * block : (i + 1) * block, lanes]
                far = value[(half + i) * block : (half + i + 1) * block, lanes]
                away[i, k] = far.astype(away.dtype)


def dot_pair(left, own, others, first, second):
    pieces = [own, *[others.at[i] for i in range(others.shape[0])]]
    right = [jnp.concatenate([piece[first], piece[second]], axis=1) for piece in pieces]
    return jnp.dot(left, jnp.concatenate(right), preferred_element_type=F32)


def first_kernel(top, own, near, out):
    total = own.shape[0]
    for first in range(0, total, 2):
        out[first // 2] = dot_pair(top[0], own, near, first, min(first + 1, total - 1))


def triangle(block):
    rows = lax.broadcasted_iota(jnp.int32, (block, block), 0)
    lanes = lax.broadcasted_iota(jnp.int32, (block, block), 1)
    return rows < lanes, rows == lanes


def pack(squares, packed, start):
    total, block = len(squares), squares[0].shape[0]
    above, diagonal = triangle(block)
    for p in range(total // 2):
        first, second = [squares[k] + squares[k].T for k in (2 * p, 2 * p + 1)]
        packed[p * block : (p + 1) * block] = jnp.where(above, first, second)
        row = jnp.sum(jnp.where(diagonal, first, 0.0), axis=0, keepdims=True)
        packed[start + p : start + p + 1] = row
    if total % 2:
        packed[(total // 2) * block : (total // 2 + 1) * block] = squares[total - 1] + squares[total - 1].T


def unpack(packed, total, block, start):
    above, diagonal = triangle(block)
    squares = []
    for p in range(total // 2):
        value = packed[p * block : (p + 1) * block]
        turned = value.T
        row = packed[start + p : start + p + 1]
        squares.append(jnp.where(above, value, jnp.where(diagonal, row, turned)))
        squares.append(jnp.where(above, turned, value))
    if total % 2:
        squares.append(packed[(total // 2) * block : (total // 2 + 1) * block])
    return squares


def second_kernel(uppers, parents, top, far_own, far, start, turned, *refs):
    own, returns, (sums_keep, sums_away, both, packed) = refs[0], refs[1:-4], refs[-4:]
    total, block, reach = turned.shape
    lowers = total - uppers
    half, chunk, _ = sums_keep.shape
    row = lax.axis_index("row")

    for first in range(0, total, 2):
        second = min(first + 1, total - 1)
        value = start[first // 2] + dot_pair(top[1], far_own, far, first, second)
        for lane, k in enumerate(range(first, second + 1)):
            part = value[:, lane * block : (lane + 1) * block]
            own[k] = part[:block]
            for o, out in enumerate(returns):
                out[k] = part[(o + 1) * block : (o + 2) * block].astype(WIRE)
            part = jnp.concatenate([0.5 * part[:block], part[block:reach]])
            high = part.astype(jnp.bfloat16)
            both[k, :, :block] = high
            both[k, :, block:] = (part - high.astype(F32)).astype(jnp.bfloat16)

    def fold(rows, k):
        value = jnp.dot(rows, both[k], preferred_element_type=F32)
        return value[:, :block] + value[:, block:]

    base = (total + 1) // 2 * block
    squares = [fold(turned[k], k) for k in range(uppers)]
    crossed = [fold(turned[uppers + m], parents[m]) for m in range(lowers)]
    for m in range(lowers):
        rows = jnp.concatenate([turned[uppers + m], turned[parents[m]]], axis=0)
        value = fold(rows, uppers + m)
        squares.append(value[:block])
        place = base + m * block
        packed[place : place + block] = value[block:] + crossed[m].T
    end = base + lowers * block
    packed[end:] = jnp.zeros((packed.shape[0] - end, block), F32)
    pack(squares, packed, end)
    for m in range(2 * half):
        place = pl.multiple_of((row ^ m) * chunk, chunk)
        (sums_away if m & 1 else sums_keep)[m // 2] = packed[pl.ds(place, chunk)]


def line_kernel(*refs):
    parts, (total_out, order) = refs[:-2], refs[-2:]
    depth, col = len(parts), lax.axis_index("col")
    for o in range(depth):
        order[lax.rem(col + o, depth)] = parts[o][...].astype(F32)
    total = order[0]
    for c in range(1, depth):
        total = total + order[c]
    total_out[...] = total.astype(total_out.dtype)


def columns_kernel(parents, upper_pattern, lower_pattern, panel, own, front, back, *refs):
    got, (upper_out, lower_out) = refs[:-2], refs[-2:]
    uppers, lowers, middle = upper_out.shape[0], lower_out.shape[0], front.shape[0]

    def product(k):
        value = own[k] + (front[k] if k < middle else back[k - middle])
        for piece in got:
            value = value + piece[k].astype(F32)
        return value

    for k in range(uppers):
        upper_out[k] = (-product(k) * upper_pattern[k].astype(F32)).astype(jnp.bfloat16)
    extensions = [
        jnp.dot(upper_out[parents[m]], panel[m], preferred_element_type=F32) for m in range(lowers)
    ]
    for m in range(lowers):
        value = -(product(uppers + m) + extensions[m]) * lower_pattern[m].astype(F32)
        lower_out[m] = value.astype(jnp.bfloat16)


def split(wide):
    high = wide.astype(jnp.bfloat16)
    return high, (wide - high.astype(F32)).astype(jnp.bfloat16)


def blocks_kernel(
    width,
    parents,
    near,
    far,
    upper_diagonal,
    lower_diagonal,
    panel,
    panel_turned,
    upper_out,
    cross_out,
    lower_out,
    packed,
    halves,
):
    uppers, lowers = upper_out.shape[0], lower_out.shape[0]
    block = panel.shape[-1]
    chunk = near.shape[1]
    row = lax.axis_index("row")
    for m in range(width):
        place = pl.multiple_of((row ^ m) * chunk, chunk)
        packed[pl.ds(place, chunk)] = (far if m & 1 else near)[m // 2].astype(F32)
    base = (uppers + lowers + 1) // 2 * block
    squares = unpack(packed, uppers + lowers, block, base + lowers * block)
    for k in range(uppers):
        value = upper_diagonal[k] + squares[k]
        upper_out[k] = value
        halves[k, :block], halves[k, block:] = split(value)
    products = [
        jnp.dot(halves[parents[m]], panel[m], preferred_element_type=F32) for m in range(lowers)
    ]
    rights = []
    for m in range(lowers):
        forms = packed[base + m * block : base + (m + 1) * block]
        cross = forms - (products[m][:block] + products[m][block:])
        cross_out[m] = cross
        rights.append(jnp.concatenate([forms.astype(jnp.bfloat16), *split(cross)], axis=1))
    backs = [
        jnp.dot(panel_turned[m], rights[m], preferred_element_type=F32) for m in range(lowers)
    ]
    for m in range(lowers):
        value = backs[m]
        rest = value[:, block : 2 * block] + value[:, 2 * block :]
        lower_out[m] = lower_diagonal[m] + squares[uppers + m] - rest - value[:, :block].T


def gather_shifts(value, axis):
    size = lax.axis_size(axis)
    return [value] + [shift(value, axis, -o) for o in range(1, size)]


def pairs(size, offset):
    takers = range(size)
    if 2 * offset == size:
        takers = [c if c % 2 == 0 else c + offset for c in range(offset)]
    return [(c, (c + offset) % size) for c in takers]


def gather_pair(value, axis, offset):
    return lax.ppermute(value, axis, [(b, c) for c, b in pairs(lax.axis_size(axis), offset)])


def return_pair(value, axis, offset):
    return lax.ppermute(value, axis, pairs(lax.axis_size(axis), offset))


def halve(value, axis, bit, left):
    place = sorted(left, reverse=True).index(bit)
    value = value.reshape((2,) * len(left) + value.shape[-3:])
    away = lax.index_in_dim(value, 1, place, keepdims=False).astype(WIRE)
    keep = lax.index_in_dim(value, 0, place, keepdims=False)
    return keep, flip(away, axis, 1 << bit)


def gather_near(value, axis):
    masks = range(2, lax.axis_size(axis), 2)
    return [value] + [flip(value, axis, m) for m in masks]


def scatter_flips(value, axis):
    masks = range(2, lax.axis_size(axis), 2)
    return [flip(value[m // 2].astype(WIRE), axis, m) for m in masks]


def tie(*values):
    return lax.optimization_barrier(values)


def per_device(
    top_inverse,
    upper_panel,
    upper_pattern,
    upper_diagonal,
    lower_panel,
    lower_pattern,
    parents,
    parent_panel,
    lower_diagonal,
):
    uppers, block = upper_panel.shape[0], upper_panel.shape[-1]
    lowers = lower_panel.shape[0]
    total = uppers + lowers
    width, depth = lax.axis_size("row"), lax.axis_size("col")
    half = width // 2
    packed_n = (total + 1) // 2 * block + lowers * block + total // 2
    chunk = ceil_to(packed_n, 16 * width) // width
    bf16 = jnp.bfloat16
    upper_pattern, lower_pattern = upper_pattern.reshape(-1), lower_pattern.reshape(-1)

    (masked,) = call(
        mask_kernel,
        "mask",
        (upper_pattern, lower_pattern),
        (upper_panel.reshape(-1, block, block), lower_panel.reshape(-1, block, block)),
        [shape_of((total, block, block), bf16)],
        limit=60 << 20,
    )
    reach = depth // 2
    pieces = [gather_pair(masked, "col", o) for o in range(1, reach + 1)]
    (turned,) = call(
        turn_kernel,
        "turn",
        (),
        (masked, *pieces),
        [shape_of((total, block, (reach + 1) * block), bf16)],
    )
    far_own = flip(masked, "row", 1)
    (near,) = call(
        stack_kernel,
        "stack",
        (),
        (*gather_near(masked, "row")[1:], turned, far_own),
        [shape_of((half - 1, total, block, block), bf16)],
    )
    far = flip(near, "row", 1)
    top, top_turned, panel_turned = call(
        top_kernel,
        "top",
        (),
        (top_inverse[0, :, :, 0], parent_panel),
        [
            shape_of((2, (reach + 1) * block, half * block), bf16),
            shape_of((width * block, reach * block), bf16),
            shape_of(parent_panel.shape, bf16),
        ],
    )
    keep, away = call(
        partial_kernel,
        "partial",
        (),
        (top_turned, *pieces),
        [
            shape_of((half, total, block, block), F32),
            shape_of((half, total, block, block), WIRE),
        ],
    )
    columns_n = ceil_to(total, 2) // 2
    (start,) = call(
        first_kernel,
        "first",
        (),
        (top, masked, near),
        [shape_of((columns_n, (reach + 1) * block, 2 * block), F32)],
    )
    own, *rest = call(
        functools.partial(second_kernel, uppers),
        "second",
        (parents,),
        (top, far_own, far, start, turned),
        [shape_of((total, block, block), F32)]
        + [shape_of((total, block, block), WIRE)] * reach
        + [shape_of((half, chunk, block), F32)] * 2,
        [
            shape_of((total, (reach + 1) * block, 2 * block), bf16),
            shape_of((width * chunk, block), F32),
        ],
    )
    returns, (sums_keep, sums_away) = rest[:-2], rest[-2:]

    other, across = tie(flip(sums_away, "row", 1), flip(away, "row", 1))
    sums = sums_keep + other
    pieces = scatter_flips(sums, "row")
    pieces[0], value = tie(pieces[0], keep + across.astype(F32))
    middle = total // 2
    bits = list(range(1, width.bit_length() - 1))
    sides = [value[:, :middle], value[:, middle:]]
    halves = [halve(side, "row", bit, bits) for side, bit in zip(sides, (bits[0], bits[-1]))]
    part = sums[0]
    for piece in pieces:
        part = part + piece.astype(F32)
    part = part.astype(WIRE)
    early = [return_pair(returns[o - 1], "col", o) for o in range(2, reach + 1)]
    parts = gather_shifts(part, "col")
    tied = tie(*parts, *[got for _, got in halves], *early)
    early = tied[depth + 2 :]
    (part,) = call(
        line_kernel,
        "line",
        (),
        tied[:depth],
        [shape_of((chunk, block), WIRE)],
        [shape_of((depth, chunk, block), F32)],
    )
    sides = [keep + got.astype(F32) for (keep, _), got in zip(halves, tied[depth : depth + 2])]
    part, last, *sides = tie(part, returns[0], *sides)
    nears = gather_near(part, "row")
    near = jnp.stack(nears)
    far = flip(near, "row", 1)
    got = [*early, return_pair(last, "col", 1)]
    front, back = sides
    for i in range(1, len(bits)):
        keep, across = halve(front, "row", bits[i], bits[i:])
        front = keep + across.astype(F32)
        keep, across = halve(back, "row", bits[-1 - i], bits[: len(bits) - i])
        back = keep + across.astype(F32)
    front, back = [side.reshape(-1, block, block) for side in (front, back)]

    upper_blocks, lower_cross, lower_blocks = call(
        functools.partial(blocks_kernel, width),
        "blocks",
        (parents,),
        (near, far, upper_diagonal, lower_diagonal, parent_panel, panel_turned),
        [
            shape_of((uppers, block, block), F32),
            shape_of((lowers, block, block), F32),
            shape_of((lowers, block, block), F32),
        ],
        [shape_of((width * chunk, block), F32), shape_of((uppers, 2 * block, block), bf16)],
    )
    upper_blocks, *got = tie(upper_blocks, *got)
    upper_columns, lower_columns = call(
        columns_kernel,
        "columns",
        (parents, upper_pattern, lower_pattern),
        (parent_panel, own, front, back, *got),
        [
            shape_of((uppers, block, block), bf16),
            shape_of((lowers, block, block), bf16),
        ],
    )
    return (
        upper_columns[:, None, None],
        upper_blocks,
        lower_columns[:, None, None],
        lower_cross,
        lower_blocks,
    )


def solution(mesh):
    return jax.shard_map(
        per_device,
        mesh=mesh,
        in_specs=(
            P("row", None, None, "col", None, None),
            P(None, "row", "col", None, None),
            P(None, "row", "col"),
            P(),
            P(None, "row", "col", None, None),
            P(None, "row", "col"),
            P(),
            P(),
            P(),
        ),
        out_specs=(
            P(None, "row", "col", None, None),
            P(),
            P(None, "row", "col", None, None),
            P(),
            P(),
        ),
        check_vma=False,
    )
```

```python
import functools

import jax
import jax.numpy as jnp
import numpy as np
from jax import lax
from jax.experimental import pallas as pl
from jax.experimental.pallas import tpu as pltpu
from jax.sharding import PartitionSpec as P

F32 = jnp.float32
WIRE = jnp.bfloat16
VMEM = pl.BlockSpec(memory_space=pltpu.VMEM)
SMEM = pl.BlockSpec(memory_space=pltpu.SMEM)


def shape_of(dims, kind):
    return jax.ShapeDtypeStruct(dims, kind)


def flip(value, axis, mask):
    size = lax.axis_size(axis)
    return lax.ppermute(value, axis, [(i, i ^ mask) for i in range(size)])


def shift(value, axis, step):
    size = lax.axis_size(axis)
    return lax.ppermute(value, axis, [(i, (i + step) % size) for i in range(size)])


def ceil_to(value, step):
    return -(-value // step) * step


def params(refs, limit):
    size = sum(int(np.prod(r.shape)) * np.dtype(r.dtype).itemsize for r in refs)
    return pltpu.CompilerParams(vmem_limit_bytes=limit or ceil_to(size * 5 // 4, 1 << 20) + (4 << 20))


def call(kernel, name, scalars, arrays, outs, scratch=(), limit=0, cost=0):
    return pl.pallas_call(
        kernel,
        out_shape=outs,
        in_specs=[SMEM] * len(scalars) + [VMEM] * len(arrays),
        out_specs=[VMEM] * len(outs),
        scratch_shapes=[pltpu.VMEM(r.shape, r.dtype) for r in scratch],
        compiler_params=params([*arrays, *outs, *scratch], limit),
        cost_estimate=pl.CostEstimate(flops=cost, bytes_accessed=cost, transcendentals=0) if cost else None,
        name=name,
    )(*scalars, *arrays)


def stack_kernel(*refs):
    for i, piece in enumerate(refs[:-4]):
        refs[-1][i] = piece[...]


def mask_kernel(upper_pattern, lower_pattern, upper_panel, lower_panel, masked):
    uppers, lowers = upper_panel.shape[0], lower_panel.shape[0]
    for k in range(uppers):
        masked[k] = upper_panel[k] * upper_pattern[k].astype(F32).astype(jnp.bfloat16)
    for m in range(lowers):
        masked[uppers + m] = lower_panel[m] * lower_pattern[m].astype(F32).astype(jnp.bfloat16)


def turn_kernel(*refs):
    pieces, turned = refs[:-1], refs[-1]
    total, block = pieces[0].shape[0], pieces[0].shape[-1]
    for k in range(total):
        for o, piece in enumerate(pieces):
            turned[k, :, o * block : (o + 1) * block] = piece[k].T


def top_kernel(top, panel, out, out_turned, panel_turned):
    depth, width, block, _ = top.shape
    row, col = lax.axis_index("row"), lax.axis_index("col")
    half = width // 2

    def tile(o, i):
        return top[lax.rem(col + o, depth), row ^ (2 * (i % half) + i // half)]

    for o in range(out.shape[1] // block):
        rows = slice(o * block, (o + 1) * block)
        for i in range(width):
            out[i // half, rows, (i % half) * block : (i % half + 1) * block] = tile(o, i)

    for o in range(1, out.shape[1] // block):
        lanes = slice((o - 1) * block, o * block)
        for i in range(width):
            out_turned[i * block : (i + 1) * block, lanes] = tile(o, i).T
    for m in range(panel.shape[0]):
        panel_turned[m] = panel[m].T


def partial_kernel(top, *refs):
    pieces, (keep, away) = refs[:-2], refs[-2:]
    half, total, block, _ = keep.shape
    for first in range(0, total, 2):
        second = min(first + 1, total - 1)
        right = [jnp.concatenate([p[first], p[second]], axis=1) for p in pieces]
        value = jnp.dot(top[...], jnp.concatenate(right), preferred_element_type=F32)
        for lane, k in enumerate(range(first, second + 1)):
            for i in range(half):
                lanes = slice(lane * block, (lane + 1) * block)
                keep[i, k] = value[i * block : (i + 1) * block, lanes]
                far = value[(half + i) * block : (half + i + 1) * block, lanes]
                away[i, k] = far.astype(away.dtype)


def dot_pair(left, own, others, first, second):
    pieces = [own, *[others.at[i] for i in range(others.shape[0])]]
    right = [jnp.concatenate([piece[first], piece[second]], axis=1) for piece in pieces]
    return jnp.dot(left, jnp.concatenate(right), preferred_element_type=F32)


def first_kernel(top, own, near, out):
    total = own.shape[0]
    for first in range(0, total, 2):
        out[first // 2] = dot_pair(top[0], own, near, first, min(first + 1, total - 1))


def triangle(block):
    rows = lax.broadcasted_iota(jnp.int32, (block, block), 0)
    lanes = lax.broadcasted_iota(jnp.int32, (block, block), 1)
    return rows < lanes, rows == lanes


def pack(squares, packed, start):
    total, block = len(squares), squares[0].shape[0]
    above, diagonal = triangle(block)
    for p in range(total // 2):
        first, second = [squares[k] + squares[k].T for k in (2 * p, 2 * p + 1)]
        packed[p * block : (p + 1) * block] = jnp.where(above, first, second)
        row = jnp.sum(jnp.where(diagonal, first, 0.0), axis=0, keepdims=True)
        packed[start + p : start + p + 1] = row
    if total % 2:
        packed[(total // 2) * block : (total // 2 + 1) * block] = squares[total - 1] + squares[total - 1].T


def unpack(packed, total, block, start):
    above, diagonal = triangle(block)
    squares = []
    for p in range(total // 2):
        value = packed[p * block : (p + 1) * block]
        turned = value.T
        row = packed[start + p : start + p + 1]
        squares.append(jnp.where(above, value, jnp.where(diagonal, row, turned)))
        squares.append(jnp.where(above, turned, value))
    if total % 2:
        squares.append(packed[(total // 2) * block : (total // 2 + 1) * block])
    return squares


def second_kernel(uppers, parents, top, far_own, far, start, turned, *refs):
    own, returns, (sums_keep, sums_away, both, packed) = refs[0], refs[1:-4], refs[-4:]
    total, block, reach = turned.shape
    lowers = total - uppers
    half, chunk, _ = sums_keep.shape
    row = lax.axis_index("row")

    for first in range(0, total, 2):
        second = min(first + 1, total - 1)
        value = start[first // 2] + dot_pair(top[1], far_own, far, first, second)
        for lane, k in enumerate(range(first, second + 1)):
            part = value[:, lane * block : (lane + 1) * block]
            own[k] = part[:block]
            for o, out in enumerate(returns):
                out[k] = part[(o + 1) * block : (o + 2) * block].astype(WIRE)
            part = jnp.concatenate([0.5 * part[:block], part[block:reach]])
            high = part.astype(jnp.bfloat16)
            both[k, :, :block] = high
            both[k, :, block:] = (part - high.astype(F32)).astype(jnp.bfloat16)

    def fold(rows, k):
        value = jnp.dot(rows, both[k], preferred_element_type=F32)
        return value[:, :block] + value[:, block:]

    base = (total + 1) // 2 * block
    squares = [fold(turned[k], k) for k in range(uppers)]
    crossed = [fold(turned[uppers + m], parents[m]) for m in range(lowers)]
    for m in range(lowers):
        rows = jnp.concatenate([turned[uppers + m], turned[parents[m]]], axis=0)
        value = fold(rows, uppers + m)
        squares.append(value[:block])
        place = base + m * block
        packed[place : place + block] = value[block:] + crossed[m].T
    end = base + lowers * block
    packed[end:] = jnp.zeros((packed.shape[0] - end, block), F32)
    pack(squares, packed, end)
    for m in range(2 * half):
        place = pl.multiple_of((row ^ m) * chunk, chunk)
        (sums_away if m & 1 else sums_keep)[m // 2] = packed[pl.ds(place, chunk)]


def line_kernel(*refs):
    parts, (total_out, order) = refs[:-2], refs[-2:]
    depth, col = len(parts), lax.axis_index("col")
    for o in range(depth):
        order[lax.rem(col + o, depth)] = parts[o][...].astype(F32)
    total = order[0]
    for c in range(1, depth):
        total = total + order[c]
    total_out[...] = total.astype(total_out.dtype)


def columns_kernel(parents, upper_pattern, lower_pattern, panel, own, front, back, *refs):
    got, (upper_out, lower_out) = refs[:-2], refs[-2:]
    uppers, lowers, middle = upper_out.shape[0], lower_out.shape[0], front.shape[0]

    def product(k):
        value = own[k] + (front[k] if k < middle else back[k - middle])
        for piece in got:
            value = value + piece[k].astype(F32)
        return value

    for k in range(uppers):
        upper_out[k] = (-product(k) * upper_pattern[k].astype(F32)).astype(jnp.bfloat16)
    extensions = [
        jnp.dot(upper_out[parents[m]], panel[m], preferred_element_type=F32) for m in range(lowers)
    ]
    for m in range(lowers):
        value = -(product(uppers + m) + extensions[m]) * lower_pattern[m].astype(F32)
        lower_out[m] = value.astype(jnp.bfloat16)


def split(wide):
    high = wide.astype(jnp.bfloat16)
    return high, (wide - high.astype(F32)).astype(jnp.bfloat16)


def blocks_kernel(
    width,
    parents,
    near,
    far,
    upper_diagonal,
    lower_diagonal,
    panel,
    panel_turned,
    upper_out,
    cross_out,
    lower_out,
    packed,
    halves,
):
    uppers, lowers = upper_out.shape[0], lower_out.shape[0]
    block = panel.shape[-1]
    chunk = near.shape[1]
    row = lax.axis_index("row")
    for m in range(width):
        place = pl.multiple_of((row ^ m) * chunk, chunk)
        packed[pl.ds(place, chunk)] = (far if m & 1 else near)[m // 2].astype(F32)
    base = (uppers + lowers + 1) // 2 * block
    squares = unpack(packed, uppers + lowers, block, base + lowers * block)
    for k in range(uppers):
        value = upper_diagonal[k] + squares[k]
        upper_out[k] = value
        halves[k, :block], halves[k, block:] = split(value)
    products = [
        jnp.dot(halves[parents[m]], panel[m], preferred_element_type=F32) for m in range(lowers)
    ]
    rights = []
    for m in range(lowers):
        forms = packed[base + m * block : base + (m + 1) * block]
        cross = forms - (products[m][:block] + products[m][block:])
        cross_out[m] = cross
        rights.append(jnp.concatenate([forms.astype(jnp.bfloat16), *split(cross)], axis=1))
    backs = [
        jnp.dot(panel_turned[m], rights[m], preferred_element_type=F32) for m in range(lowers)
    ]
    for m in range(lowers):
        value = backs[m]
        rest = value[:, block : 2 * block] + value[:, 2 * block :]
        lower_out[m] = lower_diagonal[m] + squares[uppers + m] - rest - value[:, :block].T


def gather_shifts(value, axis):
    size = lax.axis_size(axis)
    return [value] + [shift(value, axis, -o) for o in range(1, size)]


def pairs(size, offset):
    takers = range(size)
    if 2 * offset == size:
        takers = [c if c % 2 == 0 else c + offset for c in range(offset)]
    return [(c, (c + offset) % size) for c in takers]


def gather_pair(value, axis, offset):
    return lax.ppermute(value, axis, [(b, c) for c, b in pairs(lax.axis_size(axis), offset)])


def return_pair(value, axis, offset):
    return lax.ppermute(value, axis, pairs(lax.axis_size(axis), offset))


def halve(value, axis, bit, left):
    place = sorted(left, reverse=True).index(bit)
    value = value.reshape((2,) * len(left) + value.shape[-3:])
    away = lax.index_in_dim(value, 1, place, keepdims=False).astype(WIRE)
    keep = lax.index_in_dim(value, 0, place, keepdims=False)
    return keep, flip(away, axis, 1 << bit)


def gather_near(value, axis):
    masks = range(2, lax.axis_size(axis), 2)
    return [value] + [flip(value, axis, m) for m in masks]


def scatter_flips(value, axis):
    masks = range(2, lax.axis_size(axis), 2)
    return [flip(value[m // 2].astype(WIRE), axis, m) for m in masks]


def tie(*values):
    return lax.optimization_barrier(values)


def per_device(
    top_inverse,
    upper_panel,
    upper_pattern,
    upper_diagonal,
    lower_panel,
    lower_pattern,
    parents,
    parent_panel,
    lower_diagonal,
):
    uppers, block = upper_panel.shape[0], upper_panel.shape[-1]
    lowers = lower_panel.shape[0]
    total = uppers + lowers
    width, depth = lax.axis_size("row"), lax.axis_size("col")
    half = width // 2
    packed_n = (total + 1) // 2 * block + lowers * block + total // 2
    chunk = ceil_to(packed_n, 16 * width) // width
    bf16 = jnp.bfloat16
    upper_pattern, lower_pattern = upper_pattern.reshape(-1), lower_pattern.reshape(-1)

    (masked,) = call(
        mask_kernel,
        "mask",
        (upper_pattern, lower_pattern),
        (upper_panel.reshape(-1, block, block), lower_panel.reshape(-1, block, block)),
        [shape_of((total, block, block), bf16)],
        limit=60 << 20,
    )
    reach = depth // 2
    pieces = [gather_pair(masked, "col", o) for o in range(1, reach + 1)]
    (turned,) = call(
        turn_kernel,
        "turn",
        (),
        (masked, *pieces),
        [shape_of((total, block, (reach + 1) * block), bf16)],
    )
    top, top_turned, panel_turned = call(
        top_kernel,
        "top",
        (),
        (top_inverse[0, :, :, 0], parent_panel),
        [
            shape_of((2, (reach + 1) * block, half * block), bf16),
            shape_of((width * block, reach * block), bf16),
            shape_of(parent_panel.shape, bf16),
        ],
    )
    far_own = flip(masked, "row", 1)
    (near,) = call(
        stack_kernel,
        "stack",
        (),
        (*gather_near(masked, "row")[1:], turned, far_own, top_turned),
        [shape_of((half - 1, total, block, block), bf16)],
    )
    far = flip(near, "row", 1)
    keep, away = call(
        partial_kernel,
        "partial",
        (),
        (top_turned, *pieces),
        [
            shape_of((half, total, block, block), F32),
            shape_of((half, total, block, block), WIRE),
        ],
    )
    columns_n = ceil_to(total, 2) // 2
    (start,) = call(
        first_kernel,
        "first",
        (),
        (top, masked, near),
        [shape_of((columns_n, (reach + 1) * block, 2 * block), F32)],
    )
    own, *rest = call(
        functools.partial(second_kernel, uppers),
        "second",
        (parents,),
        (top, far_own, far, start, turned),
        [shape_of((total, block, block), F32)]
        + [shape_of((total, block, block), WIRE)] * reach
        + [shape_of((half, chunk, block), F32)] * 2,
        [
            shape_of((total, (reach + 1) * block, 2 * block), bf16),
            shape_of((width * chunk, block), F32),
        ],
    )
    returns, (sums_keep, sums_away) = rest[:-2], rest[-2:]

    other, across = tie(flip(sums_away, "row", 1), flip(away, "row", 1))
    sums = sums_keep + other
    pieces = scatter_flips(sums, "row")
    pieces[0], value = tie(pieces[0], keep + across.astype(F32))
    middle = total // 2
    bits = list(range(1, width.bit_length() - 1))
    sides = [value[:, :middle], value[:, middle:]]
    halves = [halve(side, "row", bit, bits) for side, bit in zip(sides, (bits[0], bits[-1]))]
    part = sums[0]
    for piece in pieces:
        part = part + piece.astype(F32)
    part = part.astype(WIRE)
    early = [return_pair(returns[o - 1], "col", o) for o in range(1, reach)]
    parts = gather_shifts(part, "col")
    tied = tie(*parts, *[got for _, got in halves], *early)
    early = tied[depth + 2 :]
    (part,) = call(
        line_kernel,
        "line",
        (),
        tied[:depth],
        [shape_of((chunk, block), WIRE)],
        [shape_of((depth, chunk, block), F32)],
    )
    sides = [keep + got.astype(F32) for (keep, _), got in zip(halves, tied[depth : depth + 2])]
    part, last, *sides = tie(part, returns[-1], *sides)
    nears = gather_near(part, "row")
    near = jnp.stack(nears)
    far = flip(near, "row", 1)
    got = [*early, return_pair(last, "col", reach)]
    front, back = sides
    for i in range(1, len(bits)):
        keep, across = halve(front, "row", bits[i], bits[i:])
        front = keep + across.astype(F32)
        keep, across = halve(back, "row", bits[-1 - i], bits[: len(bits) - i])
        back = keep + across.astype(F32)
    front, back = [side.reshape(-1, block, block) for side in (front, back)]

    upper_blocks, lower_cross, lower_blocks = call(
        functools.partial(blocks_kernel, width),
        "blocks",
        (parents,),
        (near, far, upper_diagonal, lower_diagonal, parent_panel, panel_turned),
        [
            shape_of((uppers, block, block), F32),
            shape_of((lowers, block, block), F32),
            shape_of((lowers, block, block), F32),
        ],
        [shape_of((width * chunk, block), F32), shape_of((uppers, 2 * block, block), bf16)],
    )
    upper_blocks, *got = tie(upper_blocks, *got)
    upper_columns, lower_columns = call(
        columns_kernel,
        "columns",
        (parents, upper_pattern, lower_pattern),
        (parent_panel, own, front, back, *got),
        [
            shape_of((uppers, block, block), bf16),
            shape_of((lowers, block, block), bf16),
        ],
    )
    return (
        upper_columns[:, None, None],
        upper_blocks,
        lower_columns[:, None, None],
        lower_cross,
        lower_blocks,
    )


def solution(mesh):
    return jax.shard_map(
        per_device,
        mesh=mesh,
        in_specs=(
            P("row", None, None, "col", None, None),
            P(None, "row", "col", None, None),
            P(None, "row", "col"),
            P(),
            P(None, "row", "col", None, None),
            P(None, "row", "col"),
            P(),
            P(),
            P(),
        ),
        out_specs=(
            P(None, "row", "col", None, None),
            P(),
            P(None, "row", "col", None, None),
            P(),
            P(),
        ),
        check_vma=False,
    )
```
